256 devices in a mesh: band: 64 (over z_lo, x, y, core), chan: 4 (over z_hi).
Axes of the slice: x: 4, y: 4, z: 8 (z_hi: 4, z_lo: 2; z = z_hi * 2 + z_lo), core: 2. Of those that a mesh axis runs over, the one named last changes fastest.
Arguments:
- video: bfloat16 [3, 2, 512, 512], P(None, None, 'band'), may hold values from -6 to 6
- weight_one: bfloat16 [27, 12, 128], P(None, None, 'chan'), may hold values from -0.3125 to 0.3125
- weight_two: bfloat16 [27, 512, 256], P(None, 'chan'), may hold values from -0.0546875 to 0.0546875
- cotangent: bfloat16 [256, 2, 128, 128], P('chan', None, 'band'), may hold values from -6 to 6
Outputs:
- latent: bfloat16 [256, 2, 128, 128], P('chan', None, 'band')
- grad_one: float32 [27, 12, 128], P(None, None, 'chan')
- grad_two: float32 [27, 512, 256], P(None, 'chan')
The draws below stay inside these ranges and needn't reach their ends.
All inputs are finite; a program needn't handle non-finite values.
Results may differ from the reference program's by a relative error of at most 0.015.
Values may be sent and summed in bfloat16 or wider, within the bound.
No kernel may reach another device: no remote copies, remote signals or barrier semaphores. Data moves between devices by JAX's collectives and lax.ppermute only.
A program may use at most 64 MiB of HBM per device.

```python
import math
import jax
import jax.numpy as jnp
from jax import lax

FRAMES = 2
WIDTH = 512
C1 = 128
C2 = 256
ROWS = 512


def steps_of(own_key, extent, shards, least, high):
    gain, own = 1.0, jax.random.fold_in(own_key, 6)
    for axis_at, blocks in shards:
        steps = jnp.exp(jax.random.uniform(jax.random.fold_in(own, axis_at), (blocks,), jnp.float32, least / len(shards), high / len(shards)))
        gain = gain * jnp.repeat(steps, extent[axis_at] // blocks).reshape([-1 if axis == axis_at else 1 for axis in range(len(extent))])
    return gain


def gaussian(stream_key, dims, width, limit, shards=(), kind=jnp.bfloat16):
    drawn = jax.random.normal(stream_key, dims, jnp.float32) * width
    if len(shards) > 0:
        drawn = steps_of(stream_key, dims, shards, -0.22, 0.18) * drawn
    return jnp.clip(drawn, min=-limit, max=limit).astype(kind)


def setup_inputs(seed: int = 0) -> dict:
    key_list = jax.random.split(jax.random.key(seed), 5)
    return {
        "video": gaussian(key_list[0], (3, FRAMES, ROWS, WIDTH), 1.0, 6.0, ((2, 64),)),
        "weight_one": gaussian(key_list[1], (27, 12, C1), 324 ** -0.5, 0.3125, ((2, 4),)),
        "weight_two": gaussian(key_list[2], (27, 4 * C1, C2), (108 * C1) ** -0.5, 0.0546875, ((1, 4),)),
        "cotangent": gaussian(key_list[3], (C2, FRAMES, ROWS // 4, WIDTH // 4), 1.0, 6.0, ((0, 4), (2, 64))),
    }


def haar(x):
    chans = x.shape[0]
    p = x[:, :, 0::2, 0::2]
    q = x[:, :, 0::2, 1::2]
    r = x[:, :, 1::2, 0::2]
    s = x[:, :, 1::2, 1::2]
    bands = jnp.stack([p + q + r + s, p - q + r - s, p + q - r - s, p - q - r + s], axis=1) * 0.5
    return bands.reshape((chans * 4,) + p.shape[1:])

def haar_t(d):
    chans = d.shape[0] // 4
    parts = d.reshape((chans, 4) + d.shape[1:])
    a0, a1, a2, a3 = (parts[:, 0], parts[:, 1], parts[:, 2], parts[:, 3])
    p = (a0 + a1 + a2 + a3) * 0.5
    q = (a0 - a1 + a2 - a3) * 0.5
    r = (a0 + a1 - a2 - a3) * 0.5
    s = (a0 - a1 - a2 + a3) * 0.5
    frames, half_rows, half_cols = (p.shape[1], p.shape[2], p.shape[3])
    upper = jnp.stack([p, q], axis=-1).reshape(chans, frames, half_rows, 2 * half_cols)
    lower = jnp.stack([r, s], axis=-1).reshape(chans, frames, half_rows, 2 * half_cols)
    return jnp.stack([upper, lower], axis=3).reshape(chans, frames, 2 * half_rows, 2 * half_cols)

def tap_stack(window, row_count, col_count):
    return jnp.stack([window[:, tap_t, tap_r:tap_r + row_count, tap_c:tap_c + col_count] for tap_t in range(3) for tap_r in range(3) for tap_c in range(3)], 0)

def causal_conv(padded, weight):
    frames = padded.shape[1] - 2
    row_count = padded.shape[2] - 2
    col_count = padded.shape[3] - 2
    weight_f = weight.astype(jnp.float32)

    def one_frame(frame):
        window = lax.dynamic_slice_in_dim(padded, frame, 3, 1)
        taps = tap_stack(window, row_count, col_count).astype(jnp.float32)
        return jnp.einsum('kco,kcrw->orw', weight_f, taps)
    result = lax.map(one_frame, jnp.arange(frames, dtype=jnp.int32))
    return jnp.transpose(result, (1, 0, 2, 3))

def weight_grad(padded, grad):
    frames, row_count, col_count = (grad.shape[1], grad.shape[2], grad.shape[3])

    def accumulate(frame, running):
        window = lax.dynamic_slice_in_dim(padded, frame, 3, 1)
        taps = tap_stack(window, row_count, col_count).astype(jnp.float32)
        grad_frame = lax.dynamic_index_in_dim(grad, frame, 1, keepdims=False).astype(jnp.float32)
        return running + jnp.einsum('kcrw,orw->kco', taps, grad_frame)
    start = jnp.zeros((27, padded.shape[0], grad.shape[0]), jnp.float32)
    return lax.fori_loop(0, frames, accumulate, start)

def reference(video, weight_one, weight_two, cotangent):
    coef_one = haar(video.astype(jnp.float32)).astype(jnp.bfloat16)
    padded_one = jnp.pad(coef_one, ((0, 0), (2, 0), (1, 1), (1, 1)))
    pre_one = causal_conv(padded_one, weight_one)
    coef_two = haar(jax.nn.silu(pre_one)).astype(jnp.bfloat16)
    padded_two = jnp.pad(coef_two, ((0, 0), (2, 0), (1, 1), (1, 1)))
    latent = causal_conv(padded_two, weight_two).astype(jnp.bfloat16)
    cot_padded = jnp.pad(cotangent, ((0, 0), (0, 2), (1, 1), (1, 1)))
    flipped = jnp.transpose(weight_two[::-1], (0, 2, 1))
    back_two = causal_conv(cot_padded, flipped)
    back_act = haar_t(back_two)
    gate_val = jax.nn.sigmoid(pre_one)
    back_pre = (back_act * gate_val * (1.0 + pre_one * (1.0 - gate_val))).astype(jnp.bfloat16)
    scale_one = 1.0 / math.sqrt(FRAMES * (ROWS // 2) * (WIDTH // 2))
    scale_two = 1.0 / math.sqrt(FRAMES * (ROWS // 4) * (WIDTH // 4))
    grad_one = weight_grad(padded_one, back_pre) * scale_one
    grad_two = weight_grad(padded_two, cotangent) * scale_two
    return (latent, grad_one, grad_two)
```

```python
import math

import jax
import jax.numpy as jnp
import ml_dtypes
import numpy as np
from jax import lax
from jax.experimental import pallas as pl
from jax.experimental.pallas import tpu as pltpu
from jax.sharding import PartitionSpec as P

BF = jnp.bfloat16
F32 = jnp.float32


def column_matrix():
    m = np.zeros((512, 4, 2, 128), np.float32)
    for s in range(4):
        for w in range(128):
            j = 2 * w - 1 + s
            if 0 <= j < 256:
                m[2 * j, s, :, w] = 0.5
                m[2 * j + 1, s, 0, w] = 0.5
                m[2 * j + 1, s, 1, w] = -0.5
    return m.reshape(512, 1024).astype(ml_dtypes.bfloat16)


def row_matrix():
    m = np.zeros((3, 2, 2, 4, 16, 48), np.float32)
    for tb in range(2):
        for f in range(2):
            for r in range(4):
                for wi in range(4):
                    for ch in range(3):
                        y = 2 * (2 * (r - 1) - 1 + wi) + tb + 8
                        m[y // 8, tb, f, r, wi * 3 + ch, ch * 16 + f * 8 + y % 8] = 1.0
    return m.reshape(3, 256, 48).astype(ml_dtypes.bfloat16)


def select_matrix():
    m = np.zeros((4, 128, 256), np.float32)
    for phr in range(2):
        for phc in range(2):
            for b in range(3):
                for e in range(3):
                    for ch in range(3):
                        for k in range(4):
                            row = (b * 3 + e) * 12 + ch * 4 + k
                            col = (k >> 1) * 128 + ((phc + e) * 2 + (k & 1)) * 16 + (phr + b) * 3 + ch
                            m[phr * 2 + phc, row, col] = 1.0
    return m.astype(ml_dtypes.bfloat16)


def dot(a, b, ca=1, cb=0):
    return lax.dot_general(a, b, (((ca,), (cb,)), ((), ())), preferred_element_type=F32)


def expand_kernel(w1_ref, sel_ref, out_ref):
    for p in range(4):
        for a in range(2):
            out_ref[32 * p : 32 * p + 32, 256 * a : 256 * a + 256] = dot(
                w1_ref[a], sel_ref[p], 0, 0
            ).astype(BF)


def shifted(x, step):
    lanes = x.shape[1]
    lane = lax.broadcasted_iota(jnp.int32, x.shape, 1) % 128
    if step == -1:
        return jnp.where(lane == 0, 0.0, pltpu.roll(x, 1, 1))
    return jnp.where(lane == 127, 0.0, pltpu.roll(x, lanes - 1, 1))


def forward_kernel(
    prev_ref, own_ref, next_ref, row_ref, col_ref, w1_ref, wa_ref, wb_ref,
    xc_ref, lat_ref, pre_ref, win_ref, one, two,
):
    band = lax.axis_index("band")
    last = lax.axis_size("band") - 1
    v = (
        dot(row_ref[0], prev_ref[...])
        + dot(row_ref[1], own_ref[...])
        + dot(row_ref[2], next_ref[...])
    ).astype(BF)
    h = dot(v, col_ref[...])
    top, low = h[:128], h[128:]
    for pm, half in enumerate(((top + low).astype(BF), (top - low).astype(BF))):
        for f in range(2):
            for r in range(4):
                for st in range(8):
                    one[f, pm * 128 + st * 16 : pm * 128 + st * 16 + 16, r * 128 : r * 128 + 128] = half[
                        (f * 4 + r) * 16 : (f * 4 + r) * 16 + 16, st * 128 : st * 128 + 128
                    ]
    w1a, w1b = w1_ref[:, :256], w1_ref[:, 256:]
    pres = (dot(w1b, one[0]), dot(w1a, one[0]) + dot(w1b, one[1]))
    lane = lax.broadcasted_iota(jnp.int32, (32, 512), 1)
    keep = ((lane >= 128) | (band > 0)) & ((lane < 384) | (band < last))
    for f in range(2):
        pre = pres[f]
        pre_ref[:, f * 256 : f * 256 + 256] = pre[:, 128:384]
        win_ref[:, f * 256 : f * 256 + 256] = one[f, :, 128:384]
        act = pre * jax.nn.sigmoid(pre)
        p, q, r, s = act[:32], act[32:64], act[64:96], act[96:]
        pq, pmq, rs, rms = p + q, p - q, r + s, r - s
        parts = (pq + rs, pmq + rms, pq - rs, pmq - rms)
        for k in range(4):
            part = jnp.where(keep, parts[k] * 0.5, 0.0)
            for r in range(4):
                two[r, pl.ds(k, 32, stride=4), :] = part[:, r * 128 : r * 128 + 128]
        x = jnp.concatenate([two[r] for r in range(4)], 1)
        for e, xe in enumerate((shifted(x, -1), x, shifted(x, 1))):
            xe = xe.astype(BF)
            for b in range(3):
                at = (b * 3 + e) * 128
                xc_ref[at : at + 128, f * 256 : f * 256 + 256] = xe[:, b * 128 : b * 128 + 256]
    out = dot(wb_ref[...], xc_ref[...], 0, 0)
    more = dot(wa_ref[...], xc_ref[:, :256], 0, 0)
    lat_ref[:, :256] = out[:, :256].astype(BF)
    lat_ref[:, 256:] = (out[:, 256:] + more).astype(BF)


def backward_kernel(
    xc_ref, cot_ref, up_ref, down_ref, pre_ref, win_ref, wa_ref, wb_ref, sel_ref,
    g2_ref, g1_ref, grown, back_s, *, scale_one, scale_two,
):
    cot = cot_ref[...]
    for f in range(2):
        at = f * 512
        grown[:, at : at + 128] = up_ref[:, f * 128 : f * 128 + 128]
        grown[:, at + 128 : at + 384] = cot[:, f * 256 : f * 256 + 256]
        grown[:, at + 384 : at + 512] = down_ref[:, f * 128 : f * 128 + 128]
    g2_ref[1152:, :] = (dot(xc_ref[...], cot, 1, 1) * scale_two).astype(BF)
    g2_ref[:1152, :] = (dot(xc_ref[:, :256], cot[:, 256:], 1, 1) * scale_two).astype(BF)
    z0 = z1 = 0.0
    for b in range(3):
        lo = (2 - b) * 128
        c0, c1 = grown[:, lo : lo + 256], grown[:, 512 + lo : 768 + lo]
        wa, wb = wa_ref[b * 384 : b * 384 + 384, :], wb_ref[b * 384 : b * 384 + 384, :]
        z0 = z0 + dot(wb, c0) + dot(wa, c1)
        z1 = z1 + dot(wb, c1)
    for f, z in enumerate((z0, z1)):
        z = z[128:256] + shifted(z[:128], 1) + shifted(z[256:], -1)
        back_s[0], back_s[1] = z[:, :128], z[:, 128:]
        a0, a1, a2, a3 = (
            jnp.concatenate([back_s[r, pl.ds(k, 32, stride=4), :] for r in range(2)], 1)
            for k in range(4)
        )
        s01, d01, s23, d23 = a0 + a1, a0 - a1, a2 + a3, a2 - a3
        act = jnp.concatenate([s01 + s23, d01 + d23, s01 - s23, d01 - d23], 0) * 0.5
        pre = pre_ref[:, f * 256 : f * 256 + 256]
        gate = jax.nn.sigmoid(pre)
        back = (act * gate * (1.0 + pre * (1.0 - gate))).astype(BF)
        if f == 0:
            late = dot(back, win_ref[:, :256], 1, 1)
        else:
            early = dot(back, win_ref[:, :256], 1, 1)
            late = late + dot(back, win_ref[:, 256:], 1, 1)
    for a, g in enumerate((early, late)):
        g = g * scale_one
        hi = g.astype(BF)
        lo = (g - hi.astype(F32)).astype(BF)
        total = 0.0
        for p in range(4):
            rows = slice(32 * p, 32 * p + 32)
            total = total + dot(hi[rows], sel_ref[p], 1, 1) + dot(lo[rows], sel_ref[p], 1, 1)
        g1_ref[:, 128 * a : 128 * a + 128] = total.astype(BF)


def vmem(count):
    return [pl.BlockSpec(memory_space=pltpu.VMEM)] * count


def call(kernel, outs, scratch, flops, *args):
    return pl.pallas_call(
        kernel,
        out_shape=[jax.ShapeDtypeStruct(*o) for o in outs],
        in_specs=vmem(len(args)),
        out_specs=vmem(len(outs)),
        scratch_shapes=[pltpu.VMEM(*s) for s in scratch],
        compiler_params=pltpu.CompilerParams(vmem_limit_bytes=40 * 1024 * 1024),
        cost_estimate=pl.CostEstimate(flops=flops, bytes_accessed=4 << 20, transcendentals=0),
    )(*args)


def chan_gather(x):
    count = lax.axis_size("chan")
    return lax.all_to_all(
        jnp.broadcast_to(x[None], (count,) + x.shape), "chan", 0, 0, tiled=True
    )


def band_sum(x):
    got = lax.all_to_all(x, "band", 0, 0, tiled=True)
    mine = got.astype(F32).sum(0).astype(BF)
    return lax.all_to_all(jnp.broadcast_to(mine[None], x.shape), "band", 0, 0, tiled=True)


def on_device(video, weight_one, weight_two, cotangent):
    n = lax.axis_size("band")
    up = [(i, i + 1) for i in range(n - 1)]
    down = [(j, i) for i, j in up]
    flat = video.reshape(48, 512)
    before, after = lax.ppermute(flat, "band", up), lax.ppermute(flat, "band", down)
    own = cotangent.reshape(64, 512)
    rows = cotangent
    above = lax.ppermute(rows[:, :, 1].reshape(64, 256), "band", up)
    below = lax.ppermute(rows[:, :, 0].reshape(64, 256), "band", down)
    w1 = jnp.pad(weight_one[9:].reshape(2, 108, 32), ((0, 0), (0, 20), (0, 0)))
    wa, wb = weight_two[9:18].reshape(1152, 256), weight_two[18:].reshape(1152, 256)
    sel = jnp.asarray(select_matrix())
    (w1e,) = call(expand_kernel, [((128, 512), BF)], [], 1 << 20, w1, sel)
    xc, lat, pre, win = call(
        forward_kernel,
        [((1152, 512), BF), ((256, 512), BF), ((128, 512), F32), ((256, 512), BF)],
        [((2, 256, 512), BF), ((4, 128, 128), F32)],
        1 << 30,
        before, flat, after, jnp.asarray(row_matrix()), jnp.asarray(column_matrix()), w1e, wa, wb,
    )
    whole = chan_gather(own).reshape(256, 512)
    edges = chan_gather(jnp.concatenate([above, below], 1)).reshape(256, 512)
    parts = lax.all_to_all(lat.reshape(4, 64, 512), "chan", 0, 0, tiled=True)
    latent = parts.astype(F32).sum(0).astype(BF).reshape(64, 2, 2, 128)
    frames, half_rows, half_cols = video.shape[1], n * 4, video.shape[3] // 2
    scale_one = 1.0 / math.sqrt(frames * half_rows * half_cols)
    scale_two = 1.0 / math.sqrt(frames * (half_rows // 2) * (half_cols // 2))

    def backward(*refs):
        backward_kernel(*refs, scale_one=scale_one, scale_two=scale_two)

    g2, g1 = call(
        backward,
        [((2304, 256), BF), ((32, 256), BF)],
        [((256, 1024), BF), ((2, 128, 128), F32)],
        1 << 30,
        xc, whole, edges[:, :256], edges[:, 256:], pre, win, wa, wb, sel,
    )
    both = jnp.concatenate([g2.reshape(n, -1, 128), g1.reshape(n, -1, 128)], 1)
    summed = band_sum(both)
    tall = 4608 // n
    g2 = summed[:, :tall].reshape(18, 128, 256).astype(F32)
    g1 = summed[:, tall:].reshape(32, 2, 128)[:, :, :108].astype(F32)
    g1 = jnp.transpose(g1, (1, 2, 0)).reshape(18, 12, 32)
    pad = ((9, 0), (0, 0), (0, 0))
    return latent, jnp.pad(g1, pad), jnp.pad(g2, pad)


def solution(mesh):
    return jax.shard_map(
        on_device,
        mesh=mesh,
        in_specs=(
            P(None, None, "band", None),
            P(None, None, "chan"),
            P(None, "chan", None),
            P("chan", None, "band", None),
        ),
        out_specs=(P("chan", None, "band", None), P(None, None, "chan"), P(None, "chan", None)),
        check_vma=False,
    )
```

```python
import math

import jax
import jax.numpy as jnp
import ml_dtypes
import numpy as np
from jax import lax
from jax.experimental import pallas as pl
from jax.experimental.pallas import tpu as pltpu
from jax.sharding import PartitionSpec as P

BF = jnp.bfloat16
F32 = jnp.float32


def column_matrix():
    m = np.zeros((512, 4, 2, 128), np.float32)
    for s in range(4):
        for w in range(128):
            j = 2 * w - 1 + s
            if 0 <= j < 256:
                m[2 * j, s, :, w] = 0.5
                m[2 * j + 1, s, 0, w] = 0.5
                m[2 * j + 1, s, 1, w] = -0.5
    return m.reshape(512, 1024).astype(ml_dtypes.bfloat16)


def row_matrix():
    m = np.zeros((3, 2, 2, 4, 16, 48), np.float32)
    for tb in range(2):
        for f in range(2):
            for r in range(4):
                for wi in range(4):
                    for ch in range(3):
                        y = 2 * (2 * (r - 1) - 1 + wi) + tb + 8
                        m[y // 8, tb, f, r, wi * 3 + ch, ch * 16 + f * 8 + y % 8] = 1.0
    return m.reshape(3, 256, 48).astype(ml_dtypes.bfloat16)


def select_matrix():
    m = np.zeros((4, 128, 256), np.float32)
    for phr in range(2):
        for phc in range(2):
            for b in range(3):
                for e in range(3):
                    for ch in range(3):
                        for k in range(4):
                            row = (ch * 4 + k) * 9 + b * 3 + e
                            col = (k >> 1) * 128 + ((phc + e) * 2 + (k & 1)) * 16 + (phr + b) * 3 + ch
                            m[phr * 2 + phc, row, col] = 1.0
    return m.astype(ml_dtypes.bfloat16)


def dot(a, b, ca=1, cb=0):
    return lax.dot_general(a, b, (((ca,), (cb,)), ((), ())), preferred_element_type=F32)


def expand_kernel(w1_ref, sel_ref, out_ref):
    for p in range(4):
        for a in range(2):
            out_ref[32 * p : 32 * p + 32, 256 * a : 256 * a + 256] = dot(
                w1_ref[a], sel_ref[p], 0, 0
            ).astype(BF)


def shifted(x, step):
    lanes = x.shape[1]
    lane = lax.broadcasted_iota(jnp.int32, x.shape, 1) % 128
    if step == -1:
        return jnp.where(lane == 0, 0.0, pltpu.roll(x, 1, 1))
    return jnp.where(lane == 127, 0.0, pltpu.roll(x, lanes - 1, 1))


def forward_kernel(
    prev_ref, own_ref, next_ref, row_ref, col_ref, w1_ref,
    xc_ref, pre_ref, win_ref, one, two,
):
    band = lax.axis_index("band")
    last = lax.axis_size("band") - 1
    v = (
        dot(row_ref[0], prev_ref[...])
        + dot(row_ref[1], own_ref[...])
        + dot(row_ref[2], next_ref[...])
    ).astype(BF)
    h = dot(v, col_ref[...])
    top, low = h[:128], h[128:]
    for pm, half in enumerate(((top + low).astype(BF), (top - low).astype(BF))):
        for f in range(2):
            for r in range(4):
                for st in range(8):
                    one[f, pm * 128 + st * 16 : pm * 128 + st * 16 + 16, r * 128 : r * 128 + 128] = half[
                        (f * 4 + r) * 16 : (f * 4 + r) * 16 + 16, st * 128 : st * 128 + 128
                    ]
    w1a, w1b = w1_ref[:, :256], w1_ref[:, 256:]
    pres = (dot(w1b, one[0]), dot(w1a, one[0]) + dot(w1b, one[1]))
    lane = lax.broadcasted_iota(jnp.int32, (32, 512), 1)
    keep = ((lane >= 128) | (band > 0)) & ((lane < 384) | (band < last))
    for f in range(2):
        pre = pres[f]
        pre_ref[:, f * 256 : f * 256 + 256] = pre[:, 128:384]
        win_ref[:, f * 256 : f * 256 + 256] = one[f, :, 128:384]
        act = pre * jax.nn.sigmoid(pre)
        p, q, r, s = act[:32], act[32:64], act[64:96], act[96:]
        pq, pmq, rs, rms = p + q, p - q, r + s, r - s
        parts = (pq + rs, pmq + rms, pq - rs, pmq - rms)
        for k in range(4):
            part = jnp.where(keep, parts[k] * 0.5, 0.0)
            for r in range(4):
                two[r, pl.ds(k, 32, stride=4), :] = part[:, r * 128 : r * 128 + 128]
        x = jnp.concatenate([two[r] for r in range(4)], 1)
        for e, xe in enumerate((shifted(x, -1), x, shifted(x, 1))):
            xe = xe.astype(BF)
            for b in range(3):
                at = (b * 3 + e) * 128
                xc_ref[at : at + 128, f * 256 : f * 256 + 256] = xe[:, b * 128 : b * 128 + 256]


def latent_kernel(xc_ref, wa_ref, wb_ref, lat_ref):
    out = dot(wb_ref[...], xc_ref[...], 0, 0)
    more = dot(wa_ref[...], xc_ref[:, :256], 0, 0)
    lat_ref[:, :256] = out[:, :256].astype(BF)
    lat_ref[:, 256:] = (out[:, 256:] + more).astype(BF)


def second_grad_kernel(
    xc_ref, c0_ref, c1_ref, c2_ref, c3_ref,
    cot_ref, last_ref, first_ref, keep_ref, send_ref, *, scale,
):
    chan = lax.axis_index("chan")
    core = lax.axis_index("band") % 2
    for k, ref in enumerate((c0_ref, c1_ref, c2_ref, c3_ref)):
        cot_ref[pl.ds(pl.multiple_of((chan ^ k) * 64, 64), 64), :] = ref[...]
    for f in range(2):
        first_ref[:, f * 128 : f * 128 + 128] = cot_ref[:, f * 256 : f * 256 + 128]
        last_ref[:, f * 128 : f * 128 + 128] = cot_ref[:, f * 256 + 128 : f * 256 + 256]

    def put(early_ref, late_ref):
        early = dot(xc_ref[:, :256], cot_ref[:, 256:], 1, 1) * scale
        late = dot(xc_ref[...], cot_ref[...], 1, 1) * scale
        for ref, g in ((early_ref, early), (late_ref, late)):
            ref[:1152, :] = g[:, :128].astype(BF)
            ref[1152:, :] = g[:, 128:].astype(BF)

    @pl.when(core == 0)
    def _():
        put(keep_ref, send_ref)

    @pl.when(core == 1)
    def _():
        put(send_ref, keep_ref)


def backward_kernel(
    cot_ref, up_ref, down_ref, pre_ref, win_ref, wa_ref, wb_ref, sel_ref, keep_ref, got_ref,
    sum_ref, grown, back_s, *, scale,
):
    for f in range(2):
        at = f * 512
        grown[:, at : at + 128] = up_ref[:, f * 128 : f * 128 + 128]
        grown[:, at + 128 : at + 384] = cot_ref[:, f * 256 : f * 256 + 256]
        grown[:, at + 384 : at + 512] = down_ref[:, f * 128 : f * 128 + 128]
    z0 = z1 = 0.0
    for b in range(3):
        lo = (2 - b) * 128
        c0, c1 = grown[:, lo : lo + 256], grown[:, 512 + lo : 768 + lo]
        wa, wb = wa_ref[b * 384 : b * 384 + 384, :], wb_ref[b * 384 : b * 384 + 384, :]
        z0 = z0 + dot(wb, c0) + dot(wa, c1)
        z1 = z1 + dot(wb, c1)
    for f, z in enumerate((z0, z1)):
        z = z[128:256] + shifted(z[:128], 1) + shifted(z[256:], -1)
        back_s[0], back_s[1] = z[:, :128], z[:, 128:]
        a0, a1, a2, a3 = (
            jnp.concatenate([back_s[r, pl.ds(k, 32, stride=4), :] for r in range(2)], 1)
            for k in range(4)
        )
        s01, d01, s23, d23 = a0 + a1, a0 - a1, a2 + a3, a2 - a3
        act = jnp.concatenate([s01 + s23, d01 + d23, s01 - s23, d01 - d23], 0) * 0.5
        pre = pre_ref[:, f * 256 : f * 256 + 256]
        gate = jax.nn.sigmoid(pre)
        back = (act * gate * (1.0 + pre * (1.0 - gate))).astype(BF)
        if f == 0:
            late = dot(back, win_ref[:, :256], 1, 1)
        else:
            early = dot(back, win_ref[:, :256], 1, 1)
            late = late + dot(back, win_ref[:, 256:], 1, 1)
    for a, g in enumerate((early, late)):
        g = g * scale
        hi = g.astype(BF)
        lo = (g - hi.astype(F32)).astype(BF)
        total = 0.0
        for p in range(4):
            rows = slice(32 * p, 32 * p + 32)
            total = total + dot(hi[rows], sel_ref[p], 1, 1) + dot(lo[rows], sel_ref[p], 1, 1)
        sum_ref[2304 + 32 * a : 2336 + 32 * a, :] = total.astype(BF)
    sum_ref[2368:, :] = jnp.zeros((192, 128), BF)
    sum_ref[:2304, :] = (keep_ref[...].astype(F32) + got_ref[...].astype(F32)).astype(BF)


def share_kernel(got_ref, out_ref):
    count = got_ref.shape[0]
    total = got_ref[0].astype(F32)
    for i in range(1, count):
        total = total + got_ref[i].astype(F32)
    total = total.astype(BF)
    for i in range(count):
        out_ref[i] = total


def final_kernel(mine_ref, other_ref, g1_ref, g2_ref):
    core = lax.axis_index("band") % 2
    g2_ref[:1152, :] = jnp.zeros((1152, 256), F32)

    def put(refs):
        for a, ref in enumerate(refs):
            at = 1152 * (a + 1)
            g2_ref[at : at + 1152, :128] = ref[:1152, :].astype(F32)
            g2_ref[at : at + 1152, 128:] = ref[1152:2304, :].astype(F32)

    @pl.when(core == 0)
    def _():
        put((mine_ref, other_ref))

    @pl.when(core == 1)
    def _():
        put((other_ref, mine_ref))

    both = mine_ref[2304:2368, :].astype(F32) + other_ref[2304:2368, :].astype(F32)
    g1_ref[...] = jnp.zeros((12, 27, 32), F32)
    for a in range(2):
        taps = jnp.transpose(both[32 * a : 32 * a + 32, :])
        for c in range(12):
            g1_ref[c, 9 * a + 9 : 9 * a + 18, :] = taps[9 * c : 9 * c + 9, :]


def call(kernel, outs, scratch, flops, *args):
    return pl.pallas_call(
        kernel,
        out_shape=[jax.ShapeDtypeStruct(*o) for o in outs],
        in_specs=[pl.BlockSpec(memory_space=pltpu.VMEM)] * len(args),
        out_specs=[pl.BlockSpec(memory_space=pltpu.VMEM)] * len(outs),
        scratch_shapes=[pltpu.VMEM(*s) for s in scratch],
        compiler_params=pltpu.CompilerParams(vmem_limit_bytes=20 * 1024 * 1024),
        cost_estimate=pl.CostEstimate(flops=flops, bytes_accessed=1 << 20, transcendentals=0),
    )(*args)


def on_device(video, weight_one, weight_two, cotangent):
    n = lax.axis_size("band")
    up = [(i, i + 1) for i in range(n - 1)]
    down = [(j, i) for i, j in up]
    flip = [(i, i ^ 1) for i in range(n)]
    frames, half_rows, half_cols = video.shape[1], n * 4, video.shape[3] // 2
    scale_one = 1.0 / math.sqrt(frames * half_rows * half_cols)
    scale_two = 1.0 / math.sqrt(frames * (half_rows // 2) * (half_cols // 2))

    flat = video.reshape(48, 512)
    before, after = lax.ppermute(flat, "band", up), lax.ppermute(flat, "band", down)
    own = cotangent.reshape(64, 512)
    others = [lax.ppermute(own, "chan", [(i, i ^ k) for i in range(4)]) for k in (1, 2, 3)]
    w1 = weight_one[9:].reshape(2, 9, 12, 32).transpose(0, 2, 1, 3).reshape(2, 108, 32)
    w1 = jnp.pad(w1, ((0, 0), (0, 20), (0, 0)))
    wa, wb = weight_two[9:18].reshape(1152, 256), weight_two[18:].reshape(1152, 256)
    sel = jnp.asarray(select_matrix())
    (w1e,) = call(expand_kernel, [((128, 512), BF)], [], 1 << 20, w1, sel)
    xc, pre, win = call(
        forward_kernel,
        [((1152, 512), BF), ((128, 512), F32), ((256, 512), BF)],
        [((2, 256, 512), BF), ((4, 128, 128), F32)],
        1 << 30,
        before, flat, after, jnp.asarray(row_matrix()), jnp.asarray(column_matrix()), w1e,
    )

    def second_grad(*refs):
        second_grad_kernel(*refs, scale=scale_two)

    cot, last, first, keep, send = call(
        second_grad,
        [((256, 512), BF), ((256, 256), BF), ((256, 256), BF), ((2304, 128), BF), ((2304, 128), BF)],
        [],
        1 << 30,
        xc, own, *others,
    )
    above, below = lax.ppermute(last, "band", up), lax.ppermute(first, "band", down)
    got = lax.ppermute(send, "band", flip)
    (lat,) = call(latent_kernel, [((256, 512), BF)], [], 1 << 30, xc, wa, wb)
    latent = lax.psum_scatter(lat.reshape(4, 64, 512), "chan", scatter_dimension=0, tiled=True)
    latent = latent.reshape(64, 2, 2, 128)

    def backward(*refs):
        backward_kernel(*refs, scale=scale_one)

    (part,) = call(
        backward,
        [((2560, 128), BF)],
        [((256, 1024), BF), ((2, 128, 128), F32)],
        1 << 30,
        cot, above, below, pre, win, wa, wb, sel, keep, got,
    )
    half = n // 2
    groups = [[2 * i + c for i in range(half)] for c in range(2)]
    part = part.reshape(half, 2560 // half, 128)
    part = lax.all_to_all(part, "band", 0, 0, tiled=True, axis_index_groups=groups)
    (mine,) = call(share_kernel, [(part.shape, BF)], [], 1 << 20, part)
    mine = lax.all_to_all(mine, "band", 0, 0, tiled=True, axis_index_groups=groups)
    mine = mine.reshape(2560, 128)
    g1, g2 = call(
        final_kernel,
        [((12, 27, 32), F32), ((3456, 256), F32)],
        [],
        1 << 20,
        mine, lax.ppermute(mine, "band", flip),
    )
    return latent, jnp.transpose(g1, (1, 0, 2)), g2.reshape(27, 128, 256)


def solution(mesh):
    return jax.shard_map(
        on_device,
        mesh=mesh,
        in_specs=(
            P(None, None, "band", None),
            P(None, None, "chan"),
            P(None, "chan", None),
            P("chan", None, "band", None),
        ),
        out_specs=(P("chan", None, "band", None), P(None, None, "chan"), P(None, "chan", None)),
        check_vma=False,
    )
```

```python
import math

import jax
import jax.numpy as jnp
import ml_dtypes
import numpy as np
from jax import lax
from jax.experimental import pallas as pl
from jax.experimental.pallas import tpu as pltpu
from jax.sharding import PartitionSpec as P

BF = jnp.bfloat16
F32 = jnp.float32


def column_matrix():
    m = np.zeros((512, 4, 2, 128), np.float32)
    for s in range(4):
        for w in range(128):
            j = 2 * w - 1 + s
            if 0 <= j < 256:
                m[2 * j, s, :, w] = 0.5
                m[2 * j + 1, s, 0, w] = 0.5
                m[2 * j + 1, s, 1, w] = -0.5
    return m.reshape(512, 1024).astype(ml_dtypes.bfloat16)


def row_matrix():
    m = np.zeros((3, 2, 2, 4, 16, 48), np.float32)
    for tb in range(2):
        for f in range(2):
            for r in range(4):
                for wi in range(4):
                    for ch in range(3):
                        y = 2 * (2 * (r - 1) - 1 + wi) + tb + 8
                        m[y // 8, tb, f, r, wi * 3 + ch, ch * 16 + f * 8 + y % 8] = 1.0
    return m.reshape(3, 256, 48).astype(ml_dtypes.bfloat16)


def select_matrix():
    m = np.zeros((4, 128, 256), np.float32)
    for phr in range(2):
        for phc in range(2):
            for b in range(3):
                for e in range(3):
                    for ch in range(3):
                        for k in range(4):
                            row = (ch * 4 + k) * 9 + b * 3 + e
                            col = (k >> 1) * 128 + ((phc + e) * 2 + (k & 1)) * 16 + (phr + b) * 3 + ch
                            m[phr * 2 + phc, row, col] = 1.0
    return m.astype(ml_dtypes.bfloat16)


def dot(a, b, ca=1, cb=0):
    return lax.dot_general(a, b, (((ca,), (cb,)), ((), ())), preferred_element_type=F32)


def edges_kernel(video_ref, own_ref, up_ref, down_ref):
    for ref, row in ((up_ref, 1), (down_ref, 0)):
        ref[:48, :] = video_ref[...]
        for half in range(2):
            for f in range(2):
                ref[48:, half * 256 + f * 128 : half * 256 + f * 128 + 128] = own_ref[
                    half * 32 : half * 32 + 32, f * 256 + row * 128 : f * 256 + row * 128 + 128
                ]


def grown_kernel(own_ref, above_ref, below_ref, out_ref):
    for f in range(2):
        at = f * 512
        out_ref[:, at + 128 : at + 384] = own_ref[:, f * 256 : f * 256 + 256]
        for half in range(2):
            rows, lanes = slice(half * 32, half * 32 + 32), slice(half * 256 + f * 128, half * 256 + f * 128 + 128)
            out_ref[rows, at : at + 128] = above_ref[48:, lanes]
            out_ref[rows, at + 384 : at + 512] = below_ref[48:, lanes]


def stage_kernel(w1_ref, w2_ref, row_hbm, col_hbm, sel_hbm, _, w1e_ref, w2_out, row_ref, col_ref, sel_ref, sems):
    copies = [
        pltpu.make_async_copy(sel_hbm, sel_ref, sems.at[0]),
        pltpu.make_async_copy(row_hbm, row_ref, sems.at[1]),
        pltpu.make_async_copy(col_hbm, col_ref, sems.at[2]),
        pltpu.make_async_copy(w2_ref.at[pl.ds(1152, 2304)], w2_out, sems.at[3]),
    ]
    for copy in copies:
        copy.start()
    copies[0].wait()
    for p in range(4):
        for a in range(2):
            w1e_ref[32 * p : 32 * p + 32, 256 * a : 256 * a + 256] = dot(
                w1_ref[a], sel_ref[p], 0, 0
            ).astype(BF)
    for copy in copies[1:]:
        copy.wait()


def shifted(x, step):
    lanes = x.shape[1]
    lane = lax.broadcasted_iota(jnp.int32, x.shape, 1) % 128
    if step == -1:
        return jnp.where(lane == 0, 0.0, pltpu.roll(x, 1, 1))
    return jnp.where(lane == 127, 0.0, pltpu.roll(x, lanes - 1, 1))


def forward_kernel(
    prev_ref, own_ref, next_ref, row_ref, col_ref, w1_ref,
    xc_ref, pre_ref, win_ref, one, two,
):
    band = lax.axis_index("band")
    last = lax.axis_size("band") - 1
    v = (
        dot(row_ref[0], prev_ref[:48, :])
        + dot(row_ref[1], own_ref[...])
        + dot(row_ref[2], next_ref[:48, :])
    ).astype(BF)
    h = dot(v, col_ref[...])
    top, low = h[:128], h[128:]
    for pm, half in enumerate(((top + low).astype(BF), (top - low).astype(BF))):
        for f in range(2):
            for r in range(4):
                for st in range(8):
                    one[f, pm * 128 + st * 16 : pm * 128 + st * 16 + 16, r * 128 : r * 128 + 128] = half[
                        (f * 4 + r) * 16 : (f * 4 + r) * 16 + 16, st * 128 : st * 128 + 128
                    ]
    w1a, w1b = w1_ref[:, :256], w1_ref[:, 256:]
    pres = (dot(w1b, one[0]), dot(w1a, one[0]) + dot(w1b, one[1]))
    lane = lax.broadcasted_iota(jnp.int32, (32, 512), 1)
    keep = ((lane >= 128) | (band > 0)) & ((lane < 384) | (band < last))
    for f in range(2):
        pre = pres[f]
        pre_ref[:, f * 256 : f * 256 + 256] = pre[:, 128:384]
        win_ref[:, f * 256 : f * 256 + 256] = one[f, :, 128:384]
        act = pre * jax.nn.sigmoid(pre)
        p, q, r, s = act[:32], act[32:64], act[64:96], act[96:]
        pq, pmq, rs, rms = p + q, p - q, r + s, r - s
        parts = (pq + rs, pmq + rms, pq - rs, pmq - rms)
        for k in range(4):
            part = jnp.where(keep, parts[k] * 0.5, 0.0)
            for r in range(4):
                two[r, pl.ds(k, 32, stride=4), :] = part[:, r * 128 : r * 128 + 128]
        x = jnp.concatenate([two[r] for r in range(4)], 1)
        for e, xe in enumerate((shifted(x, -1), x, shifted(x, 1))):
            xe = xe.astype(BF)
            for b in range(3):
                at = (b * 3 + e) * 128
                xc_ref[at : at + 128, f * 256 : f * 256 + 256] = xe[:, b * 128 : b * 128 + 256]


def latent_kernel(xc_ref, w2_ref, lat_ref):
    out = dot(w2_ref[1152:, :], xc_ref[...], 0, 0)
    more = dot(w2_ref[:1152, :], xc_ref[:, :256], 0, 0)
    lat_ref[:, :256] = out[:, :256].astype(BF)
    lat_ref[:, 256:] = (out[:, 256:] + more).astype(BF)


def second_grad_kernel(
    xc_ref, c0_ref, c1_ref, c2_ref, c3_ref, cot_ref, keep_ref, send_ref, *, scale
):
    chan = lax.axis_index("chan")
    core = lax.axis_index("band") % 2
    for k, ref in enumerate((c0_ref, c1_ref, c2_ref, c3_ref)):
        cot_ref[pl.ds(pl.multiple_of((chan ^ k) * 64, 64), 64), :] = ref[...]

    def put(early_ref, late_ref):
        c1 = cot_ref[:, 640:896]
        early = dot(xc_ref[:, :256], c1, 1, 1) * scale
        late = (dot(xc_ref[:, :256], cot_ref[:, 128:384], 1, 1) + dot(xc_ref[:, 256:], c1, 1, 1)) * scale
        for ref, g in ((early_ref, early), (late_ref, late)):
            ref[:1152, :] = g[:, :128].astype(BF)
            ref[1152:, :] = g[:, 128:].astype(BF)

    @pl.when(core == 0)
    def _():
        put(keep_ref, send_ref)

    @pl.when(core == 1)
    def _():
        put(send_ref, keep_ref)


def backward_kernel(
    grown, pre_ref, win_ref, w2_ref, sel_ref, keep_ref, got_ref, _, sum_ref, back_s, *, scale
):
    z0 = z1 = 0.0
    for b in range(3):
        lo = (2 - b) * 128
        c0, c1 = grown[:, lo : lo + 256], grown[:, 512 + lo : 768 + lo]
        wa = w2_ref[b * 384 : b * 384 + 384, :]
        wb = w2_ref[1152 + b * 384 : 1536 + b * 384, :]
        z0 = z0 + dot(wb, c0) + dot(wa, c1)
        z1 = z1 + dot(wb, c1)
    for f, z in enumerate((z0, z1)):
        z = z[128:256] + shifted(z[:128], 1) + shifted(z[256:], -1)
        back_s[0], back_s[1] = z[:, :128], z[:, 128:]
        a0, a1, a2, a3 = (
            jnp.concatenate([back_s[r, pl.ds(k, 32, stride=4), :] for r in range(2)], 1)
            for k in range(4)
        )
        s01, d01, s23, d23 = a0 + a1, a0 - a1, a2 + a3, a2 - a3
        act = jnp.concatenate([s01 + s23, d01 + d23, s01 - s23, d01 - d23], 0) * 0.5
        pre = pre_ref[:, f * 256 : f * 256 + 256]
        gate = jax.nn.sigmoid(pre)
        back = (act * gate * (1.0 + pre * (1.0 - gate))).astype(BF)
        if f == 0:
            late = dot(back, win_ref[:, :256], 1, 1)
        else:
            early = dot(back, win_ref[:, :256], 1, 1)
            late = late + dot(back, win_ref[:, 256:], 1, 1)
    for a, g in enumerate((early, late)):
        g = g * scale
        hi = g.astype(BF)
        lo = (g - hi.astype(F32)).astype(BF)
        total = 0.0
        for p in range(4):
            rows = slice(32 * p, 32 * p + 32)
            total = total + dot(hi[rows], sel_ref[p], 1, 1) + dot(lo[rows], sel_ref[p], 1, 1)
        sum_ref[2304 + 32 * a : 2336 + 32 * a, :] = total.astype(BF)
    sum_ref[2368:, :] = jnp.zeros((192, 128), BF)
    sum_ref[:2304, :] = (keep_ref[...].astype(F32) + got_ref[...].astype(F32)).astype(BF)


def share_kernel(got_ref, out_ref):
    count = got_ref.shape[0]
    total = got_ref[0].astype(F32)
    for i in range(1, count):
        total = total + got_ref[i].astype(F32)
    total = total.astype(BF)
    for i in range(count):
        out_ref[i] = total


def first_half_kernel(mine_ref, g2_ref, zero, own, sems):
    core = lax.axis_index("band") % 2
    zero[...] = jnp.zeros((1152, 256), F32)
    clear = pltpu.make_async_copy(zero, g2_ref.at[0], sems.at[0])
    clear.start()
    own[:, :128] = mine_ref[:1152, :].astype(F32)
    own[:, 128:] = mine_ref[1152:2304, :].astype(F32)
    copy = pltpu.make_async_copy(own, g2_ref.at[1 + core], sems.at[1])
    copy.start()
    clear.wait()
    copy.wait()


def other_half_kernel(_, mine_ref, other_ref, g2_ref, g1_ref, half, sem):
    core = lax.axis_index("band") % 2
    half[:, :128] = other_ref[:1152, :].astype(F32)
    half[:, 128:] = other_ref[1152:2304, :].astype(F32)
    copy = pltpu.make_async_copy(half, g2_ref.at[2 - core], sem)
    copy.start()
    both = mine_ref[2304:2368, :].astype(F32) + other_ref[2304:2368, :].astype(F32)
    g1_ref[...] = jnp.zeros((12, 27, 32), F32)
    for a in range(2):
        taps = jnp.transpose(both[32 * a : 32 * a + 32, :])
        for c in range(12):
            g1_ref[c, 9 * a + 9 : 9 * a + 18, :] = taps[9 * c : 9 * c + 9, :]
    copy.wait()


VMEM, HBM = pltpu.VMEM, pltpu.HBM


def call(kernel, outs, scratch, flops, *args, far=(), far_out=(), aliases=None):
    return pl.pallas_call(
        kernel,
        out_shape=[jax.ShapeDtypeStruct(*o) for o in outs],
        in_specs=[pl.BlockSpec(memory_space=HBM if i in far else VMEM) for i in range(len(args))],
        out_specs=[pl.BlockSpec(memory_space=HBM if i in far_out else VMEM) for i in range(len(outs))],
        scratch_shapes=[s if not isinstance(s, tuple) else pltpu.VMEM(*s) for s in scratch],
        input_output_aliases=aliases or {},
        compiler_params=pltpu.CompilerParams(vmem_limit_bytes=20 * 1024 * 1024),
        cost_estimate=pl.CostEstimate(flops=flops, bytes_accessed=1 << 20, transcendentals=0),
    )(*args)


def on_device(video, weight_one, weight_two, cotangent):
    n = lax.axis_size("band")
    up = [(i, i + 1) for i in range(n - 1)]
    down = [(j, i) for i, j in up]
    flip = [(i, i ^ 1) for i in range(n)]
    frames, half_rows, half_cols = video.shape[1], n * 4, video.shape[3] // 2
    scale_one = 1.0 / math.sqrt(frames * half_rows * half_cols)
    scale_two = 1.0 / math.sqrt(frames * (half_rows // 2) * (half_cols // 2))

    flat, own = video.reshape(48, 512), cotangent.reshape(64, 512)
    to_next, to_prev = call(edges_kernel, [((80, 512), BF)] * 2, [], 1 << 20, flat, own)
    before, after = lax.ppermute(to_next, "band", up), lax.ppermute(to_prev, "band", down)
    (grown,) = call(grown_kernel, [((64, 1024), BF)], [], 1 << 20, own, before, after)
    others = [lax.ppermute(grown, "chan", [(i, i ^ k) for i in range(4)]) for k in (1, 2, 3)]
    w1 = weight_one[9:].reshape(2, 9, 12, 32).transpose(0, 2, 1, 3).reshape(2, 108, 32)
    w1 = jnp.pad(w1, ((0, 0), (0, 20), (0, 0)))
    w1e, w2, rows, cols, sel = call(
        stage_kernel,
        [((128, 512), BF), ((2304, 256), BF), ((3, 256, 48), BF), ((512, 1024), BF), ((4, 128, 256), BF)],
        [pltpu.SemaphoreType.DMA((4,))],
        1 << 20,
        w1, weight_two.reshape(3456, 256), jnp.asarray(row_matrix()), jnp.asarray(column_matrix()),
        jnp.asarray(select_matrix()), grown,
        far=(1, 2, 3, 4, 5),
    )
    xc, pre, win = call(
        forward_kernel,
        [((1152, 512), BF), ((128, 512), F32), ((256, 512), BF)],
        [((2, 256, 512), BF), ((4, 128, 128), F32)],
        1 << 30,
        before, flat, after, rows, cols, w1e,
    )

    def second_grad(*refs):
        second_grad_kernel(*refs, scale=scale_two)

    cot, keep, send = call(
        second_grad,
        [((256, 1024), BF), ((2304, 128), BF), ((2304, 128), BF)],
        [],
        1 << 30,
        xc, grown, *others,
    )
    got = lax.ppermute(send, "band", flip)
    (lat,) = call(latent_kernel, [((256, 512), BF)], [], 1 << 30, xc, w2)
    latent = lax.psum_scatter(lat.reshape(4, 64, 512), "chan", scatter_dimension=0, tiled=True)
    latent = latent.reshape(64, 2, 2, 128)

    def backward(*refs):
        backward_kernel(*refs, scale=scale_one)

    (part,) = call(
        backward,
        [((2560, 128), BF)],
        [((2, 128, 128), F32)],
        1 << 30,
        cot, pre, win, w2, sel, keep, got, lat,
        far=(7,),
    )
    half = n // 2
    groups = [[2 * i + c for i in range(half)] for c in range(2)]
    part = part.reshape(half, 2560 // half, 128)
    part = lax.all_to_all(part, "band", 0, 0, tiled=True, axis_index_groups=groups)
    (mine,) = call(share_kernel, [(part.shape, BF)], [], 1 << 20, part)
    mine = lax.all_to_all(mine, "band", 0, 0, tiled=True, axis_index_groups=groups)
    mine = mine.reshape(2560, 128)
    other = lax.ppermute(mine, "band", flip)
    (g2,) = call(
        first_half_kernel,
        [((3, 1152, 256), F32)],
        [((1152, 256), F32), ((1152, 256), F32), pltpu.SemaphoreType.DMA((2,))],
        1 << 20,
        mine,
        far_out=(0,),
    )
    g2, g1 = call(
        other_half_kernel,
        [((3, 1152, 256), F32), ((12, 27, 32), F32)],
        [((1152, 256), F32), pltpu.SemaphoreType.DMA],
        1 << 20,
        g2, mine, other,
        far=(0,), far_out=(0,), aliases={0: 0},
    )
    return latent, jnp.transpose(g1, (1, 0, 2)), g2.reshape(27, 128, 256)


def solution(mesh):
    return jax.shard_map(
        on_device,
        mesh=mesh,
        in_specs=(
            P(None, None, "band", None),
            P(None, None, "chan"),
            P(None, "chan", None),
            P("chan", None, "band", None),
        ),
        out_specs=(P("chan", None, "band", None), P(None, None, "chan"), P(None, "chan", None)),
        check_vma=False,
    )
```

```python
import math

import jax
import jax.numpy as jnp
import ml_dtypes
import numpy as np
from jax import lax
from jax.experimental import pallas as pl
from jax.experimental.pallas import tpu as pltpu
from jax.sharding import PartitionSpec as P

BF = jnp.bfloat16
F32 = jnp.float32


def column_matrix():
    m = np.zeros((512, 4, 2, 128), np.float32)
    for s in range(4):
        for w in range(128):
            j = 2 * w - 1 + s
            if 0 <= j < 256:
                m[2 * j, s, :, w] = 0.5
                m[2 * j + 1, s, 0, w] = 0.5
                m[2 * j + 1, s, 1, w] = -0.5
    return m.reshape(512, 1024).astype(ml_dtypes.bfloat16)


def row_matrix():
    m = np.zeros((3, 2, 2, 4, 16, 48), np.float32)
    for tb in range(2):
        for f in range(2):
            for r in range(4):
                for wi in range(4):
                    for ch in range(3):
                        y = 2 * (2 * (r - 1) - 1 + wi) + tb + 8
                        m[y // 8, tb, f, r, wi * 3 + ch, ch * 16 + f * 8 + y % 8] = 1.0
    return m.reshape(3, 256, 48).astype(ml_dtypes.bfloat16)


def select_matrix():
    m = np.zeros((4, 128, 256), np.float32)
    for phr in range(2):
        for phc in range(2):
            for b in range(3):
                for e in range(3):
                    for ch in range(3):
                        for k in range(4):
                            row = (ch * 4 + k) * 9 + b * 3 + e
                            col = (k >> 1) * 128 + ((phc + e) * 2 + (k & 1)) * 16 + (phr + b) * 3 + ch
                            m[phr * 2 + phc, row, col] = 1.0
    return m.astype(ml_dtypes.bfloat16)


def constants():
    rows = np.zeros((256, 1024), ml_dtypes.bfloat16)
    for part, block in enumerate(row_matrix()):
        rows[:, part * 128 : part * 128 + 48] = block
    sel = np.concatenate(list(select_matrix()), axis=1)
    return np.concatenate([column_matrix(), sel, rows], axis=0)


def selection(fixed_ref, p):
    return fixed_ref[512:640, 256 * p : 256 * p + 256]


def dot(a, b, ca=1, cb=0):
    return lax.dot_general(a, b, (((ca,), (cb,)), ((), ())), preferred_element_type=F32)


def edges_kernel(video_ref, own_ref, up_ref, down_ref):
    for ref, row in ((up_ref, 1), (down_ref, 0)):
        ref[:48, :] = video_ref[...]
        for half in range(2):
            for f in range(2):
                ref[48:, half * 256 + f * 128 : half * 256 + f * 128 + 128] = own_ref[
                    half * 32 : half * 32 + 32, f * 256 + row * 128 : f * 256 + row * 128 + 128
                ]


def grown_kernel(own_ref, above_ref, below_ref, out_ref):
    for f in range(2):
        at = f * 512
        out_ref[:, at + 128 : at + 384] = own_ref[:, f * 256 : f * 256 + 256]
        for half in range(2):
            rows, lanes = slice(half * 32, half * 32 + 32), slice(half * 256 + f * 128, half * 256 + f * 128 + 128)
            out_ref[rows, at : at + 128] = above_ref[48:, lanes]
            out_ref[rows, at + 384 : at + 512] = below_ref[48:, lanes]


def expand_kernel(w1_ref, fixed_ref, _, out_ref):
    for p in range(4):
        for a in range(2):
            out_ref[32 * p : 32 * p + 32, 256 * a : 256 * a + 256] = dot(
                w1_ref[a], selection(fixed_ref, p), 0, 0
            ).astype(BF)


def shifted(x, step):
    lanes = x.shape[1]
    lane = lax.broadcasted_iota(jnp.int32, x.shape, 1) % 128
    if step == -1:
        return jnp.where(lane == 0, 0.0, pltpu.roll(x, 1, 1))
    return jnp.where(lane == 127, 0.0, pltpu.roll(x, lanes - 1, 1))


def forward_kernel(
    prev_ref, own_ref, next_ref, fixed_ref, w1_ref,
    xc_ref, pre_ref, win_ref, one, two,
):
    band = lax.axis_index("band")
    last = lax.axis_size("band") - 1
    v = (
        dot(fixed_ref[640:, :48], prev_ref[:48, :])
        + dot(fixed_ref[640:, 128:176], own_ref[...])
        + dot(fixed_ref[640:, 256:304], next_ref[:48, :])
    ).astype(BF)
    h = dot(v, fixed_ref[:512, :])
    top, low = h[:128], h[128:]
    for pm, half in enumerate(((top + low).astype(BF), (top - low).astype(BF))):
        for f in range(2):
            for r in range(4):
                for st in range(8):
                    one[f, pm * 128 + st * 16 : pm * 128 + st * 16 + 16, r * 128 : r * 128 + 128] = half[
                        (f * 4 + r) * 16 : (f * 4 + r) * 16 + 16, st * 128 : st * 128 + 128
                    ]
    w1a, w1b = w1_ref[:, :256], w1_ref[:, 256:]
    pres = (dot(w1b, one[0]), dot(w1a, one[0]) + dot(w1b, one[1]))
    lane = lax.broadcasted_iota(jnp.int32, (32, 512), 1)
    keep = ((lane >= 128) | (band > 0)) & ((lane < 384) | (band < last))
    for f in range(2):
        pre = pres[f]
        pre_ref[:, f * 256 : f * 256 + 256] = pre[:, 128:384]
        win_ref[:, f * 256 : f * 256 + 256] = one[f, :, 128:384]
        act = pre * jax.nn.sigmoid(pre)
        p, q, r, s = act[:32], act[32:64], act[64:96], act[96:]
        pq, pmq, rs, rms = p + q, p - q, r + s, r - s
        parts = (pq + rs, pmq + rms, pq - rs, pmq - rms)
        for k in range(4):
            part = jnp.where(keep, parts[k] * 0.5, 0.0)
            for r in range(4):
                two[r, pl.ds(k, 32, stride=4), :] = part[:, r * 128 : r * 128 + 128]
        x = jnp.concatenate([two[r] for r in range(4)], 1)
        for e, xe in enumerate((shifted(x, -1), x, shifted(x, 1))):
            xe = xe.astype(BF)
            for b in range(3):
                at = (b * 3 + e) * 128
                xc_ref[at : at + 128, f * 256 : f * 256 + 256] = xe[:, b * 128 : b * 128 + 256]


def latent_kernel(xc_ref, w2_ref, p0_ref, p1_ref, p2_ref, p3_ref, lat):
    out = dot(w2_ref[2304:, :], xc_ref[...], 0, 0)
    more = dot(w2_ref[1152:2304, :], xc_ref[:, :256], 0, 0)
    lat[:, :256] = out[:, :256].astype(BF)
    lat[:, 256:] = (out[:, 256:] + more).astype(BF)
    chan = lax.axis_index("chan")
    for k, ref in enumerate((p0_ref, p1_ref, p2_ref, p3_ref)):
        ref[...] = lat[pl.ds(pl.multiple_of((chan ^ k) * 64, 64), 64), :]


def second_grad_kernel(
    xc_ref, c0_ref, c1_ref, c2_ref, c3_ref, _, cot_ref, keep_ref, send_ref, *, scale
):
    chan = lax.axis_index("chan")
    core = lax.axis_index("band") % 2
    for k, ref in enumerate((c0_ref, c1_ref, c2_ref, c3_ref)):
        cot_ref[pl.ds(pl.multiple_of((chan ^ k) * 64, 64), 64), :] = ref[...]

    def put(early_ref, late_ref):
        c1 = cot_ref[:, 640:896]
        early = dot(xc_ref[:, :256], c1, 1, 1) * scale
        late = (dot(xc_ref[:, :256], cot_ref[:, 128:384], 1, 1) + dot(xc_ref[:, 256:], c1, 1, 1)) * scale
        for ref, g in ((early_ref, early), (late_ref, late)):
            ref[:1152, :] = g[:, :128].astype(BF)
            ref[1152:, :] = g[:, 128:].astype(BF)

    @pl.when(core == 0)
    def _():
        put(keep_ref, send_ref)

    @pl.when(core == 1)
    def _():
        put(send_ref, keep_ref)


def backward_kernel(
    grown, pre_ref, win_ref, w2_ref, fixed_ref, _, g1_ref, back_s, *, scale
):
    z0 = z1 = 0.0
    for b in range(3):
        lo = (2 - b) * 128
        c0, c1 = grown[:, lo : lo + 256], grown[:, 512 + lo : 768 + lo]
        wa = w2_ref[1152 + b * 384 : 1536 + b * 384, :]
        wb = w2_ref[2304 + b * 384 : 2688 + b * 384, :]
        z0 = z0 + dot(wb, c0) + dot(wa, c1)
        z1 = z1 + dot(wb, c1)
    for f, z in enumerate((z0, z1)):
        z = z[128:256] + shifted(z[:128], 1) + shifted(z[256:], -1)
        back_s[0], back_s[1] = z[:, :128], z[:, 128:]
        a0, a1, a2, a3 = (
            jnp.concatenate([back_s[r, pl.ds(k, 32, stride=4), :] for r in range(2)], 1)
            for k in range(4)
        )
        s01, d01, s23, d23 = a0 + a1, a0 - a1, a2 + a3, a2 - a3
        act = jnp.concatenate([s01 + s23, d01 + d23, s01 - s23, d01 - d23], 0) * 0.5
        pre = pre_ref[:, f * 256 : f * 256 + 256]
        gate = jax.nn.sigmoid(pre)
        back = (act * gate * (1.0 + pre * (1.0 - gate))).astype(BF)
        if f == 0:
            late = dot(back, win_ref[:, :256], 1, 1)
        else:
            early = dot(back, win_ref[:, :256], 1, 1)
            late = late + dot(back, win_ref[:, 256:], 1, 1)
    for a, g in enumerate((early, late)):
        g = g * scale
        hi = g.astype(BF)
        lo = (g - hi.astype(F32)).astype(BF)
        total = 0.0
        for p in range(4):
            rows = slice(32 * p, 32 * p + 32)
            total = total + dot(hi[rows], selection(fixed_ref, p), 1, 1)
            total = total + dot(lo[rows], selection(fixed_ref, p), 1, 1)
        g1_ref[32 * a : 32 * a + 32, :] = total.astype(BF)


def join_kernel(keep_ref, got_ref, g1_ref, sum_ref):
    sum_ref[:2304, :] = (keep_ref[...].astype(F32) + got_ref[...].astype(F32)).astype(BF)
    sum_ref[2304:2368, :] = g1_ref[...]
    sum_ref[2368:, :] = jnp.zeros((192, 128), BF)


def share_kernel(got_ref, l0_ref, l1_ref, l2_ref, l3_ref, out_ref, lat_ref):
    lat = l0_ref[...].astype(F32) + l1_ref[...].astype(F32)
    lat_ref[...] = (lat + l2_ref[...].astype(F32) + l3_ref[...].astype(F32)).astype(BF)
    count = got_ref.shape[0]
    total = got_ref[0].astype(F32)
    for i in range(1, count):
        total = total + got_ref[i].astype(F32)
    total = total.astype(BF)
    for i in range(count):
        out_ref[i] = total


def first_half_kernel(mine_ref, g2_ref, zero, own, sems):
    core = lax.axis_index("band") % 2
    zero[...] = jnp.zeros((1152, 256), F32)
    clear = pltpu.make_async_copy(zero, g2_ref.at[0], sems.at[0])
    clear.start()
    own[:, :128] = mine_ref[:1152, :].astype(F32)
    own[:, 128:] = mine_ref[1152:2304, :].astype(F32)
    copy = pltpu.make_async_copy(own, g2_ref.at[1 + core], sems.at[1])
    copy.start()
    clear.wait()
    copy.wait()


def other_half_kernel(_, mine_ref, other_ref, g2_ref, g1_ref, half, sem):
    core = lax.axis_index("band") % 2
    half[:, :128] = other_ref[:1152, :].astype(F32)
    half[:, 128:] = other_ref[1152:2304, :].astype(F32)
    copy = pltpu.make_async_copy(half, g2_ref.at[2 - core], sem)
    copy.start()
    both = mine_ref[2304:2368, :].astype(F32) + other_ref[2304:2368, :].astype(F32)
    g1_ref[...] = jnp.zeros((12, 27, 32), F32)
    for a in range(2):
        taps = jnp.transpose(both[32 * a : 32 * a + 32, :])
        for c in range(12):
            g1_ref[c, 9 * a + 9 : 9 * a + 18, :] = taps[9 * c : 9 * c + 9, :]
    copy.wait()


VMEM, HBM = pltpu.VMEM, pltpu.HBM


def call(kernel, outs, scratch, flops, *args, far=(), far_out=(), aliases=None):
    return pl.pallas_call(
        kernel,
        out_shape=[jax.ShapeDtypeStruct(*o) for o in outs],
        in_specs=[pl.BlockSpec(memory_space=HBM if i in far else VMEM) for i in range(len(args))],
        out_specs=[pl.BlockSpec(memory_space=HBM if i in far_out else VMEM) for i in range(len(outs))],
        scratch_shapes=[s if not isinstance(s, tuple) else pltpu.VMEM(*s) for s in scratch],
        input_output_aliases=aliases or {},
        compiler_params=pltpu.CompilerParams(vmem_limit_bytes=20 * 1024 * 1024),
        cost_estimate=pl.CostEstimate(flops=flops, bytes_accessed=1 << 20, transcendentals=0),
    )(*args)


def on_device(video, weight_one, weight_two, cotangent):
    n = lax.axis_size("band")
    up = [(i, i + 1) for i in range(n - 1)]
    down = [(j, i) for i, j in up]
    flip = [(i, i ^ 1) for i in range(n)]
    frames, half_rows, half_cols = video.shape[1], n * 4, video.shape[3] // 2
    scale_one = 1.0 / math.sqrt(frames * half_rows * half_cols)
    scale_two = 1.0 / math.sqrt(frames * (half_rows // 2) * (half_cols // 2))

    flat, own = video.reshape(48, 512), cotangent.reshape(64, 512)
    to_next, to_prev = call(edges_kernel, [((80, 512), BF)] * 2, [], 1 << 20, flat, own)
    before, after = lax.ppermute(to_next, "band", up), lax.ppermute(to_prev, "band", down)
    (grown,) = call(grown_kernel, [((64, 1024), BF)], [], 1 << 20, own, before, after)
    others = [lax.ppermute(grown, "chan", [(i, i ^ k) for i in range(4)]) for k in (1, 2, 3)]
    w1 = weight_one[9:].reshape(2, 9, 12, 32).transpose(0, 2, 1, 3).reshape(2, 108, 32)
    w1 = jnp.pad(w1, ((0, 0), (0, 20), (0, 0)))
    fixed = jnp.asarray(constants())
    w2 = weight_two.reshape(3456, 256)
    (w1e,) = call(expand_kernel, [((128, 512), BF)], [], 1 << 20, w1, fixed, grown, far=(2,))
    xc, pre, win = call(
        forward_kernel,
        [((1152, 512), BF), ((128, 512), F32), ((256, 512), BF)],
        [((2, 256, 512), BF), ((4, 128, 128), F32)],
        1 << 30,
        before, flat, after, fixed, w1e,
    )

    lats = call(latent_kernel, [((64, 512), BF)] * 4, [((256, 512), BF)], 1 << 30, xc, w2)
    lats = [lats[0]] + [
        lax.ppermute(lats[k], "chan", [(i, i ^ k) for i in range(4)]) for k in (1, 2, 3)
    ]

    def second_grad(*refs):
        second_grad_kernel(*refs, scale=scale_two)

    cot, keep, send = call(
        second_grad,
        [((256, 1024), BF), ((2304, 128), BF), ((2304, 128), BF)],
        [],
        1 << 30,
        xc, grown, *others, lats[0],
        far=(5,),
    )
    got = lax.ppermute(send, "band", flip)

    def backward(*refs):
        backward_kernel(*refs, scale=scale_one)

    (g1,) = call(
        backward, [((64, 128), BF)], [((2, 128, 128), F32)], 1 << 30,
        cot, pre, win, w2, fixed, keep,
        far=(5,),
    )
    (part,) = call(join_kernel, [((2560, 128), BF)], [], 1 << 20, keep, got, g1)
    half = n // 2
    groups = [[2 * i + c for i in range(half)] for c in range(2)]
    part = part.reshape(half, 2560 // half, 128)
    part = lax.all_to_all(part, "band", 0, 0, tiled=True, axis_index_groups=groups)
    mine, latent = call(
        share_kernel, [(part.shape, BF), ((64, 512), BF)], [], 1 << 20, part, *lats
    )
    latent = latent.reshape(64, 2, 2, 128)
    mine = lax.all_to_all(mine, "band", 0, 0, tiled=True, axis_index_groups=groups)
    mine = mine.reshape(2560, 128)
    other = lax.ppermute(mine, "band", flip)
    (g2,) = call(
        first_half_kernel,
        [((3, 1152, 256), F32)],
        [((1152, 256), F32), ((1152, 256), F32), pltpu.SemaphoreType.DMA((2,))],
        1 << 20,
        mine,
        far_out=(0,),
    )
    g2, g1 = call(
        other_half_kernel,
        [((3, 1152, 256), F32), ((12, 27, 32), F32)],
        [((1152, 256), F32), pltpu.SemaphoreType.DMA],
        1 << 20,
        g2, mine, other,
        far=(0,), far_out=(0,), aliases={0: 0},
    )
    return latent, jnp.transpose(g1, (1, 0, 2)), g2.reshape(27, 128, 256)


def solution(mesh):
    return jax.shard_map(
        on_device,
        mesh=mesh,
        in_specs=(
            P(None, None, "band", None),
            P(None, None, "chan"),
            P(None, "chan", None),
            P("chan", None, "band", None),
        ),
        out_specs=(P("chan", None, "band", None), P(None, None, "chan"), P(None, "chan", None)),
        check_vma=False,
    )
```

```python
import math

import jax
import jax.numpy as jnp
from jax import lax
from jax.experimental import pallas as pl
from jax.experimental.pallas import tpu as pltpu
from jax.sharding import PartitionSpec as P

BF = jnp.bfloat16
F32 = jnp.float32


def iota(shape, axis):
    return lax.broadcasted_iota(jnp.int32, shape, axis)


def matrix_kernel(col_ref, row_ref, sel_ref):
    u, w = iota((512, 128), 0), iota((512, 128), 1)
    for s in range(2):
        hit = ((u >> 2) == w) & (((u >> 1) & 1) == s)
        for t in range(2):
            value = 0.5 if t == 0 else jnp.where((u & 1) == 1, -0.5, 0.5)
            at = (s * 2 + t) * 128
            col_ref[:, at : at + 128] = jnp.where(hit, value, 0.0).astype(BF)
    at, lane = iota((256, 128), 0), iota((256, 128), 1)
    m, r, f, tb = at & 15, (at >> 4) & 3, (at >> 6) & 1, at >> 7
    wi = (m * 11) >> 5
    y = 4 * r + 2 * wi + tb + 2
    for part in range(3):
        hit = (lane == (m - 3 * wi) * 16 + f * 8 + y - 8 * part) & (m < 12)
        hit = hit & (y >= 8 * part) & (y < 8 * part + 8)
        row_ref[part] = jnp.where(hit, 1.0, 0.0).astype(BF)
    at, lane = iota((128, 256), 0), iota((128, 256), 1)
    c = (at * 57) >> 9
    tap = at - 9 * c
    b = (tap * 11) >> 5
    e = tap - 3 * b
    target = ((c >> 1) & 1) * 128 + (e * 2 + (c & 1)) * 16 + b * 3 + (c >> 2)
    for p in range(4):
        hit = (lane == target + (p & 1) * 32 + (p >> 1) * 3) & (at < 108)
        sel_ref[p] = jnp.where(hit, 1.0, 0.0).astype(BF)


def dot(a, b, ca=1, cb=0):
    return lax.dot_general(a, b, (((ca,), (cb,)), ((), ())), preferred_element_type=F32)


def edges_kernel(video_ref, own_ref, up_ref, down_ref, rows):
    rows[...] = own_ref[...].astype(F32)
    for ref, r in ((up_ref, 1), (down_ref, 0)):
        ref[:48, :] = video_ref[...]
        edge = rows[pl.ds(r, 128, stride=2), :].astype(BF)
        for i in range(4):
            ref[48:, i * 128 : i * 128 + 128] = edge[i * 32 : i * 32 + 32, :]


def outer_kernel(above_ref, below_ref, out_ref):
    for side, ref in enumerate((above_ref, below_ref)):
        for i in range(4):
            at = side * 128 + i * 32
            out_ref[at : at + 32, :] = ref[48:, i * 128 : i * 128 + 128]


def shifted(x, step):
    lanes = x.shape[1]
    lane = lax.broadcasted_iota(jnp.int32, x.shape, 1) % 128
    if step == -1:
        return jnp.where(lane == 0, 0.0, pltpu.roll(x, 1, 1))
    return jnp.where(lane == 127, 0.0, pltpu.roll(x, lanes - 1, 1))


def forward_kernel(
    prev_ref, own_ref, next_ref, col_ref, row_ref, sel_ref, w1_ref,
    xc_ref, pre_ref, win_ref, one, two,
):
    band = lax.axis_index("band")
    last = lax.axis_size("band") - 1
    v = (
        dot(row_ref[0, :, :48], prev_ref[:48, :])
        + dot(row_ref[1, :, :48], own_ref[...])
        + dot(row_ref[2, :, :48], next_ref[:48, :])
    ).astype(BF)
    h = dot(v, col_ref[...])
    top, low = h[:128], h[128:]
    for pm, half in enumerate((top + low, top - low)):
        even, odd = half[:, :256], half[:, 256:]
        streams = (shifted(odd, -1), even, odd, shifted(even, 1))
        for st in range(8):
            part = streams[st // 2][:, (st % 2) * 128 : (st % 2) * 128 + 128].astype(BF)
            for f in range(2):
                for r in range(4):
                    at = (f * 4 + r) * 16
                    one[f, pm * 128 + st * 16 : pm * 128 + st * 16 + 16, r * 128 : r * 128 + 128] = part[
                        at : at + 16, :
                    ]
    w1a, w1b = (
        jnp.concatenate([dot(w1_ref[a], sel_ref[p], 0, 0) for p in range(4)], 0).astype(BF)
        for a in range(2)
    )
    pres = (dot(w1b, one[0]), dot(w1a, one[0]) + dot(w1b, one[1]))
    lane = lax.broadcasted_iota(jnp.int32, (32, 512), 1)
    keep = ((lane >= 128) | (band > 0)) & ((lane < 384) | (band < last))
    for f in range(2):
        pre = pres[f]
        pre_ref[:, f * 256 : f * 256 + 256] = pre[:, 128:384]
        win_ref[:, f * 256 : f * 256 + 256] = one[f, :, 128:384]
        act = pre * jax.nn.sigmoid(pre)
        p, q, r, s = act[:32], act[32:64], act[64:96], act[96:]
        pq, pmq, rs, rms = p + q, p - q, r + s, r - s
        parts = (pq + rs, pmq + rms, pq - rs, pmq - rms)
        for k in range(4):
            part = jnp.where(keep, parts[k] * 0.5, 0.0)
            for r in range(4):
                two[r, pl.ds(k, 32, stride=4), :] = part[:, r * 128 : r * 128 + 128]
        x = jnp.concatenate([two[r] for r in range(4)], 1)
        for e, xe in enumerate((shifted(x, -1), x, shifted(x, 1))):
            xe = xe.astype(BF)
            for b in range(3):
                at = (b * 3 + e) * 128
                xc_ref[at : at + 128, f * 256 : f * 256 + 256] = xe[:, b * 128 : b * 128 + 256]


def latent_kernel(xc_ref, w2_ref, keep_ref, send_ref, lat):
    out = dot(w2_ref[2304:, :], xc_ref[...], 0, 0)
    more = dot(w2_ref[1152:2304, :], xc_ref[:, :256], 0, 0)
    lat[:, :256] = out[:, :256].astype(BF)
    lat[:, 256:] = (out[:, 256:] + more).astype(BF)
    chan = lax.axis_index("chan")
    for k in range(4):
        ref = send_ref if k % 2 else keep_ref
        ref[k // 2] = lat[pl.ds(pl.multiple_of((chan ^ k) * 64, 64), 64), :]


def second_grad_kernel(
    xc_ref, c0_ref, c1_ref, c2_ref, c3_ref, e0_ref, e1_ref, e2_ref, e3_ref, _,
    grown, keep_ref, send_ref, rows, *, scale
):
    chan = lax.axis_index("chan")
    core = lax.axis_index("band") % 2
    for k, ref in enumerate((c0_ref, c1_ref, c2_ref, c3_ref)):
        rows[...] = ref[...].astype(F32)
        at = pl.multiple_of((chan ^ k) * 64, 64)
        for i in range(4):
            lane = (i // 2) * 512 + (i % 2) * 128 + 128
            grown[pl.ds(at, 64), lane : lane + 128] = rows[pl.ds(i, 64, stride=4), :].astype(BF)
    for k, ref in enumerate((e0_ref, e1_ref, e2_ref, e3_ref)):
        rows[...] = ref[...].astype(F32)
        at = pl.multiple_of((chan ^ k) * 64, 64)
        for side in range(2):
            for f in range(2):
                lane = f * 512 + side * 384
                grown[pl.ds(at, 64), lane : lane + 128] = rows[
                    pl.ds(side * 128 + f, 64, stride=2), :
                ].astype(BF)

    def put(early_ref, late_ref):
        c1 = grown[:, 640:896]
        early = dot(xc_ref[:, :256], c1, 1, 1) * scale
        late = (dot(xc_ref[:, :256], grown[:, 128:384], 1, 1) + dot(xc_ref[:, 256:], c1, 1, 1)) * scale
        for ref, g in ((early_ref, early), (late_ref, late)):
            ref[:1152, :] = g[:, :128].astype(BF)
            ref[1152:, :] = g[:, 128:].astype(BF)

    @pl.when(core == 0)
    def _():
        put(keep_ref, send_ref)

    @pl.when(core == 1)
    def _():
        put(send_ref, keep_ref)


def backward_kernel(grown, pre_ref, win_ref, w2_ref, sel_ref, g1_ref, back_s, *, scale):
    z0 = z1 = 0.0
    for b in range(3):
        lo = (2 - b) * 128
        c0, c1 = grown[:, lo : lo + 256], grown[:, 512 + lo : 768 + lo]
        wa = w2_ref[1152 + b * 384 : 1536 + b * 384, :]
        wb = w2_ref[2304 + b * 384 : 2688 + b * 384, :]
        z0 = z0 + dot(wb, c0) + dot(wa, c1)
        z1 = z1 + dot(wb, c1)
    for f, z in enumerate((z0, z1)):
        z = z[128:256] + shifted(z[:128], 1) + shifted(z[256:], -1)
        back_s[0], back_s[1] = z[:, :128], z[:, 128:]
        a0, a1, a2, a3 = (
            jnp.concatenate([back_s[r, pl.ds(k, 32, stride=4), :] for r in range(2)], 1)
            for k in range(4)
        )
        s01, d01, s23, d23 = a0 + a1, a0 - a1, a2 + a3, a2 - a3
        act = jnp.concatenate([s01 + s23, d01 + d23, s01 - s23, d01 - d23], 0) * 0.5
        pre = pre_ref[:, f * 256 : f * 256 + 256]
        gate = jax.nn.sigmoid(pre)
        back = (act * gate * (1.0 + pre * (1.0 - gate))).astype(BF)
        if f == 0:
            late = dot(back, win_ref[:, :256], 1, 1)
        else:
            early = dot(back, win_ref[:, :256], 1, 1)
            late = late + dot(back, win_ref[:, 256:], 1, 1)
    for a, g in enumerate((early, late)):
        g = g * scale
        hi = g.astype(BF)
        lo = (g - hi.astype(F32)).astype(BF)
        total = 0.0
        for p in range(4):
            rows = slice(32 * p, 32 * p + 32)
            total = total + dot(hi[rows], sel_ref[p], 1, 1)
            total = total + dot(lo[rows], sel_ref[p], 1, 1)
        g1_ref[32 * a : 32 * a + 32, :] = total.astype(BF)


def join_kernel(keep_ref, got_ref, g1_ref, sum_ref):
    sum_ref[:2304, :] = (keep_ref[...].astype(F32) + got_ref[...].astype(F32)).astype(BF)
    sum_ref[2304:, :] = g1_ref[...]


def share_kernel(got_ref, lkeep_ref, lgot_ref, out_ref, own_ref, send_ref, wide, *, count):
    own_ref[...] = lkeep_ref[0].astype(F32) + lgot_ref[0].astype(F32)
    send_ref[...] = (lkeep_ref[1].astype(F32) + lgot_ref[1].astype(F32)).astype(BF)
    size = got_ref.shape[0] // count
    wide[...] = got_ref[...].astype(F32)
    total = wide[:size, :]
    for i in range(1, count):
        total = total + wide[i * size : i * size + size, :]
    for i in range(count):
        wide[i * size : i * size + size, :] = total
    out_ref[...] = wide[...].astype(BF)


def widen(from_ref, wide, to_ref, sems, first):
    copies = []
    for i in range(3):
        at = i * 384
        wide[at : at + 384, :128] = from_ref[at : at + 384, :].astype(F32)
        wide[at : at + 384, 128:] = from_ref[1152 + at : 1536 + at, :].astype(F32)
        rows = pl.ds(at, 384)
        copies.append(pltpu.make_async_copy(wide.at[rows], to_ref.at[rows], sems.at[first + i]))
        copies[-1].start()
    return copies


def first_half_kernel(mine_ref, g2_ref, zero, own, sems):
    core = lax.axis_index("band") % 2
    zero[...] = jnp.zeros((1152, 256), F32)
    clear = pltpu.make_async_copy(zero, g2_ref.at[0], sems.at[0])
    clear.start()
    copies = [clear] + widen(mine_ref, own, g2_ref.at[1 + core], sems, 1)
    for copy in copies:
        copy.wait()


def other_half_kernel(
    _, mine_ref, other_ref, lown_ref, lgot_ref, g2_ref, g1_ref, lat_ref, half, rows, sems
):
    core = lax.axis_index("band") % 2
    copies = widen(other_ref, half, g2_ref.at[2 - core], sems, 0)
    lat = lown_ref[...] + lgot_ref[...].astype(F32)
    for i in range(4):
        rows[pl.ds(i, 64, stride=4), :] = lat[:, i * 128 : i * 128 + 128]
    lat_ref[...] = rows[...].astype(BF)
    both = mine_ref[2304:2368, :].astype(F32) + other_ref[2304:2368, :].astype(F32)
    g1_ref[...] = jnp.zeros((12, 27, 32), F32)
    for a in range(2):
        taps = jnp.transpose(both[32 * a : 32 * a + 32, :])
        for c in range(12):
            g1_ref[c, 9 * a + 9 : 9 * a + 18, :] = taps[9 * c : 9 * c + 9, :]
    for copy in copies:
        copy.wait()


VMEM, HBM = pltpu.VMEM, pltpu.HBM


def call(kernel, outs, scratch, flops, *args, far=(), far_out=(), aliases=None):
    return pl.pallas_call(
        kernel,
        out_shape=[jax.ShapeDtypeStruct(*o) for o in outs],
        in_specs=[pl.BlockSpec(memory_space=HBM if i in far else VMEM) for i in range(len(args))],
        out_specs=[pl.BlockSpec(memory_space=HBM if i in far_out else VMEM) for i in range(len(outs))],
        scratch_shapes=[s if not isinstance(s, tuple) else pltpu.VMEM(*s) for s in scratch],
        input_output_aliases=aliases or {},
        compiler_params=pltpu.CompilerParams(vmem_limit_bytes=20 * 1024 * 1024),
        cost_estimate=pl.CostEstimate(flops=flops, bytes_accessed=1 << 20, transcendentals=0),
    )(*args)


def on_device(video, weight_one, weight_two, cotangent):
    n = lax.axis_size("band")
    up = [(i, i + 1) for i in range(n - 1)]
    down = [(j, i) for i, j in up]
    flip = [(i, i ^ 1) for i in range(n)]
    frames, half_rows, half_cols = video.shape[1], n * 4, video.shape[3] // 2
    scale_one = 1.0 / math.sqrt(frames * half_rows * half_cols)
    scale_two = 1.0 / math.sqrt(frames * (half_rows // 2) * (half_cols // 2))

    flat, own = video.reshape(48, 512), cotangent.reshape(256, 128)

    def swap(x, k):
        return lax.ppermute(x, "chan", [(i, i ^ k) for i in range(4)])

    others = [swap(own, k) for k in (1, 2, 3)]
    to_next, to_prev = call(
        edges_kernel, [((80, 512), BF)] * 2, [((256, 128), F32)], 1 << 20, flat, own
    )
    before, after = lax.ppermute(to_next, "band", up), lax.ppermute(to_prev, "band", down)
    (outer,) = call(outer_kernel, [((256, 128), BF)], [], 1 << 20, before, after)
    outers = [swap(outer, k) for k in (1, 2, 3)]
    cols, rows, sel = call(
        matrix_kernel,
        [((512, 512), BF), ((3, 256, 128), BF), ((4, 128, 256), BF)],
        [],
        1 << 20,
    )
    w1 = weight_one[9:].reshape(2, 9, 12, 32).transpose(0, 2, 1, 3).reshape(2, 108, 32)
    w1 = jnp.pad(w1, ((0, 0), (0, 20), (0, 0)))
    w2 = weight_two.reshape(3456, 256)
    xc, pre, win = call(
        forward_kernel,
        [((1152, 512), BF), ((128, 512), F32), ((256, 512), BF)],
        [((2, 256, 512), BF), ((4, 128, 128), F32)],
        1 << 30,
        before, flat, after, cols, rows, sel, w1,
    )
    lat_keep, lat_send = call(
        latent_kernel, [((2, 64, 512), BF)] * 2, [((256, 512), BF)], 1 << 30, xc, w2
    )
    lat_got = swap(lat_send, 1)

    def second_grad(*refs):
        second_grad_kernel(*refs, scale=scale_two)

    cot, keep, send = call(
        second_grad,
        [((256, 1024), BF), ((2304, 128), BF), ((2304, 128), BF)],
        [((256, 128), F32)],
        1 << 30,
        xc, own, *others, outer, *outers, lat_keep,
        far=(9,),
    )
    got = lax.ppermute(send, "band", flip)

    def backward(*refs):
        backward_kernel(*refs, scale=scale_one)

    (g1,) = call(
        backward,
        [((64, 128), BF)],
        [((2, 128, 128), F32)],
        1 << 30,
        cot, pre, win, w2, sel,
    )
    (part,) = call(join_kernel, [((2368, 128), BF)], [], 1 << 20, keep, got, g1)
    half = n // 2
    groups = [[2 * i + c for i in range(half)] for c in range(2)]

    def exchange(x):
        x = x.reshape(half, 1184 // half, 2, 128)
        x = lax.all_to_all(x, "band", 0, 0, tiled=True, axis_index_groups=groups)
        return x.reshape(2368, 128)

    def share(*refs):
        share_kernel(*refs, count=half)

    part = exchange(part)
    mine, lat_own, lat_send = call(
        share,
        [((2368, 128), BF), ((64, 512), F32), ((64, 512), BF)],
        [((2368, 128), F32)],
        1 << 20,
        part, lat_keep, lat_got,
    )
    lat_got = swap(lat_send, 2)
    mine = exchange(mine)
    other = lax.ppermute(mine, "band", flip)
    (g2,) = call(
        first_half_kernel,
        [((3, 1152, 256), F32)],
        [((1152, 256), F32), ((1152, 256), F32), pltpu.SemaphoreType.DMA((4,))],
        1 << 20,
        mine,
        far_out=(0,),
    )
    g2, g1, latent = call(
        other_half_kernel,
        [((3, 1152, 256), F32), ((12, 27, 32), F32), ((256, 128), BF)],
        [((1152, 256), F32), ((256, 128), F32), pltpu.SemaphoreType.DMA((3,))],
        1 << 20,
        g2, mine, other, lat_own, lat_got,
        far=(0,), far_out=(0,), aliases={0: 0},
    )
    return latent.reshape(64, 2, 2, 128), jnp.transpose(g1, (1, 0, 2)), g2.reshape(27, 128, 256)


def solution(mesh):
    return jax.shard_map(
        on_device,
        mesh=mesh,
        in_specs=(
            P(None, None, "band", None),
            P(None, None, "chan"),
            P(None, "chan", None),
            P("chan", None, "band", None),
        ),
        out_specs=(P("chan", None, "band", None), P(None, None, "chan"), P(None, "chan", None)),
        check_vma=False,
    )
```

```python
import math

import jax
import jax.numpy as jnp
from jax import lax
from jax.experimental import pallas as pl
from jax.experimental.pallas import tpu as pltpu
from jax.sharding import PartitionSpec as P

BF = jnp.bfloat16
F32 = jnp.float32


def iota(shape, axis):
    return lax.broadcasted_iota(jnp.int32, shape, axis)


def matrix_kernel(col_ref, row_ref, sel_ref):
    u, w = iota((512, 128), 0), iota((512, 128), 1)
    for s in range(2):
        hit = ((u >> 2) == w) & (((u >> 1) & 1) == s)
        for t in range(2):
            value = 0.5 if t == 0 else jnp.where((u & 1) == 1, -0.5, 0.5)
            at = (s * 2 + t) * 128
            col_ref[:, at : at + 128] = jnp.where(hit, value, 0.0).astype(BF)
    at, lane = iota((256, 128), 0), iota((256, 128), 1)
    m, r, f, tb = at & 15, (at >> 4) & 3, (at >> 6) & 1, at >> 7
    wi = (m * 11) >> 5
    y = 4 * r + 2 * wi + tb + 2
    for part in range(3):
        hit = (lane == (m - 3 * wi) * 16 + f * 8 + y - 8 * part) & (m < 12)
        hit = hit & (y >= 8 * part) & (y < 8 * part + 8)
        row_ref[part] = jnp.where(hit, 1.0, 0.0).astype(BF)
    at, lane = iota((128, 256), 0), iota((128, 256), 1)
    c = (at * 57) >> 9
    tap = at - 9 * c
    b = (tap * 11) >> 5
    e = tap - 3 * b
    target = ((c >> 1) & 1) * 128 + (e * 2 + (c & 1)) * 16 + b * 3 + (c >> 2)
    for p in range(4):
        hit = (lane == target + (p & 1) * 32 + (p >> 1) * 3) & (at < 108)
        sel_ref[p] = jnp.where(hit, 1.0, 0.0).astype(BF)


def dot(a, b, ca=1, cb=0):
    return lax.dot_general(a, b, (((ca,), (cb,)), ((), ())), preferred_element_type=F32)


def edges_kernel(video_ref, own_ref, up_ref, down_ref, rows):
    rows[...] = own_ref[...].astype(F32)
    for ref, r in ((up_ref, 1), (down_ref, 0)):
        ref[:48, :] = video_ref[...]
        edge = rows[pl.ds(r, 128, stride=2), :].astype(BF)
        for i in range(4):
            ref[48:, i * 128 : i * 128 + 128] = edge[i * 32 : i * 32 + 32, :]


def grown_kernel(own_ref, above_ref, below_ref, out_ref):
    out_ref[:256, :] = own_ref[...]
    for side, ref in enumerate((above_ref, below_ref)):
        for i in range(4):
            at = 256 + side * 128 + i * 32
            out_ref[at : at + 32, :] = ref[48:, i * 128 : i * 128 + 128]


def shifted(x, step):
    lanes = x.shape[1]
    lane = lax.broadcasted_iota(jnp.int32, x.shape, 1) % 128
    if step == -1:
        return jnp.where(lane == 0, 0.0, pltpu.roll(x, 1, 1))
    return jnp.where(lane == 127, 0.0, pltpu.roll(x, lanes - 1, 1))


def forward_kernel(
    prev_ref, own_ref, next_ref, col_ref, row_ref, sel_ref, w1_ref,
    xc_ref, pre_ref, win_ref, one, two,
):
    band = lax.axis_index("band")
    last = lax.axis_size("band") - 1
    v = (
        dot(row_ref[0, :, :48], prev_ref[:48, :])
        + dot(row_ref[1, :, :48], own_ref[...])
        + dot(row_ref[2, :, :48], next_ref[:48, :])
    ).astype(BF)
    h = dot(v, col_ref[...])
    top, low = h[:128], h[128:]
    for pm, half in enumerate((top + low, top - low)):
        even, odd = half[:, :256], half[:, 256:]
        streams = (shifted(odd, -1), even, odd, shifted(even, 1))
        for st in range(8):
            part = streams[st // 2][:, (st % 2) * 128 : (st % 2) * 128 + 128].astype(BF)
            for f in range(2):
                for r in range(4):
                    at = (f * 4 + r) * 16
                    one[f, pm * 128 + st * 16 : pm * 128 + st * 16 + 16, r * 128 : r * 128 + 128] = part[
                        at : at + 16, :
                    ]
    w1a, w1b = (
        jnp.concatenate([dot(w1_ref[a], sel_ref[p], 0, 0) for p in range(4)], 0).astype(BF)
        for a in range(2)
    )
    pres = (dot(w1b, one[0]), dot(w1a, one[0]) + dot(w1b, one[1]))
    lane = lax.broadcasted_iota(jnp.int32, (32, 512), 1)
    keep = ((lane >= 128) | (band > 0)) & ((lane < 384) | (band < last))
    for f in range(2):
        pre = pres[f]
        pre_ref[:, f * 256 : f * 256 + 256] = pre[:, 128:384]
        win_ref[:, f * 256 : f * 256 + 256] = one[f, :, 128:384]
        act = pre * jax.nn.sigmoid(pre)
        p, q, r, s = act[:32], act[32:64], act[64:96], act[96:]
        pq, pmq, rs, rms = p + q, p - q, r + s, r - s
        parts = (pq + rs, pmq + rms, pq - rs, pmq - rms)
        for k in range(4):
            part = jnp.where(keep, parts[k] * 0.5, 0.0)
            for r in range(4):
                two[r, pl.ds(k, 32, stride=4), :] = part[:, r * 128 : r * 128 + 128]
        x = jnp.concatenate([two[r] for r in range(4)], 1)
        for e, xe in enumerate((shifted(x, -1), x, shifted(x, 1))):
            xe = xe.astype(BF)
            for b in range(3):
                at = (b * 3 + e) * 128
                xc_ref[at : at + 128, f * 256 : f * 256 + 256] = xe[:, b * 128 : b * 128 + 256]


def latent_kernel(xc_ref, w2_ref, lat_ref):
    out = dot(w2_ref[2304:, :], xc_ref[...], 0, 0)
    more = dot(w2_ref[1152:2304, :], xc_ref[:, :256], 0, 0)
    lat_ref[:, :256] = out[:, :256].astype(BF)
    lat_ref[:, 256:] = (out[:, 256:] + more).astype(BF)


def second_grad_kernel(
    xc_ref, c0_ref, c1_ref, c2_ref, c3_ref, _, grown, keep_ref, send_ref, rows, *, scale
):
    chan = lax.axis_index("chan")
    core = lax.axis_index("band") % 2
    for k, ref in enumerate((c0_ref, c1_ref, c2_ref, c3_ref)):
        rows[...] = ref[...].astype(F32)
        at = pl.multiple_of((chan ^ k) * 64, 64)
        for f in range(2):
            for r in range(2):
                lane = f * 512 + r * 128 + 128
                part = rows[pl.ds(f * 2 + r, 64, stride=4), :]
                grown[pl.ds(at, 64), lane : lane + 128] = part.astype(BF)
            for side in range(2):
                lane = f * 512 + side * 384
                part = rows[pl.ds(256 + side * 128 + f, 64, stride=2), :]
                grown[pl.ds(at, 64), lane : lane + 128] = part.astype(BF)

    def put(early_ref, late_ref):
        c1 = grown[:, 640:896]
        early = dot(xc_ref[:, :256], c1, 1, 1) * scale
        late = (dot(xc_ref[:, :256], grown[:, 128:384], 1, 1) + dot(xc_ref[:, 256:], c1, 1, 1)) * scale
        for ref, g in ((early_ref, early), (late_ref, late)):
            ref[:1152, :] = g[:, :128].astype(BF)
            ref[1152:, :] = g[:, 128:].astype(BF)

    @pl.when(core == 0)
    def _():
        put(keep_ref, send_ref)

    @pl.when(core == 1)
    def _():
        put(send_ref, keep_ref)


def backward_kernel(grown, pre_ref, win_ref, w2_ref, sel_ref, g1_ref, back_s, *, scale):
    z0 = z1 = 0.0
    for b in range(3):
        lo = (2 - b) * 128
        c0, c1 = grown[:, lo : lo + 256], grown[:, 512 + lo : 768 + lo]
        wa = w2_ref[1152 + b * 384 : 1536 + b * 384, :]
        wb = w2_ref[2304 + b * 384 : 2688 + b * 384, :]
        z0 = z0 + dot(wb, c0) + dot(wa, c1)
        z1 = z1 + dot(wb, c1)
    for f, z in enumerate((z0, z1)):
        z = z[128:256] + shifted(z[:128], 1) + shifted(z[256:], -1)
        back_s[0], back_s[1] = z[:, :128], z[:, 128:]
        a0, a1, a2, a3 = (
            jnp.concatenate([back_s[r, pl.ds(k, 32, stride=4), :] for r in range(2)], 1)
            for k in range(4)
        )
        s01, d01, s23, d23 = a0 + a1, a0 - a1, a2 + a3, a2 - a3
        act = jnp.concatenate([s01 + s23, d01 + d23, s01 - s23, d01 - d23], 0) * 0.5
        pre = pre_ref[:, f * 256 : f * 256 + 256]
        gate = jax.nn.sigmoid(pre)
        back = (act * gate * (1.0 + pre * (1.0 - gate))).astype(BF)
        if f == 0:
            late = dot(back, win_ref[:, :256], 1, 1)
        else:
            early = dot(back, win_ref[:, :256], 1, 1)
            late = late + dot(back, win_ref[:, 256:], 1, 1)
    for a, g in enumerate((early, late)):
        g = g * scale
        hi = g.astype(BF)
        lo = (g - hi.astype(F32)).astype(BF)
        total = 0.0
        for p in range(4):
            rows = slice(32 * p, 32 * p + 32)
            total = total + dot(hi[rows], sel_ref[p], 1, 1)
            total = total + dot(lo[rows], sel_ref[p], 1, 1)
        g1_ref[32 * a : 32 * a + 32, :] = total.astype(BF)


def join_kernel(keep_ref, got_ref, g1_ref, sum_ref):
    sum_ref[:2304, :] = (keep_ref[...].astype(F32) + got_ref[...].astype(F32)).astype(BF)
    sum_ref[2304:, :] = g1_ref[...]


def share_kernel(got_ref, out_ref, wide, *, count):
    size = got_ref.shape[0] // count
    wide[...] = got_ref[...].astype(F32)
    total = wide[:size, :]
    for i in range(1, count):
        total = total + wide[i * size : i * size + size, :]
    for i in range(count):
        wide[i * size : i * size + size, :] = total
    out_ref[...] = wide[...].astype(BF)


def widen(from_ref, wide, to_ref, sems, first):
    copies = []
    for i in range(3):
        at = i * 384
        wide[at : at + 384, :128] = from_ref[at : at + 384, :].astype(F32)
        wide[at : at + 384, 128:] = from_ref[1152 + at : 1536 + at, :].astype(F32)
        rows = pl.ds(at, 384)
        copies.append(pltpu.make_async_copy(wide.at[rows], to_ref.at[rows], sems.at[first + i]))
        copies[-1].start()
    return copies


def first_half_kernel(mine_ref, g2_ref, zero, own, sems):
    core = lax.axis_index("band") % 2
    zero[...] = jnp.zeros((1152, 256), F32)
    clear = pltpu.make_async_copy(zero, g2_ref.at[0], sems.at[0])
    clear.start()
    copies = [clear] + widen(mine_ref, own, g2_ref.at[1 + core], sems, 1)
    for copy in copies:
        copy.wait()


def latent_rows_kernel(_, lat_ref, mine_ref, out_ref, rows):
    for i in range(4):
        rows[pl.ds(i, 64, stride=4), :] = lat_ref[:, i * 128 : i * 128 + 128].astype(F32)
    out_ref[...] = rows[...].astype(BF)


def other_half_kernel(_, mine_ref, other_ref, g2_ref, g1_ref, half, sems):
    core = lax.axis_index("band") % 2
    copies = widen(other_ref, half, g2_ref.at[2 - core], sems, 0)
    both = mine_ref[2304:2368, :].astype(F32) + other_ref[2304:2368, :].astype(F32)
    g1_ref[...] = jnp.zeros((12, 27, 32), F32)
    for a in range(2):
        taps = jnp.transpose(both[32 * a : 32 * a + 32, :])
        for c in range(12):
            g1_ref[c, 9 * a + 9 : 9 * a + 18, :] = taps[9 * c : 9 * c + 9, :]
    for copy in copies:
        copy.wait()


VMEM, HBM = pltpu.VMEM, pltpu.HBM


def call(kernel, outs, scratch, flops, *args, far=(), far_out=(), aliases=None):
    return pl.pallas_call(
        kernel,
        out_shape=[jax.ShapeDtypeStruct(*o) for o in outs],
        in_specs=[pl.BlockSpec(memory_space=HBM if i in far else VMEM) for i in range(len(args))],
        out_specs=[pl.BlockSpec(memory_space=HBM if i in far_out else VMEM) for i in range(len(outs))],
        scratch_shapes=[s if not isinstance(s, tuple) else pltpu.VMEM(*s) for s in scratch],
        input_output_aliases=aliases or {},
        compiler_params=pltpu.CompilerParams(vmem_limit_bytes=20 * 1024 * 1024),
        cost_estimate=pl.CostEstimate(flops=flops, bytes_accessed=1 << 20, transcendentals=0),
    )(*args)


def on_device(video, weight_one, weight_two, cotangent):
    n = lax.axis_size("band")
    up = [(i, i + 1) for i in range(n - 1)]
    down = [(j, i) for i, j in up]
    flip = [(i, i ^ 1) for i in range(n)]
    frames, half_rows, half_cols = video.shape[1], n * 4, video.shape[3] // 2
    scale_one = 1.0 / math.sqrt(frames * half_rows * half_cols)
    scale_two = 1.0 / math.sqrt(frames * (half_rows // 2) * (half_cols // 2))

    flat, own = video.reshape(48, 512), cotangent.reshape(256, 128)

    def swap(x, k):
        return lax.ppermute(x, "chan", [(i, i ^ k) for i in range(4)])

    to_next, to_prev = call(
        edges_kernel, [((80, 512), BF)] * 2, [((256, 128), F32)], 1 << 20, flat, own
    )
    before, after = lax.ppermute(to_next, "band", up), lax.ppermute(to_prev, "band", down)
    (own,) = call(grown_kernel, [((512, 128), BF)], [], 1 << 20, own, before, after)
    others = [swap(own, k) for k in (1, 2, 3)]
    cols, rows, sel = call(
        matrix_kernel,
        [((512, 512), BF), ((3, 256, 128), BF), ((4, 128, 256), BF)],
        [],
        1 << 20,
    )
    w1 = weight_one[9:].reshape(2, 9, 12, 32).transpose(0, 2, 1, 3).reshape(2, 108, 32)
    w1 = jnp.pad(w1, ((0, 0), (0, 20), (0, 0)))
    w2 = weight_two.reshape(3456, 256)
    xc, pre, win = call(
        forward_kernel,
        [((1152, 512), BF), ((128, 512), F32), ((256, 512), BF)],
        [((2, 256, 512), BF), ((4, 128, 128), F32)],
        1 << 30,
        before, flat, after, cols, rows, sel, w1,
    )
    (lat,) = call(latent_kernel, [((256, 512), BF)], [], 1 << 30, xc, w2)
    latent = lax.psum_scatter(lat, "chan", scatter_dimension=0, tiled=True)

    def second_grad(*refs):
        second_grad_kernel(*refs, scale=scale_two)

    cot, keep, send = call(
        second_grad,
        [((256, 1024), BF), ((2304, 128), BF), ((2304, 128), BF)],
        [((512, 128), F32)],
        1 << 30,
        xc, own, *others, lat,
        far=(5,),
    )
    got = lax.ppermute(send, "band", flip)

    def backward(*refs):
        backward_kernel(*refs, scale=scale_one)

    (g1,) = call(
        backward,
        [((64, 128), BF)],
        [((2, 128, 128), F32)],
        1 << 30,
        cot, pre, win, w2, sel,
    )
    (part,) = call(join_kernel, [((2368, 128), BF)], [], 1 << 20, keep, got, g1)
    half = n // 2
    groups = [[2 * i + c for i in range(half)] for c in range(2)]

    def exchange(x):
        x = x.reshape(half, 1184 // half, 2, 128)
        x = lax.all_to_all(x, "band", 0, 0, tiled=True, axis_index_groups=groups)
        return x.reshape(2368, 128)

    def share(*refs):
        share_kernel(*refs, count=half)

    part = exchange(part)
    (mine,) = call(share, [((2368, 128), BF)], [((2368, 128), F32)], 1 << 20, part)
    mine = exchange(mine)
    mine, latent = call(
        latent_rows_kernel,
        [((2368, 128), BF), ((256, 128), BF)],
        [((256, 128), F32)],
        1 << 20,
        mine, latent,
        far=(0,), far_out=(0,), aliases={0: 0},
    )
    other = lax.ppermute(mine, "band", flip)
    (g2,) = call(
        first_half_kernel,
        [((3, 1152, 256), F32)],
        [((1152, 256), F32), ((1152, 256), F32), pltpu.SemaphoreType.DMA((4,))],
        1 << 20,
        mine,
        far_out=(0,),
    )
    g2, g1 = call(
        other_half_kernel,
        [((3, 1152, 256), F32), ((12, 27, 32), F32)],
        [((1152, 256), F32), pltpu.SemaphoreType.DMA((3,))],
        1 << 20,
        g2, mine, other,
        far=(0,), far_out=(0,), aliases={0: 0},
    )
    return latent.reshape(64, 2, 2, 128), jnp.transpose(g1, (1, 0, 2)), g2.reshape(27, 128, 256)


def solution(mesh):
    return jax.shard_map(
        on_device,
        mesh=mesh,
        in_specs=(
            P(None, None, "band", None),
            P(None, None, "chan"),
            P(None, "chan", None),
            P("chan", None, "band", None),
        ),
        out_specs=(P("chan", None, "band", None), P(None, None, "chan"), P(None, "chan", None)),
        check_vma=False,
    )
```

```python
import math

import jax
import jax.numpy as jnp
from jax import lax
from jax.experimental import pallas as pl
from jax.experimental.pallas import tpu as pltpu
from jax.sharding import PartitionSpec as P

BF = jnp.bfloat16
F32 = jnp.float32


def iota(shape, axis):
    return lax.broadcasted_iota(jnp.int32, shape, axis)


def matrix_kernel(col_ref, row_ref, sel_ref):
    u, w = iota((512, 128), 0), iota((512, 128), 1)
    for s in range(2):
        hit = ((u >> 2) == w) & (((u >> 1) & 1) == s)
        for t in range(2):
            value = 0.5 if t == 0 else jnp.where((u & 1) == 1, -0.5, 0.5)
            at = (s * 2 + t) * 128
            col_ref[:, at : at + 128] = jnp.where(hit, value, 0.0).astype(BF)
    at, lane = iota((256, 128), 0), iota((256, 128), 1)
    m, r, f, tb = at & 15, (at >> 4) & 3, (at >> 6) & 1, at >> 7
    wi = (m * 11) >> 5
    y = 4 * r + 2 * wi + tb + 2
    for part in range(3):
        hit = (lane == (m - 3 * wi) * 16 + f * 8 + y - 8 * part) & (m < 12)
        hit = hit & (y >= 8 * part) & (y < 8 * part + 8)
        row_ref[part] = jnp.where(hit, 1.0, 0.0).astype(BF)
    at, lane = iota((128, 256), 0), iota((128, 256), 1)
    c = (at * 57) >> 9
    tap = at - 9 * c
    b = (tap * 11) >> 5
    e = tap - 3 * b
    target = ((c >> 1) & 1) * 128 + (e * 2 + (c & 1)) * 16 + b * 3 + (c >> 2)
    for p in range(4):
        hit = (lane == target + (p & 1) * 32 + (p >> 1) * 3) & (at < 108)
        sel_ref[p] = jnp.where(hit, 1.0, 0.0).astype(BF)


def dot(a, b, ca=1, cb=0):
    return lax.dot_general(a, b, (((ca,), (cb,)), ((), ())), preferred_element_type=F32)


def edges_kernel(video_ref, own_ref, up_ref, down_ref, rows):
    rows[...] = own_ref[...].astype(F32)
    for ref, r in ((up_ref, 1), (down_ref, 0)):
        ref[:48, :] = video_ref[...]
        edge = rows[pl.ds(r, 128, stride=2), :].astype(BF)
        for i in range(4):
            ref[48:, i * 128 : i * 128 + 128] = edge[i * 32 : i * 32 + 32, :]


def grown_kernel(own_ref, above_ref, below_ref, _, __, out_ref):
    out_ref[:256, :] = own_ref[...]
    for side, ref in enumerate((above_ref, below_ref)):
        for i in range(4):
            at = 256 + side * 128 + i * 32
            out_ref[at : at + 32, :] = ref[48:, i * 128 : i * 128 + 128]


def shifted(x, step):
    lanes = x.shape[1]
    lane = lax.broadcasted_iota(jnp.int32, x.shape, 1) % 128
    if step == -1:
        return jnp.where(lane == 0, 0.0, pltpu.roll(x, 1, 1))
    return jnp.where(lane == 127, 0.0, pltpu.roll(x, lanes - 1, 1))


def forward_kernel(
    prev_ref, own_ref, next_ref, col_ref, row_ref, sel_ref, w1_ref,
    xc_ref, pre_ref, win_ref, one, two,
):
    band = lax.axis_index("band")
    last = lax.axis_size("band") - 1
    v = (
        dot(row_ref[0, :, :48], prev_ref[:48, :])
        + dot(row_ref[1, :, :48], own_ref[...])
        + dot(row_ref[2, :, :48], next_ref[:48, :])
    ).astype(BF)
    h = dot(v, col_ref[...])
    top, low = h[:128], h[128:]
    for pm, half in enumerate((top + low, top - low)):
        even, odd = half[:, :256], half[:, 256:]
        streams = (shifted(odd, -1), even, odd, shifted(even, 1))
        for st in range(8):
            part = streams[st // 2][:, (st % 2) * 128 : (st % 2) * 128 + 128].astype(BF)
            for f in range(2):
                for r in range(4):
                    at = (f * 4 + r) * 16
                    one[f, pm * 128 + st * 16 : pm * 128 + st * 16 + 16, r * 128 : r * 128 + 128] = part[
                        at : at + 16, :
                    ]
    w1a, w1b = (
        jnp.concatenate([dot(w1_ref[a], sel_ref[p], 0, 0) for p in range(4)], 0).astype(BF)
        for a in range(2)
    )
    pres = (dot(w1b, one[0]), dot(w1a, one[0]) + dot(w1b, one[1]))
    lane = lax.broadcasted_iota(jnp.int32, (32, 512), 1)
    keep = ((lane >= 128) | (band > 0)) & ((lane < 384) | (band < last))
    for f in range(2):
        pre = pres[f]
        pre_ref[:, f * 256 : f * 256 + 256] = pre[:, 128:384]
        win_ref[:, f * 256 : f * 256 + 256] = one[f, :, 128:384]
        act = pre * jax.nn.sigmoid(pre)
        p, q, r, s = act[:32], act[32:64], act[64:96], act[96:]
        pq, pmq, rs, rms = p + q, p - q, r + s, r - s
        parts = (pq + rs, pmq + rms, pq - rs, pmq - rms)
        for k in range(4):
            part = jnp.where(keep, parts[k] * 0.5, 0.0)
            for r in range(4):
                two[r, pl.ds(k, 32, stride=4), :] = part[:, r * 128 : r * 128 + 128]
        x = jnp.concatenate([two[r] for r in range(4)], 1)
        for e, xe in enumerate((shifted(x, -1), x, shifted(x, 1))):
            xe = xe.astype(BF)
            for b in range(3):
                at = (b * 3 + e) * 128
                xc_ref[at : at + 128, f * 256 : f * 256 + 256] = xe[:, b * 128 : b * 128 + 256]


def hold_kernel(_, __, ___):
    pass


def latent_kernel(xc_ref, w2_ref, keep_ref, send_ref, lat):
    out = dot(w2_ref[2304:, :], xc_ref[...], 0, 0)
    more = dot(w2_ref[1152:2304, :], xc_ref[:, :256], 0, 0)
    lat[:, :256] = out[:, :256].astype(BF)
    lat[:, 256:] = (out[:, 256:] + more).astype(BF)
    chan = lax.axis_index("chan")
    for ref, i, k in ((keep_ref, 0, 0), (send_ref, 0, 1), (send_ref, 1, 2), (keep_ref, 1, 3)):
        ref[i] = lat[pl.ds(pl.multiple_of((chan ^ k) * 64, 64), 64), :]


def second_grad_kernel(
    xc_ref, c0_ref, c1_ref, c2_ref, c3_ref, _, grown, keep_ref, send_ref, rows, *, scale
):
    chan = lax.axis_index("chan")
    core = lax.axis_index("band") % 2
    for k, ref in enumerate((c0_ref, c1_ref, c2_ref, c3_ref)):
        rows[...] = ref[...].astype(F32)
        at = pl.multiple_of((chan ^ k) * 64, 64)
        for f in range(2):
            for r in range(2):
                lane = f * 512 + r * 128 + 128
                part = rows[pl.ds(f * 2 + r, 64, stride=4), :]
                grown[pl.ds(at, 64), lane : lane + 128] = part.astype(BF)
            for side in range(2):
                lane = f * 512 + side * 384
                part = rows[pl.ds(256 + side * 128 + f, 64, stride=2), :]
                grown[pl.ds(at, 64), lane : lane + 128] = part.astype(BF)

    def put(early_ref, late_ref):
        c1 = grown[:, 640:896]
        early = dot(xc_ref[:, :256], c1, 1, 1) * scale
        late = (dot(xc_ref[:, :256], grown[:, 128:384], 1, 1) + dot(xc_ref[:, 256:], c1, 1, 1)) * scale
        for ref, g in ((early_ref, early), (late_ref, late)):
            ref[:1152, :] = g[:, :128].astype(BF)
            ref[1152:, :] = g[:, 128:].astype(BF)

    @pl.when(core == 0)
    def _():
        put(keep_ref, send_ref)

    @pl.when(core == 1)
    def _():
        put(send_ref, keep_ref)


def backward_kernel(grown, pre_ref, win_ref, w2_ref, sel_ref, g1_ref, back_s, *, scale):
    z0 = z1 = 0.0
    for b in range(3):
        lo = (2 - b) * 128
        c0, c1 = grown[:, lo : lo + 256], grown[:, 512 + lo : 768 + lo]
        wa = w2_ref[1152 + b * 384 : 1536 + b * 384, :]
        wb = w2_ref[2304 + b * 384 : 2688 + b * 384, :]
        z0 = z0 + dot(wb, c0) + dot(wa, c1)
        z1 = z1 + dot(wb, c1)
    for f, z in enumerate((z0, z1)):
        z = z[128:256] + shifted(z[:128], 1) + shifted(z[256:], -1)
        back_s[0], back_s[1] = z[:, :128], z[:, 128:]
        a0, a1, a2, a3 = (
            jnp.concatenate([back_s[r, pl.ds(k, 32, stride=4), :] for r in range(2)], 1)
            for k in range(4)
        )
        s01, d01, s23, d23 = a0 + a1, a0 - a1, a2 + a3, a2 - a3
        act = jnp.concatenate([s01 + s23, d01 + d23, s01 - s23, d01 - d23], 0) * 0.5
        pre = pre_ref[:, f * 256 : f * 256 + 256]
        gate = jax.nn.sigmoid(pre)
        back = (act * gate * (1.0 + pre * (1.0 - gate))).astype(BF)
        if f == 0:
            late = dot(back, win_ref[:, :256], 1, 1)
        else:
            early = dot(back, win_ref[:, :256], 1, 1)
            late = late + dot(back, win_ref[:, 256:], 1, 1)
    for a, g in enumerate((early, late)):
        g = g * scale
        hi = g.astype(BF)
        lo = (g - hi.astype(F32)).astype(BF)
        total = 0.0
        for p in range(4):
            rows = slice(32 * p, 32 * p + 32)
            total = total + dot(hi[rows], sel_ref[p], 1, 1)
            total = total + dot(lo[rows], sel_ref[p], 1, 1)
        g1_ref[32 * a : 32 * a + 32, :] = total.astype(BF)


def join_kernel(keep_ref, got_ref, g1_ref, sum_ref):
    sum_ref[:2304, :] = (keep_ref[...].astype(F32) + got_ref[...].astype(F32)).astype(BF)
    sum_ref[2304:, :] = g1_ref[...]


def share_kernel(got_ref, lkeep_ref, lgot_ref, out_ref, lown_ref, lsend_ref, wide, *, count):
    lown_ref[...] = lkeep_ref[0].astype(F32) + lgot_ref[0].astype(F32)
    lsend_ref[...] = (lkeep_ref[1].astype(F32) + lgot_ref[1].astype(F32)).astype(BF)
    size = got_ref.shape[0] // count
    bunch = 8 if count % 8 == 0 else count
    block = bunch * size
    total = got_ref[:block, :].astype(F32)
    for i in range(block, count * size, block):
        total = total + got_ref[i : i + block, :].astype(F32)
    wide[...] = total
    total = wide[:size, :]
    for i in range(1, bunch):
        total = total + wide[i * size : i * size + size, :]
    for i in range(bunch):
        wide[i * size : i * size + size, :] = total
    total = wide[...].astype(BF)
    for i in range(0, count * size, block):
        out_ref[i : i + block, :] = total


def widen(from_ref, wide, to_ref, sems, first):
    copies = []
    for i in range(3):
        at = i * 384
        wide[at : at + 384, :128] = from_ref[at : at + 384, :].astype(F32)
        wide[at : at + 384, 128:] = from_ref[1152 + at : 1536 + at, :].astype(F32)
        rows = pl.ds(at, 384)
        copies.append(pltpu.make_async_copy(wide.at[rows], to_ref.at[rows], sems.at[first + i]))
        copies[-1].start()
    return copies


def first_half_kernel(mine_ref, g2_ref, zero, own, sems):
    core = lax.axis_index("band") % 2
    zero[...] = jnp.zeros((1152, 256), F32)
    clear = pltpu.make_async_copy(zero, g2_ref.at[0], sems.at[0])
    clear.start()
    copies = [clear] + widen(mine_ref, own, g2_ref.at[1 + core], sems, 1)
    for copy in copies:
        copy.wait()


def latent_rows_kernel(_, lown_ref, lgot_ref, mine_ref, lat_ref, rows):
    lat = lown_ref[...] + lgot_ref[...].astype(F32)
    for i in range(4):
        rows[pl.ds(i, 64, stride=4), :] = lat[:, i * 128 : i * 128 + 128]
    lat_ref[...] = rows[...].astype(BF)


def other_half_kernel(_, mine_ref, other_ref, g2_ref, g1_ref, half, sems):
    core = lax.axis_index("band") % 2
    copies = widen(other_ref, half, g2_ref.at[2 - core], sems, 0)
    both = mine_ref[2304:2368, :].astype(F32) + other_ref[2304:2368, :].astype(F32)
    g1_ref[...] = jnp.zeros((12, 27, 32), F32)
    for a in range(2):
        taps = jnp.transpose(both[32 * a : 32 * a + 32, :])
        for c in range(12):
            g1_ref[c, 9 * a + 9 : 9 * a + 18, :] = taps[9 * c : 9 * c + 9, :]
    for copy in copies:
        copy.wait()


VMEM, HBM = pltpu.VMEM, pltpu.HBM


def call(kernel, outs, scratch, flops, *args, far=(), far_out=(), aliases=None):
    return pl.pallas_call(
        kernel,
        out_shape=[jax.ShapeDtypeStruct(*o) for o in outs],
        in_specs=[pl.BlockSpec(memory_space=HBM if i in far else VMEM) for i in range(len(args))],
        out_specs=[pl.BlockSpec(memory_space=HBM if i in far_out else VMEM) for i in range(len(outs))],
        scratch_shapes=[s if not isinstance(s, tuple) else pltpu.VMEM(*s) for s in scratch],
        input_output_aliases=aliases or {},
        compiler_params=pltpu.CompilerParams(vmem_limit_bytes=20 * 1024 * 1024),
        cost_estimate=pl.CostEstimate(flops=flops, bytes_accessed=1 << 20, transcendentals=0),
    )(*args)


def on_device(video, weight_one, weight_two, cotangent):
    n = lax.axis_size("band")
    up = [(i, i + 1) for i in range(n - 1)]
    down = [(j, i) for i, j in up]
    flip = [(i, i ^ 1) for i in range(n)]
    frames, half_rows, half_cols = video.shape[1], n * 4, video.shape[3] // 2
    scale_one = 1.0 / math.sqrt(frames * half_rows * half_cols)
    scale_two = 1.0 / math.sqrt(frames * (half_rows // 2) * (half_cols // 2))

    flat, own = video.reshape(48, 512), cotangent.reshape(256, 128)

    def swap(x, k):
        return lax.ppermute(x, "chan", [(i, i ^ k) for i in range(4)])

    to_next, to_prev = call(
        edges_kernel, [((80, 512), BF)] * 2, [((256, 128), F32)], 1 << 20, flat, own
    )
    before, after = lax.ppermute(to_next, "band", up), lax.ppermute(to_prev, "band", down)
    cols, rows, sel = call(
        matrix_kernel,
        [((512, 512), BF), ((3, 256, 128), BF), ((4, 128, 256), BF)],
        [],
        1 << 20,
    )
    w1 = weight_one[9:].reshape(2, 9, 12, 32).transpose(0, 2, 1, 3).reshape(2, 108, 32)
    w1 = jnp.pad(w1, ((0, 0), (0, 20), (0, 0)))
    (own,) = call(
        grown_kernel, [((512, 128), BF)], [], 1 << 20, own, before, after, sel, w1,
        far=(3, 4),
    )
    near, far = swap(own, 1), swap(own, 3)
    w2 = weight_two.reshape(3456, 256)
    xc, pre, win = call(
        forward_kernel,
        [((1152, 512), BF), ((128, 512), F32), ((256, 512), BF)],
        [((2, 256, 512), BF), ((4, 128, 128), F32)],
        1 << 30,
        before, flat, after, cols, rows, sel, w1,
    )
    (near,) = call(
        hold_kernel, [((512, 128), BF)], [], 1 << 10, near, xc, far=(0, 1), far_out=(0,), aliases={0: 0}
    )
    others = [near, swap(near, 3), far]
    lat_keep, lat_send = call(
        latent_kernel, [((2, 64, 512), BF)] * 2, [((256, 512), BF)], 1 << 30, xc, w2
    )
    lat_got = swap(lat_send, 1)

    def second_grad(*refs):
        second_grad_kernel(*refs, scale=scale_two)

    cot, keep, send = call(
        second_grad,
        [((256, 1024), BF), ((2304, 128), BF), ((2304, 128), BF)],
        [((512, 128), F32)],
        1 << 30,
        xc, own, *others, lat_keep,
        far=(5,),
    )
    got = lax.ppermute(send, "band", flip)

    def backward(*refs):
        backward_kernel(*refs, scale=scale_one)

    (g1,) = call(
        backward, [((64, 128), BF)], [((2, 128, 128), F32)], 1 << 30, cot, pre, win, w2, sel
    )
    (part,) = call(join_kernel, [((2368, 128), BF)], [], 1 << 20, keep, got, g1)
    half = n // 2
    groups = [[2 * i + c for i in range(half)] for c in range(2)]

    def exchange(x):
        x = x.reshape(half, 1184 // half, 2, 128)
        x = lax.all_to_all(x, "band", 0, 0, tiled=True, axis_index_groups=groups)
        return x.reshape(2368, 128)

    def share(*refs):
        share_kernel(*refs, count=half)

    part = exchange(part)
    mine, lat_own, lat_send = call(
        share,
        [((2368, 128), BF), ((64, 512), F32), ((64, 512), BF)],
        [((2368 // half * min(half, 8), 128), F32)],
        1 << 20,
        part, lat_keep, lat_got,
    )
    lat_got = swap(lat_send, 3)
    mine = exchange(mine)
    mine, latent = call(
        latent_rows_kernel,
        [((2368, 128), BF), ((256, 128), BF)],
        [((256, 128), F32)],
        1 << 20,
        mine, lat_own, lat_got,
        far=(0,), far_out=(0,), aliases={0: 0},
    )
    other = lax.ppermute(mine, "band", flip)
    (g2,) = call(
        first_half_kernel,
        [((3, 1152, 256), F32)],
        [((1152, 256), F32), ((1152, 256), F32), pltpu.SemaphoreType.DMA((4,))],
        1 << 20,
        mine,
        far_out=(0,),
    )
    g2, g1 = call(
        other_half_kernel,
        [((3, 1152, 256), F32), ((12, 27, 32), F32)],
        [((1152, 256), F32), pltpu.SemaphoreType.DMA((3,))],
        1 << 20,
        g2, mine, other,
        far=(0,), far_out=(0,), aliases={0: 0},
    )
    return latent.reshape(64, 2, 2, 128), jnp.transpose(g1, (1, 0, 2)), g2.reshape(27, 128, 256)


def solution(mesh):
    return jax.shard_map(
        on_device,
        mesh=mesh,
        in_specs=(
            P(None, None, "band", None),
            P(None, None, "chan"),
            P(None, "chan", None),
            P("chan", None, "band", None),
        ),
        out_specs=(P("chan", None, "band", None), P(None, None, "chan"), P(None, "chan", None)),
        check_vma=False,
    )
```

```python
import math

import jax
import jax.numpy as jnp
from jax import lax
from jax.experimental import pallas as pl
from jax.experimental.pallas import tpu as pltpu
from jax.sharding import PartitionSpec as P

BF = jnp.bfloat16
F32 = jnp.float32


def iota(shape, axis):
    return lax.broadcasted_iota(jnp.int32, shape, axis)


def matrix_kernel(col_ref, row_ref, sel_ref):
    u, w = iota((512, 128), 0), iota((512, 128), 1)
    for s in range(2):
        hit = ((u >> 2) == w) & (((u >> 1) & 1) == s)
        for t in range(2):
            value = 0.5 if t == 0 else jnp.where((u & 1) == 1, -0.5, 0.5)
            at = (s * 2 + t) * 128
            col_ref[:, at : at + 128] = jnp.where(hit, value, 0.0).astype(BF)
    at, lane = iota((256, 128), 0), iota((256, 128), 1)
    m, r, f, tb = at & 15, (at >> 4) & 3, (at >> 6) & 1, at >> 7
    wi = (m * 11) >> 5
    y = 4 * r + 2 * wi + tb + 2
    for part in range(3):
        hit = (lane == (m - 3 * wi) * 16 + f * 8 + y - 8 * part) & (m < 12)
        hit = hit & (y >= 8 * part) & (y < 8 * part + 8)
        row_ref[part] = jnp.where(hit, 1.0, 0.0).astype(BF)
    at, lane = iota((128, 256), 0), iota((128, 256), 1)
    c = (at * 57) >> 9
    tap = at - 9 * c
    b = (tap * 11) >> 5
    e = tap - 3 * b
    target = ((c >> 1) & 1) * 128 + (e * 2 + (c & 1)) * 16 + b * 3 + (c >> 2)
    for p in range(4):
        hit = (lane == target + (p & 1) * 32 + (p >> 1) * 3) & (at < 108)
        sel_ref[p] = jnp.where(hit, 1.0, 0.0).astype(BF)


def dot(a, b, ca=1, cb=0):
    return lax.dot_general(a, b, (((ca,), (cb,)), ((), ())), preferred_element_type=F32)


def edges_kernel(video_ref, own_ref, inner_ref, outer_ref, video_out, own_out, rows):
    core = lax.axis_index("band") % 2
    video_out[...] = video_ref[...]
    own_out[...] = own_ref[...]
    rows[...] = own_ref[...].astype(F32)
    for ref, r in ((inner_ref, 1 - core), (outer_ref, core)):
        ref[:48, :] = video_ref[...]
        edge = rows[pl.ds(r, 128, stride=2), :].astype(BF)
        for i in range(4):
            ref[48:, i * 128 : i * 128 + 128] = edge[i * 32 : i * 32 + 32, :]


def grown_kernel(own_ref, inner_ref, outer_ref, _, __, out_ref):
    core = lax.axis_index("band") % 2
    out_ref[:256, :] = own_ref[...]
    for side, ref in ((1 - core, inner_ref), (core, outer_ref)):
        for i in range(4):
            at = pl.multiple_of(256 + side * 128 + i * 32, 32)
            out_ref[pl.ds(at, 32), :] = ref[48:, i * 128 : i * 128 + 128]


def shifted(x, step):
    lanes = x.shape[1]
    lane = lax.broadcasted_iota(jnp.int32, x.shape, 1) % 128
    if step == -1:
        return jnp.where(lane == 0, 0.0, pltpu.roll(x, 1, 1))
    return jnp.where(lane == 127, 0.0, pltpu.roll(x, lanes - 1, 1))


def forward_kernel(
    inner_ref, own_ref, outer_ref, col_ref, row_ref, sel_ref, w1_ref,
    xc_ref, pre_ref, win_ref, one, two,
):
    band = lax.axis_index("band")
    core = band % 2
    last = lax.axis_size("band") - 1
    v = (
        dot(row_ref[2 - 2 * core][:, :48], inner_ref[:48, :])
        + dot(row_ref[1, :, :48], own_ref[...])
        + dot(row_ref[2 * core][:, :48], outer_ref[:48, :])
    ).astype(BF)
    h = dot(v, col_ref[...])
    top, low = h[:128], h[128:]
    for pm, half in enumerate((top + low, top - low)):
        even, odd = half[:, :256], half[:, 256:]
        streams = (shifted(odd, -1), even, odd, shifted(even, 1))
        for st in range(8):
            part = streams[st // 2][:, (st % 2) * 128 : (st % 2) * 128 + 128].astype(BF)
            for f in range(2):
                for r in range(4):
                    at = (f * 4 + r) * 16
                    one[f, pm * 128 + st * 16 : pm * 128 + st * 16 + 16, r * 128 : r * 128 + 128] = part[
                        at : at + 16, :
                    ]
    w1a, w1b = (
        jnp.concatenate([dot(w1_ref[a], sel_ref[p], 0, 0) for p in range(4)], 0).astype(BF)
        for a in range(2)
    )
    pres = (dot(w1b, one[0]), dot(w1a, one[0]) + dot(w1b, one[1]))
    lane = lax.broadcasted_iota(jnp.int32, (32, 512), 1)
    keep = ((lane >= 128) | (band > 0)) & ((lane < 384) | (band < last))
    for f in range(2):
        pre = pres[f]
        pre_ref[:, f * 256 : f * 256 + 256] = pre[:, 128:384]
        win_ref[:, f * 256 : f * 256 + 256] = one[f, :, 128:384]
        act = pre * jax.nn.sigmoid(pre)
        p, q, r, s = act[:32], act[32:64], act[64:96], act[96:]
        pq, pmq, rs, rms = p + q, p - q, r + s, r - s
        parts = (pq + rs, pmq + rms, pq - rs, pmq - rms)
        for k in range(4):
            part = jnp.where(keep, parts[k] * 0.5, 0.0)
            for r in range(4):
                two[r, pl.ds(k, 32, stride=4), :] = part[:, r * 128 : r * 128 + 128]
        x = jnp.concatenate([two[r] for r in range(4)], 1)
        for e, xe in enumerate((shifted(x, -1), x, shifted(x, 1))):
            xe = xe.astype(BF)
            for b in range(3):
                at = (b * 3 + e) * 128
                xc_ref[at : at + 128, f * 256 : f * 256 + 256] = xe[:, b * 128 : b * 128 + 256]


def hold_kernel(_, __, ___):
    pass


def latent_kernel(xc_ref, w2_ref, keep_ref, send_ref, lat):
    out = dot(w2_ref[2304:, :], xc_ref[...], 0, 0)
    more = dot(w2_ref[1152:2304, :], xc_ref[:, :256], 0, 0)
    lat[:, :256] = out[:, :256].astype(BF)
    lat[:, 256:] = (out[:, 256:] + more).astype(BF)
    chan = lax.axis_index("chan")
    for ref, i, k in ((keep_ref, 0, 0), (send_ref, 0, 1), (send_ref, 1, 2), (keep_ref, 1, 3)):
        ref[i] = lat[pl.ds(pl.multiple_of((chan ^ k) * 64, 64), 64), :]


def second_grad_kernel(
    xc_ref, c0_ref, c1_ref, c2_ref, c3_ref, lkeep_ref, lgot_ref,
    grown, keep_ref, send_ref, lown_ref, lsend_ref, rows, *, scale
):
    lown_ref[...] = lkeep_ref[0].astype(F32) + lgot_ref[0].astype(F32)
    lsend_ref[...] = (lkeep_ref[1].astype(F32) + lgot_ref[1].astype(F32)).astype(BF)
    chan = lax.axis_index("chan")
    core = lax.axis_index("band") % 2
    for k, ref in enumerate((c0_ref, c1_ref, c2_ref, c3_ref)):
        rows[...] = ref[...].astype(F32)
        at = pl.multiple_of((chan ^ k) * 64, 64)
        for f in range(2):
            for r in range(2):
                lane = f * 512 + r * 128 + 128
                part = rows[pl.ds(f * 2 + r, 64, stride=4), :]
                grown[pl.ds(at, 64), lane : lane + 128] = part.astype(BF)
            for side in range(2):
                lane = f * 512 + side * 384
                part = rows[pl.ds(256 + side * 128 + f, 64, stride=2), :]
                grown[pl.ds(at, 64), lane : lane + 128] = part.astype(BF)

    def put(early_ref, late_ref):
        c1 = grown[:, 640:896]
        early = dot(xc_ref[:, :256], c1, 1, 1) * scale
        late = (dot(xc_ref[:, :256], grown[:, 128:384], 1, 1) + dot(xc_ref[:, 256:], c1, 1, 1)) * scale
        for ref, g in ((early_ref, early), (late_ref, late)):
            ref[:1152, :] = g[:, :128].astype(BF)
            ref[1152:, :] = g[:, 128:].astype(BF)

    @pl.when(core == 0)
    def _():
        put(keep_ref, send_ref)

    @pl.when(core == 1)
    def _():
        put(send_ref, keep_ref)


def backward_kernel(grown, pre_ref, win_ref, w2_ref, sel_ref, g1_ref, back_s, *, scale):
    z0 = z1 = 0.0
    for b in range(3):
        lo = (2 - b) * 128
        c0, c1 = grown[:, lo : lo + 256], grown[:, 512 + lo : 768 + lo]
        wa = w2_ref[1152 + b * 384 : 1536 + b * 384, :]
        wb = w2_ref[2304 + b * 384 : 2688 + b * 384, :]
        z0 = z0 + dot(wb, c0) + dot(wa, c1)
        z1 = z1 + dot(wb, c1)
    for f, z in enumerate((z0, z1)):
        z = z[128:256] + shifted(z[:128], 1) + shifted(z[256:], -1)
        back_s[0], back_s[1] = z[:, :128], z[:, 128:]
        a0, a1, a2, a3 = (
            jnp.concatenate([back_s[r, pl.ds(k, 32, stride=4), :] for r in range(2)], 1)
            for k in range(4)
        )
        s01, d01, s23, d23 = a0 + a1, a0 - a1, a2 + a3, a2 - a3
        act = jnp.concatenate([s01 + s23, d01 + d23, s01 - s23, d01 - d23], 0) * 0.5
        pre = pre_ref[:, f * 256 : f * 256 + 256]
        gate = jax.nn.sigmoid(pre)
        back = (act * gate * (1.0 + pre * (1.0 - gate))).astype(BF)
        if f == 0:
            late = dot(back, win_ref[:, :256], 1, 1)
        else:
            early = dot(back, win_ref[:, :256], 1, 1)
            late = late + dot(back, win_ref[:, 256:], 1, 1)
    for a, g in enumerate((early, late)):
        g = g * scale
        hi = g.astype(BF)
        lo = (g - hi.astype(F32)).astype(BF)
        total = 0.0
        for p in range(4):
            rows = slice(32 * p, 32 * p + 32)
            total = total + dot(hi[rows], sel_ref[p], 1, 1)
            total = total + dot(lo[rows], sel_ref[p], 1, 1)
        g1_ref[32 * a : 32 * a + 32, :] = total.astype(BF)


def join_kernel(keep_ref, got_ref, g1_ref, sum_ref):
    sum_ref[:2304, :] = (keep_ref[...].astype(F32) + got_ref[...].astype(F32)).astype(BF)
    sum_ref[2304:, :] = g1_ref[...]


def share_kernel(got_ref, lown_ref, lgot_ref, out_ref, lat_ref, rows, wide, *, count):
    lat = lown_ref[...] + lgot_ref[...].astype(F32)
    for i in range(4):
        rows[pl.ds(i, 64, stride=4), :] = lat[:, i * 128 : i * 128 + 128]
    lat_ref[...] = rows[...].astype(BF)
    size = got_ref.shape[0] // count
    bunch = 8 if count % 8 == 0 else count
    block = bunch * size
    total = got_ref[:block, :].astype(F32)
    for i in range(block, count * size, block):
        total = total + got_ref[i : i + block, :].astype(F32)
    wide[...] = total
    total = wide[:size, :]
    for i in range(1, bunch):
        total = total + wide[i * size : i * size + size, :]
    for i in range(bunch):
        wide[i * size : i * size + size, :] = total
    total = wide[...].astype(BF)
    for i in range(0, count * size, block):
        out_ref[i : i + block, :] = total


def widen(from_ref, wide, to_ref, sems, first):
    copies = []
    for i in range(3):
        at = i * 384
        wide[at : at + 384, :128] = from_ref[at : at + 384, :].astype(F32)
        wide[at : at + 384, 128:] = from_ref[1152 + at : 1536 + at, :].astype(F32)
        rows = pl.ds(at, 384)
        copies.append(pltpu.make_async_copy(wide.at[rows], to_ref.at[rows], sems.at[first + i]))
        copies[-1].start()
    return copies


def first_half_kernel(mine_ref, g2_ref, g1_ref, zero, own, sems):
    core = lax.axis_index("band") % 2
    zero[...] = jnp.zeros((1152, 256), F32)
    clear = pltpu.make_async_copy(zero, g2_ref.at[0], sems.at[0])
    clear.start()
    copies = [clear] + widen(mine_ref, own, g2_ref.at[1 + core], sems, 1)
    g1_ref[...] = mine_ref[2304:, :]
    for copy in copies:
        copy.wait()


def other_half_kernel(_, mine_ref, other_ref, g2_ref, g1_ref, half, sems):
    core = lax.axis_index("band") % 2
    copies = widen(other_ref, half, g2_ref.at[2 - core], sems, 0)
    both = mine_ref[...].astype(F32) + other_ref[2304:2368, :].astype(F32)
    g1_ref[...] = jnp.zeros((12, 27, 32), F32)
    for a in range(2):
        taps = jnp.transpose(both[32 * a : 32 * a + 32, :])
        for c in range(12):
            g1_ref[c, 9 * a + 9 : 9 * a + 18, :] = taps[9 * c : 9 * c + 9, :]
    for copy in copies:
        copy.wait()


VMEM, HBM = pltpu.VMEM, pltpu.HBM


def call(kernel, outs, scratch, flops, *args, far=(), far_out=(), aliases=None):
    return pl.pallas_call(
        kernel,
        out_shape=[jax.ShapeDtypeStruct(*o) for o in outs],
        in_specs=[pl.BlockSpec(memory_space=HBM if i in far else VMEM) for i in range(len(args))],
        out_specs=[pl.BlockSpec(memory_space=HBM if i in far_out else VMEM) for i in range(len(outs))],
        scratch_shapes=[s if not isinstance(s, tuple) else pltpu.VMEM(*s) for s in scratch],
        input_output_aliases=aliases or {},
        compiler_params=pltpu.CompilerParams(vmem_limit_bytes=20 * 1024 * 1024),
        cost_estimate=pl.CostEstimate(flops=flops, bytes_accessed=1 << 20, transcendentals=0),
    )(*args)


def on_device(video, weight_one, weight_two, cotangent):
    n = lax.axis_size("band")
    flip = [(i, i ^ 1) for i in range(n)]
    frames, half_rows, half_cols = video.shape[1], n * 4, video.shape[3] // 2
    scale_one = 1.0 / math.sqrt(frames * half_rows * half_cols)
    scale_two = 1.0 / math.sqrt(frames * (half_rows // 2) * (half_cols // 2))

    flat, own = video.reshape(48, 512), cotangent.reshape(256, 128)

    def swap(x, k):
        return lax.ppermute(x, "chan", [(i, i ^ k) for i in range(4)])

    inner, outer, flat, own = call(
        edges_kernel,
        [((80, 512), BF), ((80, 512), BF), ((48, 512), BF), ((256, 128), BF)],
        [((256, 128), F32)],
        1 << 20,
        flat, own,
    )
    inner = lax.ppermute(inner, "band", flip)
    outer = lax.ppermute(outer, "band", [(i, i + 1 - 2 * (i % 2 == 0)) for i in range(1, n - 1)])
    cols, rows, sel = call(
        matrix_kernel,
        [((512, 512), BF), ((3, 256, 128), BF), ((4, 128, 256), BF)],
        [],
        1 << 20,
    )
    w1 = weight_one[9:].reshape(2, 9, 12, 32).transpose(0, 2, 1, 3).reshape(2, 108, 32)
    w1 = jnp.pad(w1, ((0, 0), (0, 20), (0, 0)))
    (own,) = call(
        grown_kernel, [((512, 128), BF)], [], 1 << 20, own, inner, outer, sel, w1,
        far=(3, 4),
    )
    near, far = swap(own, 1), swap(own, 3)
    w2 = weight_two.reshape(3456, 256)
    xc, pre, win = call(
        forward_kernel,
        [((1152, 512), BF), ((128, 512), F32), ((256, 512), BF)],
        [((2, 256, 512), BF), ((4, 128, 128), F32)],
        1 << 30,
        inner, flat, outer, cols, rows, sel, w1,
    )
    (near,) = call(
        hold_kernel, [((512, 128), BF)], [], 1 << 10, near, xc, far=(0, 1), far_out=(0,), aliases={0: 0}
    )
    others = [near, swap(near, 3), far]
    lat_keep, lat_send = call(
        latent_kernel, [((2, 64, 512), BF)] * 2, [((256, 512), BF)], 1 << 30, xc, w2
    )
    lat_got = swap(lat_send, 1)

    def second_grad(*refs):
        second_grad_kernel(*refs, scale=scale_two)

    cot, keep, send, lat_own, lat_send = call(
        second_grad,
        [
            ((256, 1024), BF), ((2304, 128), BF), ((2304, 128), BF),
            ((64, 512), F32), ((64, 512), BF),
        ],
        [((512, 128), F32)],
        1 << 30,
        xc, own, *others, lat_keep, lat_got,
    )
    lat_got = swap(lat_send, 3)
    got = lax.ppermute(send, "band", flip)

    def backward(*refs):
        backward_kernel(*refs, scale=scale_one)

    (g1,) = call(
        backward, [((64, 128), BF)], [((2, 128, 128), F32)], 1 << 30, cot, pre, win, w2, sel
    )
    (part,) = call(join_kernel, [((2368, 128), BF)], [], 1 << 20, keep, got, g1)
    half = n // 2
    groups = [[2 * i + c for i in range(half)] for c in range(2)]

    def exchange(x):
        x = x.reshape(half, 1184 // half, 2, 128)
        x = lax.all_to_all(x, "band", 0, 0, tiled=True, axis_index_groups=groups)
        return x.reshape(2368, 128)

    def share(*refs):
        share_kernel(*refs, count=half)

    part = exchange(part)
    mine, latent = call(
        share,
        [((2368, 128), BF), ((256, 128), BF)],
        [((256, 128), F32), ((2368 // half * min(half, 8), 128), F32)],
        1 << 20,
        part, lat_own, lat_got,
    )
    mine = exchange(mine)
    other = lax.ppermute(mine, "band", flip)
    g2, g1 = call(
        first_half_kernel,
        [((3, 1152, 256), F32), ((64, 128), BF)],
        [((1152, 256), F32), ((1152, 256), F32), pltpu.SemaphoreType.DMA((4,))],
        1 << 20,
        mine,
        far_out=(0,),
    )
    g2, g1 = call(
        other_half_kernel,
        [((3, 1152, 256), F32), ((12, 27, 32), F32)],
        [((1152, 256), F32), pltpu.SemaphoreType.DMA((3,))],
        1 << 20,
        g2, g1, other,
        far=(0,), far_out=(0,), aliases={0: 0},
    )
    return latent.reshape(64, 2, 2, 128), jnp.transpose(g1, (1, 0, 2)), g2.reshape(27, 128, 256)


def solution(mesh):
    return jax.shard_map(
        on_device,
        mesh=mesh,
        in_specs=(
            P(None, None, "band", None),
            P(None, None, "chan"),
            P(None, "chan", None),
            P("chan", None, "band", None),
        ),
        out_specs=(P("chan", None, "band", None), P(None, None, "chan"), P(None, "chan", None)),
        check_vma=False,
    )
```

```python
import math

import jax
import jax.numpy as jnp
from jax import lax
from jax.experimental import pallas as pl
from jax.experimental.pallas import tpu as pltpu
from jax.sharding import PartitionSpec as P

BF = jnp.bfloat16
F32 = jnp.float32


def iota(shape, axis):
    return lax.broadcasted_iota(jnp.int32, shape, axis)


def matrix_kernel(col_ref, row_ref, sel_ref):
    u, w = iota((512, 128), 0), iota((512, 128), 1)
    for s in range(2):
        hit = ((u >> 2) == w) & (((u >> 1) & 1) == s)
        for t in range(2):
            value = 0.5 if t == 0 else jnp.where((u & 1) == 1, -0.5, 0.5)
            at = (s * 2 + t) * 128
            col_ref[:, at : at + 128] = jnp.where(hit, value, 0.0).astype(BF)
    at, lane = iota((256, 128), 0), iota((256, 128), 1)
    m, r, f, tb = at & 15, (at >> 4) & 3, (at >> 6) & 1, at >> 7
    wi = (m * 11) >> 5
    y = 4 * r + 2 * wi + tb + 2
    for part in range(3):
        hit = (lane == (m - 3 * wi) * 16 + f * 8 + y - 8 * part) & (m < 12)
        hit = hit & (y >= 8 * part) & (y < 8 * part + 8)
        row_ref[part] = jnp.where(hit, 1.0, 0.0).astype(BF)
    at, lane = iota((128, 256), 0), iota((128, 256), 1)
    c = (at * 57) >> 9
    tap = at - 9 * c
    b = (tap * 11) >> 5
    e = tap - 3 * b
    target = ((c >> 1) & 1) * 128 + (e * 2 + (c & 1)) * 16 + b * 3 + (c >> 2)
    for p in range(4):
        hit = (lane == target + (p & 1) * 32 + (p >> 1) * 3) & (at < 108)
        sel_ref[p] = jnp.where(hit, 1.0, 0.0).astype(BF)


def dot(a, b, ca=1, cb=0):
    return lax.dot_general(a, b, (((ca,), (cb,)), ((), ())), preferred_element_type=F32)


def edges_kernel(video_ref, own_ref, inner_ref, outer_ref, video_out, own_out, rows):
    core = lax.axis_index("band") % 2
    video_out[...] = video_ref[...]
    own_out[...] = own_ref[...]
    rows[...] = own_ref[...].astype(F32)
    for ref, r in ((inner_ref, 1 - core), (outer_ref, core)):
        ref[:48, :] = video_ref[...]
        edge = rows[pl.ds(r, 128, stride=2), :].astype(BF)
        for i in range(4):
            ref[48:, i * 128 : i * 128 + 128] = edge[i * 32 : i * 32 + 32, :]


def grown_kernel(own_ref, inner_ref, outer_ref, _, __, out_ref):
    core = lax.axis_index("band") % 2
    out_ref[:256, :] = own_ref[...]
    for side, ref in ((1 - core, inner_ref), (core, outer_ref)):
        for i in range(4):
            at = pl.multiple_of(256 + side * 128 + i * 32, 32)
            out_ref[pl.ds(at, 32), :] = ref[48:, i * 128 : i * 128 + 128]


def shifted(x, step):
    lanes = x.shape[1]
    lane = lax.broadcasted_iota(jnp.int32, x.shape, 1) % 128
    if step == -1:
        return jnp.where(lane == 0, 0.0, pltpu.roll(x, 1, 1))
    return jnp.where(lane == 127, 0.0, pltpu.roll(x, lanes - 1, 1))


def forward_kernel(
    inner_ref, own_ref, outer_ref, col_ref, row_ref, sel_ref, w1_ref, cot_ref,
    xc_ref, pre_ref, win_ref, cot_out, one, two,
):
    band = lax.axis_index("band")
    core = band % 2
    cot_out[...] = cot_ref[...]
    last = lax.axis_size("band") - 1
    v = (
        dot(row_ref[2 - 2 * core][:, :48], inner_ref[:48, :])
        + dot(row_ref[1, :, :48], own_ref[...])
        + dot(row_ref[2 * core][:, :48], outer_ref[:48, :])
    ).astype(BF)
    h = dot(v, col_ref[...])
    top, low = h[:128], h[128:]
    for pm, half in enumerate((top + low, top - low)):
        even, odd = half[:, :256], half[:, 256:]
        streams = (shifted(odd, -1), even, odd, shifted(even, 1))
        for st in range(8):
            part = streams[st // 2][:, (st % 2) * 128 : (st % 2) * 128 + 128].astype(BF)
            for f in range(2):
                for r in range(4):
                    at = (f * 4 + r) * 16
                    one[f, pm * 128 + st * 16 : pm * 128 + st * 16 + 16, r * 128 : r * 128 + 128] = part[
                        at : at + 16, :
                    ]
    w1a, w1b = (
        jnp.concatenate([dot(w1_ref[a], sel_ref[p], 0, 0) for p in range(4)], 0).astype(BF)
        for a in range(2)
    )
    pres = (dot(w1b, one[0]), dot(w1a, one[0]) + dot(w1b, one[1]))
    lane = lax.broadcasted_iota(jnp.int32, (32, 512), 1)
    keep = ((lane >= 128) | (band > 0)) & ((lane < 384) | (band < last))
    for f in range(2):
        pre = pres[f]
        pre_ref[:, f * 256 : f * 256 + 256] = pre[:, 128:384]
        win_ref[:, f * 256 : f * 256 + 256] = one[f, :, 128:384]
        act = pre * jax.nn.sigmoid(pre)
        p, q, r, s = act[:32], act[32:64], act[64:96], act[96:]
        pq, pmq, rs, rms = p + q, p - q, r + s, r - s
        parts = (pq + rs, pmq + rms, pq - rs, pmq - rms)
        for k in range(4):
            part = jnp.where(keep, parts[k] * 0.5, 0.0)
            for r in range(4):
                two[r, pl.ds(k, 32, stride=4), :] = part[:, r * 128 : r * 128 + 128]
        x = jnp.concatenate([two[r] for r in range(4)], 1)
        for e, xe in enumerate((shifted(x, -1), x, shifted(x, 1))):
            xe = xe.astype(BF)
            for b in range(3):
                at = (b * 3 + e) * 128
                xc_ref[at : at + 128, f * 256 : f * 256 + 256] = xe[:, b * 128 : b * 128 + 256]


def hold_kernel(_, __, ___):
    pass


def latent_kernel(xc_ref, w2_ref, keep_ref, send_ref, lat):
    out = dot(w2_ref[2304:, :], xc_ref[...], 0, 0)
    more = dot(w2_ref[1152:2304, :], xc_ref[:, :256], 0, 0)
    lat[:, :256] = out[:, :256].astype(BF)
    lat[:, 256:] = (out[:, 256:] + more).astype(BF)
    chan = lax.axis_index("chan")
    for ref, i, k in ((keep_ref, 0, 0), (send_ref, 0, 1), (send_ref, 1, 2), (keep_ref, 1, 3)):
        ref[i] = lat[pl.ds(pl.multiple_of((chan ^ k) * 64, 64), 64), :]


def second_grad_kernel(
    xc_ref, c0_ref, c1_ref, c2_ref, c3_ref, lkeep_ref, lgot_ref,
    grown, keep_ref, send_ref, lown_ref, lsend_ref, rows, *, scale
):
    lown_ref[...] = lkeep_ref[0].astype(F32) + lgot_ref[0].astype(F32)
    lsend_ref[...] = (lkeep_ref[1].astype(F32) + lgot_ref[1].astype(F32)).astype(BF)
    chan = lax.axis_index("chan")
    core = lax.axis_index("band") % 2
    for k, ref in enumerate((c0_ref, c1_ref, c2_ref, c3_ref)):
        rows[...] = ref[...].astype(F32)
        at = pl.multiple_of((chan ^ k) * 64, 64)
        for f in range(2):
            for r in range(2):
                lane = f * 512 + r * 128 + 128
                part = rows[pl.ds(f * 2 + r, 64, stride=4), :]
                grown[pl.ds(at, 64), lane : lane + 128] = part.astype(BF)
            for side in range(2):
                lane = f * 512 + side * 384
                part = rows[pl.ds(256 + side * 128 + f, 64, stride=2), :]
                grown[pl.ds(at, 64), lane : lane + 128] = part.astype(BF)

    def put(early_ref, late_ref):
        c1 = grown[:, 640:896]
        early = dot(xc_ref[:, :256], c1, 1, 1) * scale
        late = (dot(xc_ref[:, :256], grown[:, 128:384], 1, 1) + dot(xc_ref[:, 256:], c1, 1, 1)) * scale
        for ref, g in ((early_ref, early), (late_ref, late)):
            ref[:1152, :] = g[:, :128].astype(BF)
            ref[1152:, :] = g[:, 128:].astype(BF)

    @pl.when(core == 0)
    def _():
        put(keep_ref, send_ref)

    @pl.when(core == 1)
    def _():
        put(send_ref, keep_ref)


def backward_kernel(grown, pre_ref, win_ref, w2_ref, sel_ref, g1_ref, back_s, *, scale):
    z0 = z1 = 0.0
    for b in range(3):
        lo = (2 - b) * 128
        c0, c1 = grown[:, lo : lo + 256], grown[:, 512 + lo : 768 + lo]
        wa = w2_ref[1152 + b * 384 : 1536 + b * 384, :]
        wb = w2_ref[2304 + b * 384 : 2688 + b * 384, :]
        z0 = z0 + dot(wb, c0) + dot(wa, c1)
        z1 = z1 + dot(wb, c1)
    for f, z in enumerate((z0, z1)):
        z = z[128:256] + shifted(z[:128], 1) + shifted(z[256:], -1)
        back_s[0], back_s[1] = z[:, :128], z[:, 128:]
        a0, a1, a2, a3 = (
            jnp.concatenate([back_s[r, pl.ds(k, 32, stride=4), :] for r in range(2)], 1)
            for k in range(4)
        )
        s01, d01, s23, d23 = a0 + a1, a0 - a1, a2 + a3, a2 - a3
        act = jnp.concatenate([s01 + s23, d01 + d23, s01 - s23, d01 - d23], 0) * 0.5
        pre = pre_ref[:, f * 256 : f * 256 + 256]
        gate = jax.nn.sigmoid(pre)
        back = (act * gate * (1.0 + pre * (1.0 - gate))).astype(BF)
        if f == 0:
            late = dot(back, win_ref[:, :256], 1, 1)
        else:
            early = dot(back, win_ref[:, :256], 1, 1)
            late = late + dot(back, win_ref[:, 256:], 1, 1)
    for a, g in enumerate((early, late)):
        g = g * scale
        hi = g.astype(BF)
        lo = (g - hi.astype(F32)).astype(BF)
        total = 0.0
        for p in range(4):
            rows = slice(32 * p, 32 * p + 32)
            total = total + dot(hi[rows], sel_ref[p], 1, 1)
            total = total + dot(lo[rows], sel_ref[p], 1, 1)
        g1_ref[32 * a : 32 * a + 32, :] = total.astype(BF)


def join_kernel(keep_ref, got_ref, g1_ref, sum_ref):
    sum_ref[:2304, :] = (keep_ref[...].astype(F32) + got_ref[...].astype(F32)).astype(BF)
    sum_ref[2304:, :] = g1_ref[...]


def share_kernel(got_ref, lown_ref, lgot_ref, out_ref, lat_ref, rows, wide, *, count):
    lat = lown_ref[...] + lgot_ref[...].astype(F32)
    for i in range(4):
        rows[pl.ds(i, 64, stride=4), :] = lat[:, i * 128 : i * 128 + 128]
    lat_ref[...] = rows[...].astype(BF)
    size = got_ref.shape[0] // count
    bunch = 8 if count % 8 == 0 else count
    block = bunch * size
    total = got_ref[:block, :].astype(F32)
    for i in range(block, count * size, block):
        total = total + got_ref[i : i + block, :].astype(F32)
    wide[...] = total
    total = wide[:size, :]
    for i in range(1, bunch):
        total = total + wide[i * size : i * size + size, :]
    for i in range(bunch):
        wide[i * size : i * size + size, :] = total
    total = wide[...].astype(BF)
    for i in range(0, count * size, block):
        out_ref[i : i + block, :] = total


def widen(from_ref, wide, to_ref, sems, first):
    copies = []
    for i in range(3):
        at = i * 384
        wide[at : at + 384, :128] = from_ref[at : at + 384, :].astype(F32)
        wide[at : at + 384, 128:] = from_ref[1152 + at : 1536 + at, :].astype(F32)
        rows = pl.ds(at, 384)
        copies.append(pltpu.make_async_copy(wide.at[rows], to_ref.at[rows], sems.at[first + i]))
        copies[-1].start()
    return copies


def first_half_kernel(mine_ref, g2_ref, g1_ref, zero, own, sems):
    core = lax.axis_index("band") % 2
    zero[...] = jnp.zeros((1152, 256), F32)
    clear = pltpu.make_async_copy(zero, g2_ref.at[0], sems.at[0])
    clear.start()
    copies = [clear] + widen(mine_ref, own, g2_ref.at[1 + core], sems, 1)
    g1_ref[...] = mine_ref[2304:, :]
    for copy in copies:
        copy.wait()


def other_half_kernel(_, mine_ref, other_ref, g2_ref, g1_ref, half, taps_s, sems):
    core = lax.axis_index("band") % 2
    both = mine_ref[...].astype(F32) + other_ref[2304:2368, :].astype(F32)
    taps_s[...] = jnp.zeros((12, 27, 32), F32)
    for a in range(2):
        taps = jnp.transpose(both[32 * a : 32 * a + 32, :])
        for c in range(12):
            taps_s[c, 9 * a + 9 : 9 * a + 18, :] = taps[9 * c : 9 * c + 9, :]
    first = pltpu.make_async_copy(taps_s, g1_ref, sems.at[3])
    first.start()
    for copy in [first] + widen(other_ref, half, g2_ref.at[2 - core], sems, 0):
        copy.wait()


VMEM, HBM = pltpu.VMEM, pltpu.HBM


def call(kernel, outs, scratch, flops, *args, far=(), far_out=(), aliases=None):
    return pl.pallas_call(
        kernel,
        out_shape=[jax.ShapeDtypeStruct(*o) for o in outs],
        in_specs=[pl.BlockSpec(memory_space=HBM if i in far else VMEM) for i in range(len(args))],
        out_specs=[pl.BlockSpec(memory_space=HBM if i in far_out else VMEM) for i in range(len(outs))],
        scratch_shapes=[s if not isinstance(s, tuple) else pltpu.VMEM(*s) for s in scratch],
        input_output_aliases=aliases or {},
        compiler_params=pltpu.CompilerParams(vmem_limit_bytes=20 * 1024 * 1024),
        cost_estimate=pl.CostEstimate(flops=flops, bytes_accessed=1 << 20, transcendentals=0),
    )(*args)


def on_device(video, weight_one, weight_two, cotangent):
    n = lax.axis_size("band")
    flip = [(i, i ^ 1) for i in range(n)]
    frames, half_rows, half_cols = video.shape[1], n * 4, video.shape[3] // 2
    scale_one = 1.0 / math.sqrt(frames * half_rows * half_cols)
    scale_two = 1.0 / math.sqrt(frames * (half_rows // 2) * (half_cols // 2))

    flat, own = video.reshape(48, 512), cotangent.reshape(256, 128)

    def swap(x, k):
        return lax.ppermute(x, "chan", [(i, i ^ k) for i in range(4)])

    inner, outer, flat, own = call(
        edges_kernel,
        [((80, 512), BF), ((80, 512), BF), ((48, 512), BF), ((256, 128), BF)],
        [((256, 128), F32)],
        1 << 20,
        flat, own,
    )
    inner = lax.ppermute(inner, "band", flip)
    outer = lax.ppermute(outer, "band", [(i, i + 1 - 2 * (i % 2 == 0)) for i in range(1, n - 1)])
    cols, rows, sel = call(
        matrix_kernel,
        [((512, 512), BF), ((3, 256, 128), BF), ((4, 128, 256), BF)],
        [],
        1 << 20,
    )
    w1 = weight_one[9:].reshape(2, 9, 12, 32).transpose(0, 2, 1, 3).reshape(2, 108, 32)
    w1 = jnp.pad(w1, ((0, 0), (0, 20), (0, 0)))
    (own,) = call(
        grown_kernel, [((512, 128), BF)], [], 1 << 20, own, inner, outer, sel, w1,
        far=(3, 4),
    )
    near = swap(own, 1)
    w2 = weight_two.reshape(3456, 256)
    xc, pre, win, own = call(
        forward_kernel,
        [((1152, 512), BF), ((128, 512), F32), ((256, 512), BF), ((512, 128), BF)],
        [((2, 256, 512), BF), ((4, 128, 128), F32)],
        1 << 30,
        inner, flat, outer, cols, rows, sel, w1, own,
    )
    far = swap(own, 3)
    (near,) = call(
        hold_kernel, [((512, 128), BF)], [], 1 << 10, near, xc, far=(0, 1), far_out=(0,), aliases={0: 0}
    )
    others = [near, swap(near, 3), far]
    lat_keep, lat_send = call(
        latent_kernel, [((2, 64, 512), BF)] * 2, [((256, 512), BF)], 1 << 30, xc, w2
    )
    lat_got = swap(lat_send, 1)

    def second_grad(*refs):
        second_grad_kernel(*refs, scale=scale_two)

    cot, keep, send, lat_own, lat_send = call(
        second_grad,
        [
            ((256, 1024), BF), ((2304, 128), BF), ((2304, 128), BF),
            ((64, 512), F32), ((64, 512), BF),
        ],
        [((512, 128), F32)],
        1 << 30,
        xc, own, *others, lat_keep, lat_got,
    )
    lat_got = swap(lat_send, 3)
    got = lax.ppermute(send, "band", flip)

    def backward(*refs):
        backward_kernel(*refs, scale=scale_one)

    (g1,) = call(
        backward, [((64, 128), BF)], [((2, 128, 128), F32)], 1 << 30, cot, pre, win, w2, sel
    )
    (part,) = call(join_kernel, [((2368, 128), BF)], [], 1 << 20, keep, got, g1)
    half = n // 2
    groups = [[2 * i + c for i in range(half)] for c in range(2)]

    def exchange(x):
        x = x.reshape(half, 1184 // half, 2, 128)
        x = lax.all_to_all(x, "band", 0, 0, tiled=True, axis_index_groups=groups)
        return x.reshape(2368, 128)

    def share(*refs):
        share_kernel(*refs, count=half)

    part = exchange(part)
    mine, latent = call(
        share,
        [((2368, 128), BF), ((256, 128), BF)],
        [((256, 128), F32), ((2368 // half * min(half, 8), 128), F32)],
        1 << 20,
        part, lat_own, lat_got,
    )
    mine = exchange(mine)
    other = lax.ppermute(mine, "band", flip)
    g2, g1 = call(
        first_half_kernel,
        [((3, 1152, 256), F32), ((64, 128), BF)],
        [((1152, 256), F32), ((1152, 256), F32), pltpu.SemaphoreType.DMA((4,))],
        1 << 20,
        mine,
        far_out=(0,),
    )
    g2, g1 = call(
        other_half_kernel,
        [((3, 1152, 256), F32), ((12, 27, 32), F32)],
        [((1152, 256), F32), ((12, 27, 32), F32), pltpu.SemaphoreType.DMA((4,))],
        1 << 20,
        g2, g1, other,
        far=(0,), far_out=(0, 1), aliases={0: 0},
    )
    return latent.reshape(64, 2, 2, 128), jnp.transpose(g1, (1, 0, 2)), g2.reshape(27, 128, 256)


def solution(mesh):
    return jax.shard_map(
        on_device,
        mesh=mesh,
        in_specs=(
            P(None, None, "band", None),
            P(None, None, "chan"),
            P(None, "chan", None),
            P("chan", None, "band", None),
        ),
        out_specs=(P("chan", None, "band", None), P(None, None, "chan"), P(None, "chan", None)),
        check_vma=False,
    )
```

```python
import math

import jax
import jax.numpy as jnp
from jax import lax
from jax.experimental import pallas as pl
from jax.experimental.pallas import tpu as pltpu
from jax.sharding import PartitionSpec as P

BF = jnp.bfloat16
F32 = jnp.float32


def iota(shape, axis):
    return lax.broadcasted_iota(jnp.int32, shape, axis)


def matrix_kernel(col_ref, row_ref, sel_ref):
    u, w = iota((512, 128), 0), iota((512, 128), 1)
    for s in range(2):
        hit = ((u >> 2) == w) & (((u >> 1) & 1) == s)
        for t in range(2):
            value = 0.5 if t == 0 else jnp.where((u & 1) == 1, -0.5, 0.5)
            at = (s * 2 + t) * 128
            col_ref[:, at : at + 128] = jnp.where(hit, value, 0.0).astype(BF)
    at, lane = iota((256, 128), 0), iota((256, 128), 1)
    m, r, f, tb = at & 15, (at >> 4) & 3, (at >> 6) & 1, at >> 7
    wi = (m * 11) >> 5
    y = 4 * r + 2 * wi + tb + 2
    for part in range(3):
        hit = (lane == (m - 3 * wi) * 16 + f * 8 + y - 8 * part) & (m < 12)
        hit = hit & (y >= 8 * part) & (y < 8 * part + 8)
        row_ref[part] = jnp.where(hit, 1.0, 0.0).astype(BF)
    at, lane = iota((128, 256), 0), iota((128, 256), 1)
    c = (at * 57) >> 9
    tap = at - 9 * c
    b = (tap * 11) >> 5
    e = tap - 3 * b
    target = ((c >> 1) & 1) * 128 + (e * 2 + (c & 1)) * 16 + b * 3 + (c >> 2)
    for p in range(4):
        hit = (lane == target + (p & 1) * 32 + (p >> 1) * 3) & (at < 108)
        sel_ref[p] = jnp.where(hit, 1.0, 0.0).astype(BF)


def dot(a, b, ca=1, cb=0):
    return lax.dot_general(a, b, (((ca,), (cb,)), ((), ())), preferred_element_type=F32)


def edges_kernel(video_ref, own_ref, inner_ref, outer_ref, video_out, own_out, rows):
    core = lax.axis_index("band") % 2
    video_out[...] = video_ref[...]
    own_out[...] = own_ref[...]
    rows[...] = own_ref[...].astype(F32)
    for ref, r in ((inner_ref, 1 - core), (outer_ref, core)):
        ref[:48, :] = video_ref[...]
        edge = rows[pl.ds(r, 128, stride=2), :].astype(BF)
        for i in range(4):
            ref[48:, i * 128 : i * 128 + 128] = edge[i * 32 : i * 32 + 32, :]


def grown_kernel(own_ref, inner_ref, outer_ref, _, __, out_ref):
    core = lax.axis_index("band") % 2
    out_ref[:256, :] = own_ref[...]
    for side, ref in ((1 - core, inner_ref), (core, outer_ref)):
        for i in range(4):
            at = pl.multiple_of(256 + side * 128 + i * 32, 32)
            out_ref[pl.ds(at, 32), :] = ref[48:, i * 128 : i * 128 + 128]


def shifted(x, step):
    lanes = x.shape[1]
    lane = lax.broadcasted_iota(jnp.int32, x.shape, 1) % 128
    if step == -1:
        return jnp.where(lane == 0, 0.0, pltpu.roll(x, 1, 1))
    return jnp.where(lane == 127, 0.0, pltpu.roll(x, lanes - 1, 1))


def forward_kernel(
    inner_ref, own_ref, outer_ref, col_ref, row_ref, sel_ref, w1_ref, cot_ref,
    xc_ref, pre_ref, win_ref, cot_out, one, two,
):
    band = lax.axis_index("band")
    core = band % 2
    cot_out[...] = cot_ref[...]
    last = lax.axis_size("band") - 1
    v = (
        dot(row_ref[2 - 2 * core][:, :48], inner_ref[:48, :])
        + dot(row_ref[1, :, :48], own_ref[...])
        + dot(row_ref[2 * core][:, :48], outer_ref[:48, :])
    ).astype(BF)
    h = dot(v, col_ref[...])
    top, low = h[:128], h[128:]
    for pm, half in enumerate((top + low, top - low)):
        even, odd = half[:, :256], half[:, 256:]
        streams = (shifted(odd, -1), even, odd, shifted(even, 1))
        for st in range(8):
            part = streams[st // 2][:, (st % 2) * 128 : (st % 2) * 128 + 128].astype(BF)
            for f in range(2):
                for r in range(4):
                    at = (f * 4 + r) * 16
                    one[f, pm * 128 + st * 16 : pm * 128 + st * 16 + 16, r * 128 : r * 128 + 128] = part[
                        at : at + 16, :
                    ]
    w1a, w1b = (
        jnp.concatenate([dot(w1_ref[a], sel_ref[p], 0, 0) for p in range(4)], 0).astype(BF)
        for a in range(2)
    )
    pres = (dot(w1b, one[0]), dot(w1a, one[0]) + dot(w1b, one[1]))
    lane = lax.broadcasted_iota(jnp.int32, (32, 512), 1)
    keep = ((lane >= 128) | (band > 0)) & ((lane < 384) | (band < last))
    for f in range(2):
        pre = pres[f]
        pre_ref[:, f * 256 : f * 256 + 256] = pre[:, 128:384]
        win_ref[:, f * 256 : f * 256 + 256] = one[f, :, 128:384]
        act = pre * jax.nn.sigmoid(pre)
        p, q, r, s = act[:32], act[32:64], act[64:96], act[96:]
        pq, pmq, rs, rms = p + q, p - q, r + s, r - s
        parts = (pq + rs, pmq + rms, pq - rs, pmq - rms)
        for k in range(4):
            part = jnp.where(keep, parts[k] * 0.5, 0.0)
            for r in range(4):
                two[r, pl.ds(k, 32, stride=4), :] = part[:, r * 128 : r * 128 + 128]
        x = jnp.concatenate([two[r] for r in range(4)], 1)
        for e, xe in enumerate((shifted(x, -1), x, shifted(x, 1))):
            xe = xe.astype(BF)
            for b in range(3):
                at = (b * 3 + e) * 128
                xc_ref[at : at + 128, f * 256 : f * 256 + 256] = xe[:, b * 128 : b * 128 + 256]


def first_rows_kernel(in_ref, _, out_ref):
    out_ref[...] = in_ref[:256, :]


def last_rows_kernel(in_ref, out_ref):
    out_ref[...] = in_ref[256:, :]


def latent_kernel(xc_ref, w2_ref, keep_ref, send_ref, lat):
    out = dot(w2_ref[2304:, :], xc_ref[...], 0, 0)
    more = dot(w2_ref[1152:2304, :], xc_ref[:, :256], 0, 0)
    lat[:, :256] = out[:, :256].astype(BF)
    lat[:, 256:] = (out[:, 256:] + more).astype(BF)
    chan = lax.axis_index("chan")
    for ref, i, k in ((keep_ref, 0, 0), (send_ref, 0, 1), (send_ref, 1, 2), (keep_ref, 1, 3)):
        ref[i] = lat[pl.ds(pl.multiple_of((chan ^ k) * 64, 64), 64), :]


def second_grad_kernel(
    xc_ref, c0_ref, c1_ref, c3_ref, own2_ref, outer2_ref, lkeep_ref, lgot_ref,
    grown, keep_ref, send_ref, lown_ref, lsend_ref, rows, *, scale
):
    lown_ref[...] = lkeep_ref[0].astype(F32) + lgot_ref[0].astype(F32)
    lsend_ref[...] = (lkeep_ref[1].astype(F32) + lgot_ref[1].astype(F32)).astype(BF)
    chan = lax.axis_index("chan")
    core = lax.axis_index("band") % 2
    for k, ref in enumerate((c0_ref, c1_ref, None, c3_ref)):
        if ref is None:
            rows[:256, :] = own2_ref[...].astype(F32)
            rows[256:, :] = outer2_ref[...].astype(F32)
        else:
            rows[...] = ref[...].astype(F32)
        at = pl.multiple_of((chan ^ k) * 64, 64)
        for f in range(2):
            for r in range(2):
                lane = f * 512 + r * 128 + 128
                part = rows[pl.ds(f * 2 + r, 64, stride=4), :]
                grown[pl.ds(at, 64), lane : lane + 128] = part.astype(BF)
            for side in range(2):
                lane = f * 512 + side * 384
                part = rows[pl.ds(256 + side * 128 + f, 64, stride=2), :]
                grown[pl.ds(at, 64), lane : lane + 128] = part.astype(BF)

    def put(early_ref, late_ref):
        c1 = grown[:, 640:896]
        early = dot(xc_ref[:, :256], c1, 1, 1) * scale
        late = (dot(xc_ref[:, :256], grown[:, 128:384], 1, 1) + dot(xc_ref[:, 256:], c1, 1, 1)) * scale
        for ref, g in ((early_ref, early), (late_ref, late)):
            ref[:1152, :] = g[:, :128].astype(BF)
            ref[1152:, :] = g[:, 128:].astype(BF)

    @pl.when(core == 0)
    def _():
        put(keep_ref, send_ref)

    @pl.when(core == 1)
    def _():
        put(send_ref, keep_ref)


def backward_kernel(grown, pre_ref, win_ref, w2_ref, sel_ref, g1_ref, back_s, *, scale):
    z0 = z1 = 0.0
    for b in range(3):
        lo = (2 - b) * 128
        c0, c1 = grown[:, lo : lo + 256], grown[:, 512 + lo : 768 + lo]
        wa = w2_ref[1152 + b * 384 : 1536 + b * 384, :]
        wb = w2_ref[2304 + b * 384 : 2688 + b * 384, :]
        z0 = z0 + dot(wb, c0) + dot(wa, c1)
        z1 = z1 + dot(wb, c1)
    for f, z in enumerate((z0, z1)):
        z = z[128:256] + shifted(z[:128], 1) + shifted(z[256:], -1)
        back_s[0], back_s[1] = z[:, :128], z[:, 128:]
        a0, a1, a2, a3 = (
            jnp.concatenate([back_s[r, pl.ds(k, 32, stride=4), :] for r in range(2)], 1)
            for k in range(4)
        )
        s01, d01, s23, d23 = a0 + a1, a0 - a1, a2 + a3, a2 - a3
        act = jnp.concatenate([s01 + s23, d01 + d23, s01 - s23, d01 - d23], 0) * 0.5
        pre = pre_ref[:, f * 256 : f * 256 + 256]
        gate = jax.nn.sigmoid(pre)
        back = (act * gate * (1.0 + pre * (1.0 - gate))).astype(BF)
        if f == 0:
            late = dot(back, win_ref[:, :256], 1, 1)
        else:
            early = dot(back, win_ref[:, :256], 1, 1)
            late = late + dot(back, win_ref[:, 256:], 1, 1)
    for a, g in enumerate((early, late)):
        g = g * scale
        hi = g.astype(BF)
        lo = (g - hi.astype(F32)).astype(BF)
        total = 0.0
        for p in range(4):
            rows = slice(32 * p, 32 * p + 32)
            total = total + dot(hi[rows], sel_ref[p], 1, 1)
            total = total + dot(lo[rows], sel_ref[p], 1, 1)
        g1_ref[32 * a : 32 * a + 32, :] = total.astype(BF)


def join_kernel(keep_ref, got_ref, g1_ref, sum_ref):
    sum_ref[:2304, :] = (keep_ref[...].astype(F32) + got_ref[...].astype(F32)).astype(BF)
    sum_ref[2304:, :] = g1_ref[...]


def share_kernel(got_ref, lown_ref, lgot_ref, out_ref, lat_ref, rows, wide, *, count):
    lat = lown_ref[...] + lgot_ref[...].astype(F32)
    for i in range(4):
        rows[pl.ds(i, 64, stride=4), :] = lat[:, i * 128 : i * 128 + 128]
    lat_ref[...] = rows[...].astype(BF)
    size = got_ref.shape[0] // count
    bunch = 8 if count % 8 == 0 else count
    block = bunch * size
    total = got_ref[:block, :].astype(F32)
    for i in range(block, count * size, block):
        total = total + got_ref[i : i + block, :].astype(F32)
    wide[...] = total
    total = wide[:size, :]
    for i in range(1, bunch):
        total = total + wide[i * size : i * size + size, :]
    for i in range(bunch):
        wide[i * size : i * size + size, :] = total
    total = wide[...].astype(BF)
    for i in range(0, count * size, block):
        out_ref[i : i + block, :] = total


def widen(from_ref, wide, to_ref, sems, first):
    copies = []
    for i in range(3):
        at = i * 384
        wide[at : at + 384, :128] = from_ref[at : at + 384, :].astype(F32)
        wide[at : at + 384, 128:] = from_ref[1152 + at : 1536 + at, :].astype(F32)
        rows = pl.ds(at, 384)
        copies.append(pltpu.make_async_copy(wide.at[rows], to_ref.at[rows], sems.at[first + i]))
        copies[-1].start()
    return copies


def first_half_kernel(mine_ref, g2_ref, g1_ref, zero, own, sems):
    core = lax.axis_index("band") % 2
    zero[...] = jnp.zeros((1152, 256), F32)
    clear = pltpu.make_async_copy(zero, g2_ref.at[0], sems.at[0])
    clear.start()
    copies = [clear] + widen(mine_ref, own, g2_ref.at[1 + core], sems, 1)
    g1_ref[...] = mine_ref[2304:, :]
    for copy in copies:
        copy.wait()


def other_half_kernel(_, mine_ref, other_ref, g2_ref, g1_ref, half, taps_s, sems):
    core = lax.axis_index("band") % 2
    both = mine_ref[...].astype(F32) + other_ref[2304:2368, :].astype(F32)
    taps_s[...] = jnp.zeros((12, 27, 32), F32)
    for a in range(2):
        taps = jnp.transpose(both[32 * a : 32 * a + 32, :])
        for c in range(12):
            taps_s[c, 9 * a + 9 : 9 * a + 18, :] = taps[9 * c : 9 * c + 9, :]
    first = pltpu.make_async_copy(taps_s, g1_ref, sems.at[3])
    first.start()
    for copy in [first] + widen(other_ref, half, g2_ref.at[2 - core], sems, 0):
        copy.wait()


VMEM, HBM = pltpu.VMEM, pltpu.HBM


def call(kernel, outs, scratch, flops, *args, far=(), far_out=(), aliases=None):
    return pl.pallas_call(
        kernel,
        out_shape=[jax.ShapeDtypeStruct(*o) for o in outs],
        in_specs=[pl.BlockSpec(memory_space=HBM if i in far else VMEM) for i in range(len(args))],
        out_specs=[pl.BlockSpec(memory_space=HBM if i in far_out else VMEM) for i in range(len(outs))],
        scratch_shapes=[s if not isinstance(s, tuple) else pltpu.VMEM(*s) for s in scratch],
        input_output_aliases=aliases or {},
        compiler_params=pltpu.CompilerParams(vmem_limit_bytes=20 * 1024 * 1024),
        cost_estimate=pl.CostEstimate(flops=flops, bytes_accessed=1 << 20, transcendentals=0),
    )(*args)


def on_device(video, weight_one, weight_two, cotangent):
    n = lax.axis_size("band")
    flip = [(i, i ^ 1) for i in range(n)]
    frames, half_rows, half_cols = video.shape[1], n * 4, video.shape[3] // 2
    scale_one = 1.0 / math.sqrt(frames * half_rows * half_cols)
    scale_two = 1.0 / math.sqrt(frames * (half_rows // 2) * (half_cols // 2))

    flat, own = video.reshape(48, 512), cotangent.reshape(256, 128)

    def swap(x, k):
        return lax.ppermute(x, "chan", [(i, i ^ k) for i in range(4)])

    inner, outer, flat, own = call(
        edges_kernel,
        [((80, 512), BF), ((80, 512), BF), ((48, 512), BF), ((256, 128), BF)],
        [((256, 128), F32)],
        1 << 20,
        flat, own,
    )
    inner = lax.ppermute(inner, "band", flip)
    outer = lax.ppermute(outer, "band", [(i, i + 1 - 2 * (i % 2 == 0)) for i in range(1, n - 1)])
    cols, rows, sel = call(
        matrix_kernel,
        [((512, 512), BF), ((3, 256, 128), BF), ((4, 128, 256), BF)],
        [],
        1 << 20,
    )
    w1 = weight_one[9:].reshape(2, 9, 12, 32).transpose(0, 2, 1, 3).reshape(2, 108, 32)
    w1 = jnp.pad(w1, ((0, 0), (0, 20), (0, 0)))
    (own,) = call(
        grown_kernel, [((512, 128), BF)], [], 1 << 20, own, inner, outer, sel, w1,
        far=(3, 4),
    )
    near = swap(own, 1)
    w2 = weight_two.reshape(3456, 256)
    xc, pre, win, own = call(
        forward_kernel,
        [((1152, 512), BF), ((128, 512), F32), ((256, 512), BF), ((512, 128), BF)],
        [((2, 256, 512), BF), ((4, 128, 128), F32)],
        1 << 30,
        inner, flat, outer, cols, rows, sel, w1, own,
    )
    far = swap(own, 3)
    (near_part,) = call(first_rows_kernel, [((256, 128), BF)], [], 1 << 10, near, xc, far=(1,))
    (far_part,) = call(last_rows_kernel, [((256, 128), BF)], [], 1 << 10, far)
    others = [near, far, swap(near_part, 3), swap(far_part, 1)]
    lat_keep, lat_send = call(
        latent_kernel, [((2, 64, 512), BF)] * 2, [((256, 512), BF)], 1 << 30, xc, w2
    )
    lat_got = swap(lat_send, 1)

    def second_grad(*refs):
        second_grad_kernel(*refs, scale=scale_two)

    cot, keep, send, lat_own, lat_send = call(
        second_grad,
        [
            ((256, 1024), BF), ((2304, 128), BF), ((2304, 128), BF),
            ((64, 512), F32), ((64, 512), BF),
        ],
        [((512, 128), F32)],
        1 << 30,
        xc, own, *others, lat_keep, lat_got,
    )
    lat_got = swap(lat_send, 3)
    got = lax.ppermute(send, "band", flip)

    def backward(*refs):
        backward_kernel(*refs, scale=scale_one)

    (g1,) = call(
        backward, [((64, 128), BF)], [((2, 128, 128), F32)], 1 << 30, cot, pre, win, w2, sel
    )
    (part,) = call(join_kernel, [((2368, 128), BF)], [], 1 << 20, keep, got, g1)
    half = n // 2
    groups = [[2 * i + c for i in range(half)] for c in range(2)]

    def exchange(x):
        x = x.reshape(half, 1184 // half, 2, 128)
        x = lax.all_to_all(x, "band", 0, 0, tiled=True, axis_index_groups=groups)
        return x.reshape(2368, 128)

    def share(*refs):
        share_kernel(*refs, count=half)

    part = exchange(part)
    mine, latent = call(
        share,
        [((2368, 128), BF), ((256, 128), BF)],
        [((256, 128), F32), ((2368 // half * min(half, 8), 128), F32)],
        1 << 20,
        part, lat_own, lat_got,
    )
    mine = exchange(mine)
    other = lax.ppermute(mine, "band", flip)
    g2, g1 = call(
        first_half_kernel,
        [((3, 1152, 256), F32), ((64, 128), BF)],
        [((1152, 256), F32), ((1152, 256), F32), pltpu.SemaphoreType.DMA((4,))],
        1 << 20,
        mine,
        far_out=(0,),
    )
    g2, g1 = call(
        other_half_kernel,
        [((3, 1152, 256), F32), ((12, 27, 32), F32)],
        [((1152, 256), F32), ((12, 27, 32), F32), pltpu.SemaphoreType.DMA((4,))],
        1 << 20,
        g2, g1, other,
        far=(0,), far_out=(0, 1), aliases={0: 0},
    )
    return latent.reshape(64, 2, 2, 128), jnp.transpose(g1, (1, 0, 2)), g2.reshape(27, 128, 256)


def solution(mesh):
    return jax.shard_map(
        on_device,
        mesh=mesh,
        in_specs=(
            P(None, None, "band", None),
            P(None, None, "chan"),
            P(None, "chan", None),
            P("chan", None, "band", None),
        ),
        out_specs=(P("chan", None, "band", None), P(None, None, "chan"), P(None, "chan", None)),
        check_vma=False,
    )
```

```python
import math

import jax
import jax.numpy as jnp
from jax import lax
from jax.experimental import pallas as pl
from jax.experimental.pallas import tpu as pltpu
from jax.sharding import PartitionSpec as P

BF = jnp.bfloat16
F32 = jnp.float32


def iota(shape, axis):
    return lax.broadcasted_iota(jnp.int32, shape, axis)


def matrix_kernel(col_ref, row_ref, sel_ref):
    u, w = iota((512, 128), 0), iota((512, 128), 1)
    for s in range(2):
        hit = ((u >> 2) == w) & (((u >> 1) & 1) == s)
        for t in range(2):
            value = 0.5 if t == 0 else jnp.where((u & 1) == 1, -0.5, 0.5)
            at = (s * 2 + t) * 128
            col_ref[:, at : at + 128] = jnp.where(hit, value, 0.0).astype(BF)
    at, lane = iota((256, 128), 0), iota((256, 128), 1)
    m, r, f, tb = at & 15, (at >> 4) & 3, (at >> 6) & 1, at >> 7
    wi = (m * 11) >> 5
    y = 4 * r + 2 * wi + tb + 2
    for part, (first, count) in enumerate(((2, 6), (8, 8), (16, 6))):
        hit = (lane == ((m - 3 * wi) * 2 + f) * count + y - first) & (m < 12)
        hit = hit & (y >= first) & (y < first + count)
        row_ref[part] = jnp.where(hit, 1.0, 0.0).astype(BF)
    at, lane = iota((128, 256), 0), iota((128, 256), 1)
    c = (at * 57) >> 9
    tap = at - 9 * c
    b = (tap * 11) >> 5
    e = tap - 3 * b
    target = ((c >> 1) & 1) * 128 + (e * 2 + (c & 1)) * 16 + b * 3 + (c >> 2)
    for p in range(4):
        hit = (lane == target + (p & 1) * 32 + (p >> 1) * 3) & (at < 108)
        sel_ref[p] = jnp.where(hit, 1.0, 0.0).astype(BF)


def dot(a, b, ca=1, cb=0):
    return lax.dot_general(a, b, (((ca,), (cb,)), ((), ())), preferred_element_type=F32)


def edges_kernel(
    video_ref, own_ref, outer_ref, inner_ref, video_out, own_out, rows, pixels, packed
):
    core = lax.axis_index("band") % 2
    video_out[...] = video_ref[...]
    own_out[...] = own_ref[...]
    rows[...] = own_ref[...].astype(F32)
    pixels[...] = video_ref[...].astype(F32)

    def put(ref, r):
        ref[:128, :] = rows[pl.ds(r, 128, stride=2), :].astype(BF)
        for g in range(6):
            for i in range(4):
                packed[i * 36 + g * 6 : i * 36 + g * 6 + 6, :] = pixels[
                    g * 8 + 2 * r : g * 8 + 2 * r + 6, i * 128 : i * 128 + 128
                ]
        ref[128:, :] = packed[...].astype(BF)

    @pl.when(core == 0)
    def _():
        put(inner_ref, 1)
        put(outer_ref, 0)

    @pl.when(core == 1)
    def _():
        put(inner_ref, 0)
        put(outer_ref, 1)


def grown_kernel(own_ref, outer_ref, inner_ref, _, __, out_ref):
    core = lax.axis_index("band") % 2
    out_ref[:256, :] = own_ref[...]
    for side, ref in ((1 - core, inner_ref), (core, outer_ref)):
        out_ref[pl.ds(pl.multiple_of(256 + side * 128, 128), 128), :] = ref[:128, :]


def shifted(x, step):
    lanes = x.shape[1]
    lane = lax.broadcasted_iota(jnp.int32, x.shape, 1) % 128
    if step == -1:
        return jnp.where(lane == 0, 0.0, pltpu.roll(x, 1, 1))
    return jnp.where(lane == 127, 0.0, pltpu.roll(x, lanes - 1, 1))


def forward_kernel(
    outer_ref, own_ref, inner_ref, col_ref, row_ref, sel_ref, w1_ref, cot_ref,
    xc_ref, pre_ref, win_ref, cot_out, one, two, packed,
):
    band = lax.axis_index("band")
    core = band % 2
    cot_out[...] = cot_ref[...]
    last = lax.axis_size("band") - 1
    beyond = []
    for ref in (inner_ref, outer_ref):
        packed[...] = ref[128:, :].astype(F32)
        beyond.append(jnp.concatenate([packed[k * 36 : k * 36 + 36, :] for k in range(4)], 1).astype(BF))
    v = (
        dot(row_ref[2 - 2 * core][:, :36], beyond[0])
        + dot(row_ref[1, :, :48], own_ref[...])
        + dot(row_ref[2 * core][:, :36], beyond[1])
    ).astype(BF)
    h = dot(v, col_ref[...])
    top, low = h[:128], h[128:]
    for pm, half in enumerate((top + low, top - low)):
        even, odd = half[:, :256], half[:, 256:]
        streams = (shifted(odd, -1), even, odd, shifted(even, 1))
        for st in range(8):
            part = streams[st // 2][:, (st % 2) * 128 : (st % 2) * 128 + 128].astype(BF)
            for f in range(2):
                for r in range(4):
                    at = (f * 4 + r) * 16
                    one[f, pm * 128 + st * 16 : pm * 128 + st * 16 + 16, r * 128 : r * 128 + 128] = part[
                        at : at + 16, :
                    ]
    w1a, w1b = (
        jnp.concatenate([dot(w1_ref[a], sel_ref[p], 0, 0) for p in range(4)], 0).astype(BF)
        for a in range(2)
    )
    pres = (dot(w1b, one[0]), dot(w1a, one[0]) + dot(w1b, one[1]))
    lane = lax.broadcasted_iota(jnp.int32, (32, 512), 1)
    keep = ((lane >= 128) | (band > 0)) & ((lane < 384) | (band < last))
    for f in range(2):
        pre = pres[f]
        pre_ref[:, f * 256 : f * 256 + 256] = pre[:, 128:384]
        win_ref[:, f * 256 : f * 256 + 256] = one[f, :, 128:384]
        act = pre * jax.nn.sigmoid(pre)
        p, q, r, s = act[:32], act[32:64], act[64:96], act[96:]
        pq, pmq, rs, rms = p + q, p - q, r + s, r - s
        parts = (pq + rs, pmq + rms, pq - rs, pmq - rms)
        for k in range(4):
            part = jnp.where(keep, parts[k] * 0.5, 0.0)
            for r in range(4):
                two[r, pl.ds(k, 32, stride=4), :] = part[:, r * 128 : r * 128 + 128]
        x = jnp.concatenate([two[r] for r in range(4)], 1)
        for e, xe in enumerate((shifted(x, -1), x, shifted(x, 1))):
            xe = xe.astype(BF)
            for b in range(3):
                at = (b * 3 + e) * 128
                xc_ref[at : at + 128, f * 256 : f * 256 + 256] = xe[:, b * 128 : b * 128 + 256]


def first_rows_kernel(in_ref, _, out_ref):
    out_ref[...] = in_ref[:256, :]


def last_rows_kernel(in_ref, out_ref):
    out_ref[...] = in_ref[256:, :]


def latent_kernel(xc_ref, w2_ref, keep_ref, send_ref, lat):
    out = dot(w2_ref[2304:, :], xc_ref[...], 0, 0)
    more = dot(w2_ref[1152:2304, :], xc_ref[:, :256], 0, 0)
    lat[:, :256] = out[:, :256].astype(BF)
    lat[:, 256:] = (out[:, 256:] + more).astype(BF)
    chan = lax.axis_index("chan")
    for ref, i, k in ((keep_ref, 0, 0), (send_ref, 0, 1), (send_ref, 1, 2), (keep_ref, 1, 3)):
        ref[i] = lat[pl.ds(pl.multiple_of((chan ^ k) * 64, 64), 64), :]


def second_grad_kernel(
    xc_ref, c0_ref, c1_ref, c3_ref, own2_ref, outer2_ref, lkeep_ref, lgot_ref,
    grown, keep_ref, send_ref, lown_ref, lsend_ref, rows, *, scale
):
    lown_ref[...] = lkeep_ref[0].astype(F32) + lgot_ref[0].astype(F32)
    lsend_ref[...] = (lkeep_ref[1].astype(F32) + lgot_ref[1].astype(F32)).astype(BF)
    chan = lax.axis_index("chan")
    core = lax.axis_index("band") % 2
    for k, ref in enumerate((c0_ref, c1_ref, None, c3_ref)):
        if ref is None:
            rows[:256, :] = own2_ref[...].astype(F32)
            rows[256:, :] = outer2_ref[...].astype(F32)
        else:
            rows[...] = ref[...].astype(F32)
        at = pl.multiple_of((chan ^ k) * 64, 64)
        for f in range(2):
            for r in range(2):
                lane = f * 512 + r * 128 + 128
                part = rows[pl.ds(f * 2 + r, 64, stride=4), :]
                grown[pl.ds(at, 64), lane : lane + 128] = part.astype(BF)
            for side in range(2):
                lane = f * 512 + side * 384
                part = rows[pl.ds(256 + side * 128 + f, 64, stride=2), :]
                grown[pl.ds(at, 64), lane : lane + 128] = part.astype(BF)

    def put(early_ref, late_ref):
        c1 = grown[:, 640:896]
        early = dot(xc_ref[:, :256], c1, 1, 1) * scale
        late = (dot(xc_ref[:, :256], grown[:, 128:384], 1, 1) + dot(xc_ref[:, 256:], c1, 1, 1)) * scale
        for ref, g in ((early_ref, early), (late_ref, late)):
            ref[:1152, :] = g[:, :128].astype(BF)
            ref[1152:, :] = g[:, 128:].astype(BF)

    @pl.when(core == 0)
    def _():
        put(keep_ref, send_ref)

    @pl.when(core == 1)
    def _():
        put(send_ref, keep_ref)


def backward_kernel(grown, pre_ref, win_ref, w2_ref, sel_ref, g1_ref, back_s, *, scale):
    z0 = z1 = 0.0
    for b in range(3):
        lo = (2 - b) * 128
        c0, c1 = grown[:, lo : lo + 256], grown[:, 512 + lo : 768 + lo]
        wa = w2_ref[1152 + b * 384 : 1536 + b * 384, :]
        wb = w2_ref[2304 + b * 384 : 2688 + b * 384, :]
        z0 = z0 + dot(wb, c0) + dot(wa, c1)
        z1 = z1 + dot(wb, c1)
    for f, z in enumerate((z0, z1)):
        z = z[128:256] + shifted(z[:128], 1) + shifted(z[256:], -1)
        back_s[0], back_s[1] = z[:, :128], z[:, 128:]
        a0, a1, a2, a3 = (
            jnp.concatenate([back_s[r, pl.ds(k, 32, stride=4), :] for r in range(2)], 1)
            for k in range(4)
        )
        s01, d01, s23, d23 = a0 + a1, a0 - a1, a2 + a3, a2 - a3
        act = jnp.concatenate([s01 + s23, d01 + d23, s01 - s23, d01 - d23], 0) * 0.5
        pre = pre_ref[:, f * 256 : f * 256 + 256]
        gate = jax.nn.sigmoid(pre)
        back = (act * gate * (1.0 + pre * (1.0 - gate))).astype(BF)
        if f == 0:
            late = dot(back, win_ref[:, :256], 1, 1)
        else:
            early = dot(back, win_ref[:, :256], 1, 1)
            late = late + dot(back, win_ref[:, 256:], 1, 1)
    for a, g in enumerate((early, late)):
        g = g * scale
        hi = g.astype(BF)
        lo = (g - hi.astype(F32)).astype(BF)
        total = 0.0
        for p in range(4):
            rows = slice(32 * p, 32 * p + 32)
            total = total + dot(hi[rows], sel_ref[p], 1, 1)
            total = total + dot(lo[rows], sel_ref[p], 1, 1)
        g1_ref[32 * a : 32 * a + 32, :] = total.astype(BF)


def join_kernel(keep_ref, got_ref, g1_ref, sum_ref):
    sum_ref[:2304, :] = (keep_ref[...].astype(F32) + got_ref[...].astype(F32)).astype(BF)
    sum_ref[2304:, :] = g1_ref[...]


def share_kernel(got_ref, lown_ref, lgot_ref, out_ref, lat_ref, rows, wide, *, count):
    lat = lown_ref[...] + lgot_ref[...].astype(F32)
    for i in range(4):
        rows[pl.ds(i, 64, stride=4), :] = lat[:, i * 128 : i * 128 + 128]
    lat_ref[...] = rows[...].astype(BF)
    size = got_ref.shape[0] // count
    bunch = 8 if count % 8 == 0 else count
    block = bunch * size
    total = got_ref[:block, :].astype(F32)
    for i in range(block, count * size, block):
        total = total + got_ref[i : i + block, :].astype(F32)
    wide[...] = total
    total = wide[:size, :]
    for i in range(1, bunch):
        total = total + wide[i * size : i * size + size, :]
    for i in range(bunch):
        wide[i * size : i * size + size, :] = total
    total = wide[...].astype(BF)
    for i in range(0, count * size, block):
        out_ref[i : i + block, :] = total


def widen(from_ref, wide, to_ref, sems, first):
    copies = []
    for i in range(3):
        at = i * 384
        wide[at : at + 384, :128] = from_ref[at : at + 384, :].astype(F32)
        wide[at : at + 384, 128:] = from_ref[1152 + at : 1536 + at, :].astype(F32)
        rows = pl.ds(at, 384)
        copies.append(pltpu.make_async_copy(wide.at[rows], to_ref.at[rows], sems.at[first + i]))
        copies[-1].start()
    return copies


def first_half_kernel(mine_ref, g2_ref, g1_ref, zero, own, sems):
    core = lax.axis_index("band") % 2
    zero[...] = jnp.zeros((1152, 256), F32)
    clear = pltpu.make_async_copy(zero, g2_ref.at[0], sems.at[0])
    clear.start()
    copies = [clear] + widen(mine_ref, own, g2_ref.at[1 + core], sems, 1)
    g1_ref[...] = mine_ref[2304:, :]
    for copy in copies:
        copy.wait()


def other_half_kernel(_, mine_ref, other_ref, g2_ref, g1_ref, half, taps_s, sems):
    core = lax.axis_index("band") % 2
    both = mine_ref[...].astype(F32) + other_ref[2304:2368, :].astype(F32)
    taps_s[...] = jnp.zeros((12, 27, 32), F32)
    for a in range(2):
        taps = jnp.transpose(both[32 * a : 32 * a + 32, :])
        for c in range(12):
            taps_s[c, 9 * a + 9 : 9 * a + 18, :] = taps[9 * c : 9 * c + 9, :]
    first = pltpu.make_async_copy(taps_s, g1_ref, sems.at[3])
    first.start()
    for copy in [first] + widen(other_ref, half, g2_ref.at[2 - core], sems, 0):
        copy.wait()


VMEM, HBM = pltpu.VMEM, pltpu.HBM


def call(kernel, outs, scratch, flops, *args, far=(), far_out=(), aliases=None):
    return pl.pallas_call(
        kernel,
        out_shape=[jax.ShapeDtypeStruct(*o) for o in outs],
        in_specs=[pl.BlockSpec(memory_space=HBM if i in far else VMEM) for i in range(len(args))],
        out_specs=[pl.BlockSpec(memory_space=HBM if i in far_out else VMEM) for i in range(len(outs))],
        scratch_shapes=[s if not isinstance(s, tuple) else pltpu.VMEM(*s) for s in scratch],
        input_output_aliases=aliases or {},
        compiler_params=pltpu.CompilerParams(vmem_limit_bytes=20 * 1024 * 1024),
        cost_estimate=pl.CostEstimate(flops=flops, bytes_accessed=1 << 20, transcendentals=0),
    )(*args)


def on_device(video, weight_one, weight_two, cotangent):
    n = lax.axis_size("band")
    flip = [(i, i ^ 1) for i in range(n)]
    frames, half_rows, half_cols = video.shape[1], n * 4, video.shape[3] // 2
    scale_one = 1.0 / math.sqrt(frames * half_rows * half_cols)
    scale_two = 1.0 / math.sqrt(frames * (half_rows // 2) * (half_cols // 2))

    flat, own = video.reshape(48, 512), cotangent.reshape(256, 128)

    def swap(x, k):
        return lax.ppermute(x, "chan", [(i, i ^ k) for i in range(4)])

    outer, inner, flat, own = call(
        edges_kernel,
        [((272, 128), BF), ((272, 128), BF), ((48, 512), BF), ((256, 128), BF)],
        [((256, 128), F32), ((48, 512), F32), ((144, 128), F32)],
        1 << 20,
        flat, own,
    )
    outer = lax.ppermute(outer, "band", [(i, i + 1 - 2 * (i % 2 == 0)) for i in range(1, n - 1)])
    inner = lax.ppermute(inner, "band", flip)
    cols, rows, sel = call(
        matrix_kernel,
        [((512, 512), BF), ((3, 256, 128), BF), ((4, 128, 256), BF)],
        [],
        1 << 20,
    )
    w1 = weight_one[9:].reshape(2, 9, 12, 32).transpose(0, 2, 1, 3).reshape(2, 108, 32)
    w1 = jnp.pad(w1, ((0, 0), (0, 20), (0, 0)))
    (own,) = call(
        grown_kernel, [((512, 128), BF)], [], 1 << 20, own, outer, inner, sel, w1,
        far=(3, 4),
    )
    near = swap(own, 1)
    w2 = weight_two.reshape(3456, 256)
    xc, pre, win, own = call(
        forward_kernel,
        [((1152, 512), BF), ((128, 512), F32), ((256, 512), BF), ((512, 128), BF)],
        [((2, 256, 512), BF), ((4, 128, 128), F32), ((144, 128), F32)],
        1 << 30,
        outer, flat, inner, cols, rows, sel, w1, own,
    )
    far = swap(own, 3)
    (near_part,) = call(first_rows_kernel, [((256, 128), BF)], [], 1 << 10, near, xc, far=(1,))
    (far_part,) = call(last_rows_kernel, [((256, 128), BF)], [], 1 << 10, far)
    others = [near, far, swap(near_part, 3), swap(far_part, 1)]
    lat_keep, lat_send = call(
        latent_kernel, [((2, 64, 512), BF)] * 2, [((256, 512), BF)], 1 << 30, xc, w2
    )
    lat_got = swap(lat_send, 1)

    def second_grad(*refs):
        second_grad_kernel(*refs, scale=scale_two)

    cot, keep, send, lat_own, lat_send = call(
        second_grad,
        [
            ((256, 1024), BF), ((2304, 128), BF), ((2304, 128), BF),
            ((64, 512), F32), ((64, 512), BF),
        ],
        [((512, 128), F32)],
        1 << 30,
        xc, own, *others, lat_keep, lat_got,
    )
    lat_got = swap(lat_send, 3)
    got = lax.ppermute(send, "band", flip)

    def backward(*refs):
        backward_kernel(*refs, scale=scale_one)

    (g1,) = call(
        backward, [((64, 128), BF)], [((2, 128, 128), F32)], 1 << 30, cot, pre, win, w2, sel
    )
    (part,) = call(join_kernel, [((2368, 128), BF)], [], 1 << 20, keep, got, g1)
    half = n // 2
    groups = [[2 * i + c for i in range(half)] for c in range(2)]

    def exchange(x):
        x = x.reshape(half, 1184 // half, 2, 128)
        x = lax.all_to_all(x, "band", 0, 0, tiled=True, axis_index_groups=groups)
        return x.reshape(2368, 128)

    def share(*refs):
        share_kernel(*refs, count=half)

    part = exchange(part)
    mine, latent = call(
        share,
        [((2368, 128), BF), ((256, 128), BF)],
        [((256, 128), F32), ((2368 // half * min(half, 8), 128), F32)],
        1 << 20,
        part, lat_own, lat_got,
    )
    mine = exchange(mine)
    other = lax.ppermute(mine, "band", flip)
    g2, g1 = call(
        first_half_kernel,
        [((3, 1152, 256), F32), ((64, 128), BF)],
        [((1152, 256), F32), ((1152, 256), F32), pltpu.SemaphoreType.DMA((4,))],
        1 << 20,
        mine,
        far_out=(0,),
    )
    g2, g1 = call(
        other_half_kernel,
        [((3, 1152, 256), F32), ((12, 27, 32), F32)],
        [((1152, 256), F32), ((12, 27, 32), F32), pltpu.SemaphoreType.DMA((4,))],
        1 << 20,
        g2, g1, other,
        far=(0,), far_out=(0, 1), aliases={0: 0},
    )
    return latent.reshape(64, 2, 2, 128), jnp.transpose(g1, (1, 0, 2)), g2.reshape(27, 128, 256)


def solution(mesh):
    return jax.shard_map(
        on_device,
        mesh=mesh,
        in_specs=(
            P(None, None, "band", None),
            P(None, None, "chan"),
            P(None, "chan", None),
            P("chan", None, "band", None),
        ),
        out_specs=(P("chan", None, "band", None), P(None, None, "chan"), P(None, "chan", None)),
        check_vma=False,
    )
```

```python
import math

import jax
import jax.numpy as jnp
from jax import lax
from jax.experimental import pallas as pl
from jax.experimental.pallas import tpu as pltpu
from jax.sharding import PartitionSpec as P

BF = jnp.bfloat16
F32 = jnp.float32


def iota(shape, axis):
    return lax.broadcasted_iota(jnp.int32, shape, axis)


def matrix_kernel(col_ref, row_ref, sel_ref):
    u, w = iota((512, 128), 0), iota((512, 128), 1)
    for s in range(2):
        hit = ((u >> 2) == w) & (((u >> 1) & 1) == s)
        for t in range(2):
            value = 0.5 if t == 0 else jnp.where((u & 1) == 1, -0.5, 0.5)
            at = (s * 2 + t) * 128
            col_ref[:, at : at + 128] = jnp.where(hit, value, 0.0).astype(BF)
    at, lane = iota((256, 128), 0), iota((256, 128), 1)
    m, r, f, tb = at & 15, (at >> 4) & 3, (at >> 6) & 1, at >> 7
    wi = (m * 11) >> 5
    y = 4 * r + 2 * wi + tb + 2
    for part, (first, count) in enumerate(((2, 6), (8, 8), (16, 6))):
        hit = (lane == ((m - 3 * wi) * 2 + f) * count + y - first) & (m < 12)
        hit = hit & (y >= first) & (y < first + count)
        row_ref[part] = jnp.where(hit, 1.0, 0.0).astype(BF)
    at, lane = iota((128, 256), 0), iota((128, 256), 1)
    c = (at * 57) >> 9
    tap = at - 9 * c
    b = (tap * 11) >> 5
    e = tap - 3 * b
    target = ((c >> 1) & 1) * 128 + (e * 2 + (c & 1)) * 16 + b * 3 + (c >> 2)
    for p in range(4):
        hit = (lane == target + (p & 1) * 32 + (p >> 1) * 3) & (at < 108)
        sel_ref[p] = jnp.where(hit, 1.0, 0.0).astype(BF)


def dot(a, b, ca=1, cb=0):
    return lax.dot_general(a, b, (((ca,), (cb,)), ((), ())), preferred_element_type=F32)


def edges_kernel(
    video_ref, own_ref, outer_ref, inner_ref, video_out, own_out, rows, pixels, packed
):
    core = lax.axis_index("band") % 2
    video_out[...] = video_ref[...]
    own_out[...] = own_ref[...]
    rows[...] = own_ref[...].astype(F32)
    pixels[:48, :] = video_ref[...].astype(F32)

    def put(ref, r):
        ref[:128, :] = rows[pl.ds(r, 128, stride=2), :].astype(BF)
        for g in range(6):
            for i in range(4):
                packed[i * 36 + g * 6 : i * 36 + g * 6 + 6, :] = pixels[
                    g * 8 + 2 * r : g * 8 + 2 * r + 6, i * 128 : i * 128 + 128
                ]
        ref[128:, :] = packed[:144, :].astype(BF)

    @pl.when(core == 0)
    def _():
        put(inner_ref, 1)
        put(outer_ref, 0)

    @pl.when(core == 1)
    def _():
        put(inner_ref, 0)
        put(outer_ref, 1)


def grown_kernel(own_ref, outer_ref, inner_ref, _, __, out_ref):
    core = lax.axis_index("band") % 2
    out_ref[:256, :] = own_ref[...]
    for side, ref in ((1 - core, inner_ref), (core, outer_ref)):
        out_ref[pl.ds(pl.multiple_of(256 + side * 128, 128), 128), :] = ref[:128, :]


def shifted(x, step):
    lanes = x.shape[1]
    lane = lax.broadcasted_iota(jnp.int32, x.shape, 1) % 128
    if step == -1:
        return jnp.where(lane == 0, 0.0, pltpu.roll(x, 1, 1))
    return jnp.where(lane == 127, 0.0, pltpu.roll(x, lanes - 1, 1))


def forward_kernel(
    outer_ref, own_ref, inner_ref, col_ref, row_ref, sel_ref, w1_ref, cot_ref,
    xc_ref, pre_ref, win_ref, cot_out, one, two, packed,
):
    band = lax.axis_index("band")
    core = band % 2
    cot_out[...] = cot_ref[...]
    last = lax.axis_size("band") - 1
    beyond = []
    for ref in (inner_ref, outer_ref):
        packed[:144, :] = ref[128:, :].astype(F32)
        beyond.append(jnp.concatenate([packed[k * 36 : k * 36 + 36, :] for k in range(4)], 1).astype(BF))
    v = (
        dot(row_ref[2 - 2 * core][:, :36], beyond[0])
        + dot(row_ref[1, :, :48], own_ref[...])
        + dot(row_ref[2 * core][:, :36], beyond[1])
    ).astype(BF)
    h = dot(v, col_ref[...])
    top, low = h[:128], h[128:]
    for pm, half in enumerate((top + low, top - low)):
        even, odd = half[:, :256], half[:, 256:]
        streams = (shifted(odd, -1), even, odd, shifted(even, 1))
        for st in range(8):
            part = streams[st // 2][:, (st % 2) * 128 : (st % 2) * 128 + 128].astype(BF)
            for f in range(2):
                for r in range(4):
                    at = (f * 4 + r) * 16
                    one[f, pm * 128 + st * 16 : pm * 128 + st * 16 + 16, r * 128 : r * 128 + 128] = part[
                        at : at + 16, :
                    ]
    w1a, w1b = (
        jnp.concatenate([dot(w1_ref[a], sel_ref[p], 0, 0) for p in range(4)], 0).astype(BF)
        for a in range(2)
    )
    pres = (dot(w1b, one[0]), dot(w1a, one[0]) + dot(w1b, one[1]))
    lane = lax.broadcasted_iota(jnp.int32, (32, 512), 1)
    keep = ((lane >= 128) | (band > 0)) & ((lane < 384) | (band < last))
    for f in range(2):
        pre = pres[f]
        pre_ref[:, f * 256 : f * 256 + 256] = pre[:, 128:384]
        win_ref[:, f * 256 : f * 256 + 256] = one[f, :, 128:384]
        act = pre * jax.nn.sigmoid(pre)
        p, q, r, s = act[:32], act[32:64], act[64:96], act[96:]
        pq, pmq, rs, rms = p + q, p - q, r + s, r - s
        parts = (pq + rs, pmq + rms, pq - rs, pmq - rms)
        for k in range(4):
            part = jnp.where(keep, parts[k] * 0.5, 0.0)
            for r in range(4):
                two[r, pl.ds(k, 32, stride=4), :] = part[:, r * 128 : r * 128 + 128]
        x = jnp.concatenate([two[r] for r in range(4)], 1)
        for e, xe in enumerate((shifted(x, -1), x, shifted(x, 1))):
            xe = xe.astype(BF)
            for b in range(3):
                at = (b * 3 + e) * 128
                xc_ref[at : at + 128, f * 256 : f * 256 + 256] = xe[:, b * 128 : b * 128 + 256]


def first_rows_kernel(in_ref, _, out_ref):
    out_ref[...] = in_ref[:256, :]


def last_rows_kernel(in_ref, out_ref):
    out_ref[...] = in_ref[256:, :]


def latent_kernel(xc_ref, w2_ref, keep_ref, send_ref, lat):
    out = dot(w2_ref[2304:, :], xc_ref[...], 0, 0)
    more = dot(w2_ref[1152:2304, :], xc_ref[:, :256], 0, 0)
    lat[:, :256] = out[:, :256].astype(BF)
    lat[:, 256:] = (out[:, 256:] + more).astype(BF)
    chan = lax.axis_index("chan")
    for ref, i, k in ((keep_ref, 0, 0), (send_ref, 0, 1), (send_ref, 1, 2), (keep_ref, 1, 3)):
        ref[i] = lat[pl.ds(pl.multiple_of((chan ^ k) * 64, 64), 64), :]


def second_grad_kernel(
    xc_ref, c0_ref, c1_ref, c3_ref, own2_ref, outer2_ref, lkeep_ref, lgot_ref,
    grown, keep_ref, send_ref, lown_ref, lsend_ref, rows, *, scale
):
    lown_ref[...] = lkeep_ref[0].astype(F32) + lgot_ref[0].astype(F32)
    lsend_ref[...] = (lkeep_ref[1].astype(F32) + lgot_ref[1].astype(F32)).astype(BF)
    chan = lax.axis_index("chan")
    core = lax.axis_index("band") % 2
    for k, ref in enumerate((c0_ref, c1_ref, None, c3_ref)):
        if ref is None:
            rows[:256, :] = own2_ref[...].astype(F32)
            rows[256:, :] = outer2_ref[...].astype(F32)
        else:
            rows[...] = ref[...].astype(F32)
        at = pl.multiple_of((chan ^ k) * 64, 64)
        for f in range(2):
            for r in range(2):
                lane = f * 512 + r * 128 + 128
                part = rows[pl.ds(f * 2 + r, 64, stride=4), :]
                grown[pl.ds(at, 64), lane : lane + 128] = part.astype(BF)
            for side in range(2):
                lane = f * 512 + side * 384
                part = rows[pl.ds(256 + side * 128 + f, 64, stride=2), :]
                grown[pl.ds(at, 64), lane : lane + 128] = part.astype(BF)

    def put(early_ref, late_ref):
        c1 = grown[:, 640:896]
        early = dot(xc_ref[:, :256], c1, 1, 1) * scale
        late = (dot(xc_ref[:, :256], grown[:, 128:384], 1, 1) + dot(xc_ref[:, 256:], c1, 1, 1)) * scale
        for ref, g in ((early_ref, early), (late_ref, late)):
            ref[:1152, :] = g[:, :128].astype(BF)
            ref[1152:, :] = g[:, 128:].astype(BF)

    @pl.when(core == 0)
    def _():
        put(keep_ref, send_ref)

    @pl.when(core == 1)
    def _():
        put(send_ref, keep_ref)


def backward_kernel(grown, pre_ref, win_ref, w2_ref, sel_ref, g1_ref, back_s, *, scale):
    z0 = z1 = 0.0
    for b in range(3):
        lo = (2 - b) * 128
        c0, c1 = grown[:, lo : lo + 256], grown[:, 512 + lo : 768 + lo]
        wa = w2_ref[1152 + b * 384 : 1536 + b * 384, :]
        wb = w2_ref[2304 + b * 384 : 2688 + b * 384, :]
        z0 = z0 + dot(wb, c0) + dot(wa, c1)
        z1 = z1 + dot(wb, c1)
    for f, z in enumerate((z0, z1)):
        z = z[128:256] + shifted(z[:128], 1) + shifted(z[256:], -1)
        back_s[0], back_s[1] = z[:, :128], z[:, 128:]
        a0, a1, a2, a3 = (
            jnp.concatenate([back_s[r, pl.ds(k, 32, stride=4), :] for r in range(2)], 1)
            for k in range(4)
        )
        s01, d01, s23, d23 = a0 + a1, a0 - a1, a2 + a3, a2 - a3
        act = jnp.concatenate([s01 + s23, d01 + d23, s01 - s23, d01 - d23], 0) * 0.5
        pre = pre_ref[:, f * 256 : f * 256 + 256]
        gate = jax.nn.sigmoid(pre)
        back = (act * gate * (1.0 + pre * (1.0 - gate))).astype(BF)
        if f == 0:
            late = dot(back, win_ref[:, :256], 1, 1)
        else:
            early = dot(back, win_ref[:, :256], 1, 1)
            late = late + dot(back, win_ref[:, 256:], 1, 1)
    for a, g in enumerate((early, late)):
        g = g * scale
        hi = g.astype(BF)
        lo = (g - hi.astype(F32)).astype(BF)
        total = 0.0
        for p in range(4):
            rows = slice(32 * p, 32 * p + 32)
            total = total + dot(hi[rows], sel_ref[p], 1, 1)
            total = total + dot(lo[rows], sel_ref[p], 1, 1)
        g1_ref[32 * a : 32 * a + 32, :] = total.astype(BF)


def join_kernel(keep_ref, got_ref, g1_ref, sum_ref):
    sum_ref[:2304, :] = (keep_ref[...].astype(F32) + got_ref[...].astype(F32)).astype(BF)
    sum_ref[2304:, :] = g1_ref[...]


def share_kernel(got_ref, lown_ref, lgot_ref, out_ref, lat_ref, rows, wide, *, count):
    lat = lown_ref[...] + lgot_ref[...].astype(F32)
    for i in range(4):
        rows[pl.ds(i, 64, stride=4), :] = lat[:, i * 128 : i * 128 + 128]
    lat_ref[...] = rows[...].astype(BF)
    size = got_ref.shape[0] // count
    bunch = 8 if count % 8 == 0 else count
    block = bunch * size
    total = got_ref[:block, :].astype(F32)
    for i in range(block, count * size, block):
        total = total + got_ref[i : i + block, :].astype(F32)
    wide[:block, :] = total
    total = wide[:size, :]
    for i in range(1, bunch):
        total = total + wide[i * size : i * size + size, :]
    for i in range(bunch):
        wide[i * size : i * size + size, :] = total
    total = wide[:block, :].astype(BF)
    for i in range(0, count * size, block):
        out_ref[i : i + block, :] = total


def widen(from_ref, wide, to_ref, sems, first):
    copies = []
    for i in range(3):
        at = i * 384
        wide[at : at + 384, :128] = from_ref[at : at + 384, :].astype(F32)
        wide[at : at + 384, 128:] = from_ref[1152 + at : 1536 + at, :].astype(F32)
        rows = pl.ds(at, 384)
        copies.append(pltpu.make_async_copy(wide.at[rows], to_ref.at[rows], sems.at[first + i]))
        copies[-1].start()
    return copies


def first_half_kernel(mine_ref, g2_ref, g1_ref, zero, own, sems):
    core = lax.axis_index("band") % 2
    zero[...] = jnp.zeros((1152, 256), F32)
    clear = pltpu.make_async_copy(zero, g2_ref.at[0], sems.at[0])
    clear.start()
    copies = [clear] + widen(mine_ref, own, g2_ref.at[1 + core], sems, 1)
    g1_ref[...] = mine_ref[2304:, :]
    for copy in copies:
        copy.wait()


def other_half_kernel(_, mine_ref, other_ref, g2_ref, g1_ref, half, taps_s, stage, sems):
    core = lax.axis_index("band") % 2
    both = mine_ref[...].astype(F32) + other_ref[2304:2368, :].astype(F32)
    taps = [jnp.transpose(both[32 * a : 32 * a + 32, :]) for a in range(2)]
    stage[...] = jnp.zeros((12, 48, 32), F32)
    for c in range(12):
        for a in range(2):
            stage[c, 9 * a + 9 : 9 * a + 18, :] = taps[a][9 * c : 9 * c + 9, :]
    for c in range(12):
        taps_s[c] = stage[c, :27, :]
    first = pltpu.make_async_copy(taps_s, g1_ref, sems.at[3])
    first.start()
    for copy in [first] + widen(other_ref, half, g2_ref.at[2 - core], sems, 0):
        copy.wait()


VMEM, HBM = pltpu.VMEM, pltpu.HBM


def call(kernel, outs, scratch, flops, *args, far=(), far_out=(), aliases=None):
    return pl.pallas_call(
        kernel,
        out_shape=[jax.ShapeDtypeStruct(*o) for o in outs],
        in_specs=[pl.BlockSpec(memory_space=HBM if i in far else VMEM) for i in range(len(args))],
        out_specs=[pl.BlockSpec(memory_space=HBM if i in far_out else VMEM) for i in range(len(outs))],
        scratch_shapes=[s if not isinstance(s, tuple) else pltpu.VMEM(*s) for s in scratch],
        input_output_aliases=aliases or {},
        compiler_params=pltpu.CompilerParams(vmem_limit_bytes=20 * 1024 * 1024),
        cost_estimate=pl.CostEstimate(flops=flops, bytes_accessed=1 << 20, transcendentals=0),
    )(*args)


def on_device(video, weight_one, weight_two, cotangent):
    n = lax.axis_size("band")
    flip = [(i, i ^ 1) for i in range(n)]
    frames, half_rows, half_cols = video.shape[1], n * 4, video.shape[3] // 2
    scale_one = 1.0 / math.sqrt(frames * half_rows * half_cols)
    scale_two = 1.0 / math.sqrt(frames * (half_rows // 2) * (half_cols // 2))

    flat, own = video.reshape(48, 512), cotangent.reshape(256, 128)

    def swap(x, k):
        return lax.ppermute(x, "chan", [(i, i ^ k) for i in range(4)])

    outer, inner, flat, own = call(
        edges_kernel,
        [((272, 128), BF), ((272, 128), BF), ((48, 512), BF), ((256, 128), BF)],
        [((256, 128), F32), ((64, 512), F32), ((160, 128), F32)],
        1 << 20,
        flat, own,
    )
    outer = lax.ppermute(outer, "band", [(i, i + 1 - 2 * (i % 2 == 0)) for i in range(1, n - 1)])
    inner = lax.ppermute(inner, "band", flip)
    cols, rows, sel = call(
        matrix_kernel,
        [((512, 512), BF), ((3, 256, 128), BF), ((4, 128, 256), BF)],
        [],
        1 << 20,
    )
    w1 = weight_one[9:].reshape(2, 9, 12, 32).transpose(0, 2, 1, 3).reshape(2, 108, 32)
    w1 = jnp.pad(w1, ((0, 0), (0, 20), (0, 0)))
    (own,) = call(
        grown_kernel, [((512, 128), BF)], [], 1 << 20, own, outer, inner, sel, w1,
        far=(3, 4),
    )
    near = swap(own, 1)
    w2 = weight_two.reshape(3456, 256)
    xc, pre, win, own = call(
        forward_kernel,
        [((1152, 512), BF), ((128, 512), F32), ((256, 512), BF), ((512, 128), BF)],
        [((2, 256, 512), BF), ((4, 128, 128), F32), ((160, 128), F32)],
        1 << 30,
        outer, flat, inner, cols, rows, sel, w1, own,
    )
    far = swap(own, 3)
    (near_part,) = call(first_rows_kernel, [((256, 128), BF)], [], 1 << 10, near, xc, far=(1,))
    (far_part,) = call(last_rows_kernel, [((256, 128), BF)], [], 1 << 10, far)
    others = [near, far, swap(near_part, 3), swap(far_part, 1)]
    lat_keep, lat_send = call(
        latent_kernel, [((2, 64, 512), BF)] * 2, [((256, 512), BF)], 1 << 30, xc, w2
    )
    lat_got = swap(lat_send, 1)

    def second_grad(*refs):
        second_grad_kernel(*refs, scale=scale_two)

    cot, keep, send, lat_own, lat_send = call(
        second_grad,
        [
            ((256, 1024), BF), ((2304, 128), BF), ((2304, 128), BF),
            ((64, 512), F32), ((64, 512), BF),
        ],
        [((512, 128), F32)],
        1 << 30,
        xc, own, *others, lat_keep, lat_got,
    )
    lat_got = swap(lat_send, 3)
    got = lax.ppermute(send, "band", flip)

    def backward(*refs):
        backward_kernel(*refs, scale=scale_one)

    (g1,) = call(
        backward, [((64, 128), BF)], [((2, 128, 128), F32)], 1 << 30, cot, pre, win, w2, sel
    )
    (part,) = call(join_kernel, [((2368, 128), BF)], [], 1 << 20, keep, got, g1)
    half = n // 2
    groups = [[2 * i + c for i in range(half)] for c in range(2)]

    def exchange(x):
        x = x.reshape(half, 1184 // half, 2, 128)
        x = lax.all_to_all(x, "band", 0, 0, tiled=True, axis_index_groups=groups)
        return x.reshape(2368, 128)

    def share(*refs):
        share_kernel(*refs, count=half)

    part = exchange(part)
    mine, latent = call(
        share,
        [((2368, 128), BF), ((256, 128), BF)],
        [((256, 128), F32), ((2368 // half * min(half, 8) + 16, 128), F32)],
        1 << 20,
        part, lat_own, lat_got,
    )
    mine = exchange(mine)
    other = lax.ppermute(mine, "band", flip)
    g2, g1 = call(
        first_half_kernel,
        [((3, 1152, 256), F32), ((64, 128), BF)],
        [((1152, 256), F32), ((1152, 256), F32), pltpu.SemaphoreType.DMA((4,))],
        1 << 20,
        mine,
        far_out=(0,),
    )
    g2, g1 = call(
        other_half_kernel,
        [((3, 1152, 256), F32), ((12, 27, 32), F32)],
        [((1152, 256), F32), ((12, 27, 32), F32), ((12, 48, 32), F32), pltpu.SemaphoreType.DMA((4,))],
        1 << 20,
        g2, g1, other,
        far=(0,), far_out=(0, 1), aliases={0: 0},
    )
    return latent.reshape(64, 2, 2, 128), jnp.transpose(g1, (1, 0, 2)), g2.reshape(27, 128, 256)


def solution(mesh):
    return jax.shard_map(
        on_device,
        mesh=mesh,
        in_specs=(
            P(None, None, "band", None),
            P(None, None, "chan"),
            P(None, "chan", None),
            P("chan", None, "band", None),
        ),
        out_specs=(P("chan", None, "band", None), P(None, None, "chan"), P(None, "chan", None)),
        check_vma=False,
    )
```

```python
import math

import jax
import jax.numpy as jnp
from jax import lax
from jax.experimental import pallas as pl
from jax.experimental.pallas import tpu as pltpu
from jax.sharding import PartitionSpec as P

BF = jnp.bfloat16
F32 = jnp.float32


def iota(shape, axis):
    return lax.broadcasted_iota(jnp.int32, shape, axis)


def matrix_kernel(col_ref, row_ref, sel_ref):
    u, w = iota((512, 128), 0), iota((512, 128), 1)
    for s in range(2):
        hit = ((u >> 2) == w) & (((u >> 1) & 1) == s)
        for t in range(2):
            value = 0.5 if t == 0 else jnp.where((u & 1) == 1, -0.5, 0.5)
            at = (s * 2 + t) * 128
            col_ref[:, at : at + 128] = jnp.where(hit, value, 0.0).astype(BF)
    at, lane = iota((256, 128), 0), iota((256, 128), 1)
    m, r, f, tb = at & 15, (at >> 4) & 3, (at >> 6) & 1, at >> 7
    wi = (m * 11) >> 5
    y = 4 * r + 2 * wi + tb + 2
    for part, (first, count) in enumerate(((2, 6), (8, 8), (16, 6))):
        hit = (lane == ((m - 3 * wi) * 2 + f) * count + y - first) & (m < 12)
        hit = hit & (y >= first) & (y < first + count)
        row_ref[part] = jnp.where(hit, 1.0, 0.0).astype(BF)
    at, lane = iota((128, 256), 0), iota((128, 256), 1)
    c = (at * 57) >> 9
    tap = at - 9 * c
    b = (tap * 11) >> 5
    e = tap - 3 * b
    target = ((c >> 1) & 1) * 128 + (e * 2 + (c & 1)) * 16 + b * 3 + (c >> 2)
    for p in range(4):
        hit = (lane == target + (p & 1) * 32 + (p >> 1) * 3) & (at < 108)
        sel_ref[p] = jnp.where(hit, 1.0, 0.0).astype(BF)


def dot(a, b, ca=1, cb=0):
    return lax.dot_general(a, b, (((ca,), (cb,)), ((), ())), preferred_element_type=F32)


def edges_kernel(
    both_ref, outer_ref, inner_ref, video_out, own_out, rows, pixels, packed
):
    core = lax.axis_index("band") % 2
    video_out[...] = both_ref[:48, 128:]
    own_out[...] = both_ref[:, :128]
    rows[...] = both_ref[:, :128].astype(F32)
    pixels[:48, :] = both_ref[:48, 128:].astype(F32)

    def put(ref, r):
        ref[:128, :] = rows[pl.ds(r, 128, stride=2), :].astype(BF)
        for g in range(6):
            for i in range(4):
                packed[i * 36 + g * 6 : i * 36 + g * 6 + 6, :] = pixels[
                    g * 8 + 2 * r : g * 8 + 2 * r + 6, i * 128 : i * 128 + 128
                ]
        ref[128:, :] = packed[:144, :].astype(BF)

    @pl.when(core == 0)
    def _():
        put(inner_ref, 1)
        put(outer_ref, 0)

    @pl.when(core == 1)
    def _():
        put(inner_ref, 0)
        put(outer_ref, 1)


def grown_kernel(own_ref, outer_ref, inner_ref, _, __, out_ref):
    core = lax.axis_index("band") % 2
    out_ref[:256, :] = own_ref[...]
    for side, ref in ((1 - core, inner_ref), (core, outer_ref)):
        out_ref[pl.ds(pl.multiple_of(256 + side * 128, 128), 128), :] = ref[:128, :]


def shifted(x, step):
    lanes = x.shape[1]
    lane = lax.broadcasted_iota(jnp.int32, x.shape, 1) % 128
    if step == -1:
        return jnp.where(lane == 0, 0.0, pltpu.roll(x, 1, 1))
    return jnp.where(lane == 127, 0.0, pltpu.roll(x, lanes - 1, 1))


def forward_kernel(
    outer_ref, own_ref, inner_ref, col_ref, row_ref, sel_ref, w1_ref, cot_ref,
    xc_ref, pre_ref, win_ref, cot_out, one, two, packed,
):
    band = lax.axis_index("band")
    core = band % 2
    cot_out[...] = cot_ref[...]
    last = lax.axis_size("band") - 1
    beyond = []
    for ref in (inner_ref, outer_ref):
        packed[:144, :] = ref[128:, :].astype(F32)
        beyond.append(jnp.concatenate([packed[k * 36 : k * 36 + 36, :] for k in range(4)], 1).astype(BF))
    v = (
        dot(row_ref[2 - 2 * core][:, :36], beyond[0])
        + dot(row_ref[1, :, :48], own_ref[...])
        + dot(row_ref[2 * core][:, :36], beyond[1])
    ).astype(BF)
    h = dot(v, col_ref[...])
    top, low = h[:128], h[128:]
    for pm, half in enumerate((top + low, top - low)):
        even, odd = half[:, :256], half[:, 256:]
        streams = (shifted(odd, -1), even, odd, shifted(even, 1))
        for st in range(8):
            part = streams[st // 2][:, (st % 2) * 128 : (st % 2) * 128 + 128].astype(BF)
            for f in range(2):
                for r in range(4):
                    at = (f * 4 + r) * 16
                    one[f, pm * 128 + st * 16 : pm * 128 + st * 16 + 16, r * 128 : r * 128 + 128] = part[
                        at : at + 16, :
                    ]
    w1a, w1b = (
        jnp.concatenate([dot(w1_ref[a], sel_ref[p], 0, 0) for p in range(4)], 0).astype(BF)
        for a in range(2)
    )
    pres = (dot(w1b, one[0]), dot(w1a, one[0]) + dot(w1b, one[1]))
    lane = lax.broadcasted_iota(jnp.int32, (32, 512), 1)
    keep = ((lane >= 128) | (band > 0)) & ((lane < 384) | (band < last))
    for f in range(2):
        pre = pres[f]
        pre_ref[:, f * 256 : f * 256 + 256] = pre[:, 128:384]
        win_ref[:, f * 256 : f * 256 + 256] = one[f, :, 128:384]
        act = pre * jax.nn.sigmoid(pre)
        p, q, r, s = act[:32], act[32:64], act[64:96], act[96:]
        pq, pmq, rs, rms = p + q, p - q, r + s, r - s
        parts = (pq + rs, pmq + rms, pq - rs, pmq - rms)
        for k in range(4):
            part = jnp.where(keep, parts[k] * 0.5, 0.0)
            for r in range(4):
                two[r, pl.ds(k, 32, stride=4), :] = part[:, r * 128 : r * 128 + 128]
        x = jnp.concatenate([two[r] for r in range(4)], 1)
        for e, xe in enumerate((shifted(x, -1), x, shifted(x, 1))):
            xe = xe.astype(BF)
            for b in range(3):
                at = (b * 3 + e) * 128
                xc_ref[at : at + 128, f * 256 : f * 256 + 256] = xe[:, b * 128 : b * 128 + 256]


def first_rows_kernel(in_ref, _, out_ref):
    out_ref[...] = in_ref[:256, :]


def last_rows_kernel(in_ref, out_ref):
    out_ref[...] = in_ref[256:, :]


def latent_kernel(xc_ref, w2_ref, keep_ref, send_ref, lat):
    out = dot(w2_ref[2304:, :], xc_ref[...], 0, 0)
    more = dot(w2_ref[1152:2304, :], xc_ref[:, :256], 0, 0)
    lat[:, :256] = out[:, :256].astype(BF)
    lat[:, 256:] = (out[:, 256:] + more).astype(BF)
    chan = lax.axis_index("chan")
    for ref, i, k in ((keep_ref, 0, 0), (send_ref, 0, 1), (send_ref, 1, 2), (keep_ref, 1, 3)):
        ref[i] = lat[pl.ds(pl.multiple_of((chan ^ k) * 64, 64), 64), :]


def second_grad_kernel(
    xc_ref, c0_ref, c1_ref, c3_ref, own2_ref, outer2_ref, lkeep_ref, lgot_ref,
    grown, send_ref, lown_ref, lsend_ref, rows, *, scale
):
    lown_ref[...] = lkeep_ref[0].astype(F32) + lgot_ref[0].astype(F32)
    lsend_ref[...] = (lkeep_ref[1].astype(F32) + lgot_ref[1].astype(F32)).astype(BF)
    chan = lax.axis_index("chan")
    core = lax.axis_index("band") % 2
    for k, ref in enumerate((c0_ref, c1_ref, None, c3_ref)):
        if ref is None:
            rows[:256, :] = own2_ref[...].astype(F32)
            rows[256:, :] = outer2_ref[...].astype(F32)
        else:
            rows[...] = ref[...].astype(F32)
        at = pl.multiple_of((chan ^ k) * 64, 64)
        for f in range(2):
            for r in range(2):
                lane = f * 512 + r * 128 + 128
                part = rows[pl.ds(f * 2 + r, 64, stride=4), :]
                grown[pl.ds(at, 64), lane : lane + 128] = part.astype(BF)
            for side in range(2):
                lane = f * 512 + side * 384
                part = rows[pl.ds(256 + side * 128 + f, 64, stride=2), :]
                grown[pl.ds(at, 64), lane : lane + 128] = part.astype(BF)

    half_gradient(xc_ref, grown, send_ref, 1 - core, scale)


def half_gradient(xc_ref, grown, out_ref, half, scale):
    def put(g):
        g = g * scale
        out_ref[:1152, :] = g[:, :128].astype(BF)
        out_ref[1152:, :] = g[:, 128:].astype(BF)

    @pl.when(half == 0)
    def _():
        put(dot(xc_ref[:, :256], grown[:, 640:896], 1, 1))

    @pl.when(half == 1)
    def _():
        put(dot(xc_ref[:, :256], grown[:, 128:384], 1, 1) + dot(xc_ref[:, 256:], grown[:, 640:896], 1, 1))


def kept_kernel(xc_ref, grown, keep_ref, *, scale):
    half_gradient(xc_ref, grown, keep_ref, lax.axis_index("band") % 2, scale)


def backward_kernel(grown, pre_ref, win_ref, w2_ref, sel_ref, g1_ref, back_s, *, scale):
    z0 = z1 = 0.0
    for b in range(3):
        lo = (2 - b) * 128
        c0, c1 = grown[:, lo : lo + 256], grown[:, 512 + lo : 768 + lo]
        wa = w2_ref[1152 + b * 384 : 1536 + b * 384, :]
        wb = w2_ref[2304 + b * 384 : 2688 + b * 384, :]
        z0 = z0 + dot(wb, c0) + dot(wa, c1)
        z1 = z1 + dot(wb, c1)
    for f, z in enumerate((z0, z1)):
        z = z[128:256] + shifted(z[:128], 1) + shifted(z[256:], -1)
        back_s[0], back_s[1] = z[:, :128], z[:, 128:]
        a0, a1, a2, a3 = (
            jnp.concatenate([back_s[r, pl.ds(k, 32, stride=4), :] for r in range(2)], 1)
            for k in range(4)
        )
        s01, d01, s23, d23 = a0 + a1, a0 - a1, a2 + a3, a2 - a3
        act = jnp.concatenate([s01 + s23, d01 + d23, s01 - s23, d01 - d23], 0) * 0.5
        pre = pre_ref[:, f * 256 : f * 256 + 256]
        gate = jax.nn.sigmoid(pre)
        back = (act * gate * (1.0 + pre * (1.0 - gate))).astype(BF)
        if f == 0:
            late = dot(back, win_ref[:, :256], 1, 1)
        else:
            early = dot(back, win_ref[:, :256], 1, 1)
            late = late + dot(back, win_ref[:, 256:], 1, 1)
    for a, g in enumerate((early, late)):
        g = g * scale
        hi = g.astype(BF)
        lo = (g - hi.astype(F32)).astype(BF)
        total = 0.0
        for p in range(4):
            rows = slice(32 * p, 32 * p + 32)
            total = total + dot(hi[rows], sel_ref[p], 1, 1)
            total = total + dot(lo[rows], sel_ref[p], 1, 1)
        g1_ref[32 * a : 32 * a + 32, :] = total.astype(BF)


def join_kernel(keep_ref, got_ref, g1_ref, sum_ref):
    sum_ref[:2304, :] = (keep_ref[...].astype(F32) + got_ref[...].astype(F32)).astype(BF)
    sum_ref[2304:, :] = g1_ref[...]


def share_kernel(got_ref, lown_ref, lgot_ref, out_ref, lat_ref, rows, wide, *, count):
    lat = lown_ref[...] + lgot_ref[...].astype(F32)
    for i in range(4):
        rows[pl.ds(i, 64, stride=4), :] = lat[:, i * 128 : i * 128 + 128]
    lat_ref[...] = rows[...].astype(BF)
    size = got_ref.shape[0] // count
    bunch = 8 if count % 8 == 0 else count
    block = bunch * size
    total = got_ref[:block, :].astype(F32)
    for i in range(block, count * size, block):
        total = total + got_ref[i : i + block, :].astype(F32)
    wide[:block, :] = total
    total = wide[:size, :]
    for i in range(1, bunch):
        total = total + wide[i * size : i * size + size, :]
    for i in range(bunch):
        wide[i * size : i * size + size, :] = total
    total = wide[:block, :].astype(BF)
    for i in range(0, count * size, block):
        out_ref[i : i + block, :] = total


def widen(from_ref, wide, to_ref, sems, first):
    copies = []
    for i in range(3):
        at = i * 384
        wide[at : at + 384, :128] = from_ref[at : at + 384, :].astype(F32)
        wide[at : at + 384, 128:] = from_ref[1152 + at : 1536 + at, :].astype(F32)
        rows = pl.ds(at, 384)
        copies.append(pltpu.make_async_copy(wide.at[rows], to_ref.at[rows], sems.at[first + i]))
        copies[-1].start()
    return copies


def first_half_kernel(mine_ref, g2_ref, g1_ref, zero, own, sems):
    core = lax.axis_index("band") % 2
    zero[...] = jnp.zeros((1152, 256), F32)
    clear = pltpu.make_async_copy(zero, g2_ref.at[0], sems.at[0])
    clear.start()
    copies = [clear] + widen(mine_ref, own, g2_ref.at[1 + core], sems, 1)
    g1_ref[...] = mine_ref[2304:, :]
    for copy in copies:
        copy.wait()


def other_half_kernel(_, mine_ref, other_ref, g2_ref, g1_ref, half, taps_s, stage, sems):
    core = lax.axis_index("band") % 2
    both = mine_ref[...].astype(F32) + other_ref[2304:2368, :].astype(F32)
    taps = [jnp.transpose(both[32 * a : 32 * a + 32, :]) for a in range(2)]
    stage[...] = jnp.zeros((12, 48, 32), F32)
    for c in range(12):
        for a in range(2):
            stage[c, 9 * a + 9 : 9 * a + 18, :] = taps[a][9 * c : 9 * c + 9, :]
    for c in range(12):
        taps_s[c] = stage[c, :27, :]
    first = pltpu.make_async_copy(taps_s, g1_ref, sems.at[3])
    first.start()
    for copy in [first] + widen(other_ref, half, g2_ref.at[2 - core], sems, 0):
        copy.wait()


VMEM, HBM = pltpu.VMEM, pltpu.HBM


def call(kernel, outs, scratch, flops, *args, far=(), far_out=(), aliases=None):
    return pl.pallas_call(
        kernel,
        out_shape=[jax.ShapeDtypeStruct(*o) for o in outs],
        in_specs=[pl.BlockSpec(memory_space=HBM if i in far else VMEM) for i in range(len(args))],
        out_specs=[pl.BlockSpec(memory_space=HBM if i in far_out else VMEM) for i in range(len(outs))],
        scratch_shapes=[s if not isinstance(s, tuple) else pltpu.VMEM(*s) for s in scratch],
        input_output_aliases=aliases or {},
        compiler_params=pltpu.CompilerParams(vmem_limit_bytes=20 * 1024 * 1024),
        cost_estimate=pl.CostEstimate(flops=flops, bytes_accessed=1 << 20, transcendentals=0),
    )(*args)


def on_device(video, weight_one, weight_two, cotangent):
    n = lax.axis_size("band")
    flip = [(i, i ^ 1) for i in range(n)]
    frames, half_rows, half_cols = video.shape[1], n * 4, video.shape[3] // 2
    scale_one = 1.0 / math.sqrt(frames * half_rows * half_cols)
    scale_two = 1.0 / math.sqrt(frames * (half_rows // 2) * (half_cols // 2))

    flat, own = video.reshape(48, 512), cotangent.reshape(256, 128)

    def swap(x, k):
        return lax.ppermute(x, "chan", [(i, i ^ k) for i in range(4)])

    outer, inner, flat, own = call(
        edges_kernel,
        [((272, 128), BF), ((272, 128), BF), ((48, 512), BF), ((256, 128), BF)],
        [((256, 128), F32), ((64, 512), F32), ((160, 128), F32)],
        1 << 20,
        jnp.concatenate([own, jnp.pad(flat, ((0, 208), (0, 0)))], 1),
    )
    outer = lax.ppermute(outer, "band", [(i, i + 1 - 2 * (i % 2 == 0)) for i in range(1, n - 1)])
    inner = lax.ppermute(inner, "band", flip)
    cols, rows, sel = call(
        matrix_kernel,
        [((512, 512), BF), ((3, 256, 128), BF), ((4, 128, 256), BF)],
        [],
        1 << 20,
    )
    w1 = weight_one[9:].reshape(2, 9, 12, 32).transpose(0, 2, 1, 3).reshape(2, 108, 32)
    w1 = jnp.pad(w1, ((0, 0), (0, 20), (0, 0)))
    (own,) = call(
        grown_kernel, [((512, 128), BF)], [], 1 << 20, own, outer, inner, sel, w1,
        far=(3, 4),
    )
    near = swap(own, 1)
    w2 = weight_two.reshape(3456, 256)
    xc, pre, win, own = call(
        forward_kernel,
        [((1152, 512), BF), ((128, 512), F32), ((256, 512), BF), ((512, 128), BF)],
        [((2, 256, 512), BF), ((4, 128, 128), F32), ((160, 128), F32)],
        1 << 30,
        outer, flat, inner, cols, rows, sel, w1, own,
    )
    far = swap(own, 3)
    (near_part,) = call(first_rows_kernel, [((256, 128), BF)], [], 1 << 10, near, xc, far=(1,))
    (far_part,) = call(last_rows_kernel, [((256, 128), BF)], [], 1 << 10, far)
    others = [near, far, swap(near_part, 3), swap(far_part, 1)]
    lat_keep, lat_send = call(
        latent_kernel, [((2, 64, 512), BF)] * 2, [((256, 512), BF)], 1 << 30, xc, w2
    )
    lat_got = swap(lat_send, 1)

    def second_grad(*refs):
        second_grad_kernel(*refs, scale=scale_two)

    cot, send, lat_own, lat_send = call(
        second_grad,
        [
            ((256, 1024), BF), ((2304, 128), BF),
            ((64, 512), F32), ((64, 512), BF),
        ],
        [((512, 128), F32)],
        1 << 30,
        xc, own, *others, lat_keep, lat_got,
    )
    lat_got = swap(lat_send, 3)
    got = lax.ppermute(send, "band", flip)

    def kept(*refs):
        kept_kernel(*refs, scale=scale_two)

    (keep,) = call(kept, [((2304, 128), BF)], [], 1 << 30, xc, cot)

    def backward(*refs):
        backward_kernel(*refs, scale=scale_one)

    (g1,) = call(
        backward, [((64, 128), BF)], [((2, 128, 128), F32)], 1 << 30, cot, pre, win, w2, sel
    )
    (part,) = call(join_kernel, [((2368, 128), BF)], [], 1 << 20, keep, got, g1)
    half = n // 2
    groups = [[2 * i + c for i in range(half)] for c in range(2)]

    def exchange(x):
        x = x.reshape(half, 1184 // half, 2, 128)
        x = lax.all_to_all(x, "band", 0, 0, tiled=True, axis_index_groups=groups)
        return x.reshape(2368, 128)

    def share(*refs):
        share_kernel(*refs, count=half)

    part = exchange(part)
    mine, latent = call(
        share,
        [((2368, 128), BF), ((256, 128), BF)],
        [((256, 128), F32), ((2368 // half * min(half, 8) + 16, 128), F32)],
        1 << 20,
        part, lat_own, lat_got,
    )
    mine = exchange(mine)
    other = lax.ppermute(mine, "band", flip)
    g2, g1 = call(
        first_half_kernel,
        [((3, 1152, 256), F32), ((64, 128), BF)],
        [((1152, 256), F32), ((1152, 256), F32), pltpu.SemaphoreType.DMA((4,))],
        1 << 20,
        mine,
        far_out=(0,),
    )
    g2, g1 = call(
        other_half_kernel,
        [((3, 1152, 256), F32), ((12, 27, 32), F32)],
        [((1152, 256), F32), ((12, 27, 32), F32), ((12, 48, 32), F32), pltpu.SemaphoreType.DMA((4,))],
        1 << 20,
        g2, g1, other,
        far=(0,), far_out=(0, 1), aliases={0: 0},
    )
    return latent.reshape(64, 2, 2, 128), jnp.transpose(g1, (1, 0, 2)), g2.reshape(27, 128, 256)


def solution(mesh):
    return jax.shard_map(
        on_device,
        mesh=mesh,
        in_specs=(
            P(None, None, "band", None),
            P(None, None, "chan"),
            P(None, "chan", None),
            P("chan", None, "band", None),
        ),
        out_specs=(P("chan", None, "band", None), P(None, None, "chan"), P(None, "chan", None)),
        check_vma=False,
    )
```

```python
import math

import jax
import jax.numpy as jnp
from jax import lax
from jax.experimental import pallas as pl
from jax.experimental.pallas import tpu as pltpu
from jax.sharding import PartitionSpec as P

BF = jnp.bfloat16
F32 = jnp.float32


def iota(shape, axis):
    return lax.broadcasted_iota(jnp.int32, shape, axis)


def matrix_kernel(col_ref, row_ref, sel_ref):
    u, w = iota((512, 128), 0), iota((512, 128), 1)
    for s in range(2):
        hit = ((u >> 2) == w) & (((u >> 1) & 1) == s)
        for t in range(2):
            value = 0.5 if t == 0 else jnp.where((u & 1) == 1, -0.5, 0.5)
            at = (s * 2 + t) * 128
            col_ref[:, at : at + 128] = jnp.where(hit, value, 0.0).astype(BF)
    at, lane = iota((256, 128), 0), iota((256, 128), 1)
    m, r, f, tb = at & 15, (at >> 4) & 3, (at >> 6) & 1, at >> 7
    wi = (m * 11) >> 5
    y = 4 * r + 2 * wi + tb + 2
    for part, (first, count) in enumerate(((2, 6), (8, 8), (16, 6))):
        hit = (lane == ((m - 3 * wi) * 2 + f) * count + y - first) & (m < 12)
        hit = hit & (y >= first) & (y < first + count)
        row_ref[part] = jnp.where(hit, 1.0, 0.0).astype(BF)
    at, lane = iota((128, 256), 0), iota((128, 256), 1)
    c = (at * 57) >> 9
    tap = at - 9 * c
    b = (tap * 11) >> 5
    e = tap - 3 * b
    target = ((c >> 1) & 1) * 128 + (e * 2 + (c & 1)) * 16 + b * 3 + (c >> 2)
    for p in range(4):
        hit = (lane == target + (p & 1) * 32 + (p >> 1) * 3) & (at < 108)
        sel_ref[p] = jnp.where(hit, 1.0, 0.0).astype(BF)


def dot(a, b, ca=1, cb=0):
    return lax.dot_general(a, b, (((ca,), (cb,)), ((), ())), preferred_element_type=F32)


def edges_kernel(
    both_ref, outer_ref, inner_ref, video_out, own_out, rows, pixels, packed
):
    core = lax.axis_index("band") % 2
    video_out[...] = both_ref[:48, 128:]
    own_out[...] = both_ref[:, :128]
    rows[...] = both_ref[:, :128].astype(F32)
    pixels[:48, :] = both_ref[:48, 128:].astype(F32)

    def put(ref, r):
        ref[:128, :] = rows[pl.ds(r, 128, stride=2), :].astype(BF)
        for g in range(6):
            for i in range(4):
                packed[i * 36 + g * 6 : i * 36 + g * 6 + 6, :] = pixels[
                    g * 8 + 2 * r : g * 8 + 2 * r + 6, i * 128 : i * 128 + 128
                ]
        ref[128:, :] = packed[:144, :].astype(BF)

    @pl.when(core == 0)
    def _():
        put(inner_ref, 1)
        put(outer_ref, 0)

    @pl.when(core == 1)
    def _():
        put(inner_ref, 0)
        put(outer_ref, 1)


def grown_kernel(own_ref, outer_ref, inner_ref, _, __, out_ref):
    core = lax.axis_index("band") % 2
    out_ref[:256, :] = own_ref[...]
    for side, ref in ((1 - core, inner_ref), (core, outer_ref)):
        out_ref[pl.ds(pl.multiple_of(256 + side * 128, 128), 128), :] = ref[:128, :]


def shifted(x, step):
    lanes = x.shape[1]
    lane = lax.broadcasted_iota(jnp.int32, x.shape, 1) % 128
    if step == -1:
        return jnp.where(lane == 0, 0.0, pltpu.roll(x, 1, 1))
    return jnp.where(lane == 127, 0.0, pltpu.roll(x, lanes - 1, 1))


def forward_kernel(
    outer_ref, own_ref, inner_ref, col_ref, row_ref, sel_ref, w1_ref, cot_ref,
    xc_ref, pre_ref, win_ref, cot_out, one, two, packed,
):
    band = lax.axis_index("band")
    core = band % 2
    cot_out[...] = cot_ref[...]
    last = lax.axis_size("band") - 1
    beyond = []
    for ref in (inner_ref, outer_ref):
        packed[:144, :] = ref[128:, :].astype(F32)
        beyond.append(jnp.concatenate([packed[k * 36 : k * 36 + 36, :] for k in range(4)], 1).astype(BF))
    v = (
        dot(row_ref[2 - 2 * core][:, :36], beyond[0])
        + dot(row_ref[1, :, :48], own_ref[...])
        + dot(row_ref[2 * core][:, :36], beyond[1])
    ).astype(BF)
    h = dot(v, col_ref[...])
    top, low = h[:128], h[128:]
    for pm, half in enumerate((top + low, top - low)):
        even, odd = half[:, :256], half[:, 256:]
        streams = (shifted(odd, -1), even, odd, shifted(even, 1))
        for st in range(8):
            part = streams[st // 2][:, (st % 2) * 128 : (st % 2) * 128 + 128].astype(BF)
            for f in range(2):
                for r in range(4):
                    at = (f * 4 + r) * 16
                    one[f, pm * 128 + st * 16 : pm * 128 + st * 16 + 16, r * 128 : r * 128 + 128] = part[
                        at : at + 16, :
                    ]
    w1a, w1b = (
        jnp.concatenate([dot(w1_ref[a], sel_ref[p], 0, 0) for p in range(4)], 0).astype(BF)
        for a in range(2)
    )
    pres = (dot(w1b, one[0]), dot(w1a, one[0]) + dot(w1b, one[1]))
    lane = lax.broadcasted_iota(jnp.int32, (32, 512), 1)
    keep = ((lane >= 128) | (band > 0)) & ((lane < 384) | (band < last))
    for f in range(2):
        pre = pres[f]
        pre_ref[:, f * 256 : f * 256 + 256] = pre[:, 128:384]
        win_ref[:, f * 256 : f * 256 + 256] = one[f, :, 128:384]
        act = pre * jax.nn.sigmoid(pre)
        p, q, r, s = act[:32], act[32:64], act[64:96], act[96:]
        pq, pmq, rs, rms = p + q, p - q, r + s, r - s
        parts = (pq + rs, pmq + rms, pq - rs, pmq - rms)
        for k in range(4):
            part = jnp.where(keep, parts[k] * 0.5, 0.0)
            for r in range(4):
                two[r, pl.ds(k, 32, stride=4), :] = part[:, r * 128 : r * 128 + 128]
        x = jnp.concatenate([two[r] for r in range(4)], 1)
        for e, xe in enumerate((shifted(x, -1), x, shifted(x, 1))):
            xe = xe.astype(BF)
            for b in range(3):
                at = (b * 3 + e) * 128
                xc_ref[at : at + 128, f * 256 : f * 256 + 256] = xe[:, b * 128 : b * 128 + 256]


def first_rows_kernel(in_ref, _, out_ref):
    out_ref[...] = in_ref[:256, :]


def hold_kernel(_, __, ___):
    pass


def last_rows_kernel(in_ref, out_ref):
    out_ref[...] = in_ref[256:, :]


def latent_kernel(xc_ref, w2_ref, keep_ref, send_ref, lat):
    out = dot(w2_ref[2304:, :], xc_ref[...], 0, 0)
    more = dot(w2_ref[1152:2304, :], xc_ref[:, :256], 0, 0)
    lat[:, :256] = out[:, :256].astype(BF)
    lat[:, 256:] = (out[:, 256:] + more).astype(BF)
    chan = lax.axis_index("chan")
    for ref, i, k in ((keep_ref, 0, 0), (send_ref, 0, 1), (send_ref, 1, 2), (keep_ref, 1, 3)):
        ref[i] = lat[pl.ds(pl.multiple_of((chan ^ k) * 64, 64), 64), :]


def second_grad_kernel(
    xc_ref, c0_ref, c1_ref, c3_ref, own2_ref, outer2_ref, lkeep_ref, lgot_ref,
    grown, send_ref, lown_ref, lsend_ref, rows, *, scale
):
    lown_ref[...] = lkeep_ref[0].astype(F32) + lgot_ref[0].astype(F32)
    lsend_ref[...] = (lkeep_ref[1].astype(F32) + lgot_ref[1].astype(F32)).astype(BF)
    chan = lax.axis_index("chan")
    core = lax.axis_index("band") % 2
    for k, ref in enumerate((c0_ref, c1_ref, None, c3_ref)):
        if ref is None:
            rows[:256, :] = own2_ref[...].astype(F32)
            rows[256:, :] = outer2_ref[...].astype(F32)
        else:
            rows[...] = ref[...].astype(F32)
        at = pl.multiple_of((chan ^ k) * 64, 64)
        for f in range(2):
            for r in range(2):
                lane = f * 512 + r * 128 + 128
                part = rows[pl.ds(f * 2 + r, 64, stride=4), :]
                grown[pl.ds(at, 64), lane : lane + 128] = part.astype(BF)
            for side in range(2):
                lane = f * 512 + side * 384
                part = rows[pl.ds(256 + side * 128 + f, 64, stride=2), :]
                grown[pl.ds(at, 64), lane : lane + 128] = part.astype(BF)

    half_gradient(xc_ref, grown, send_ref, 1 - core, scale)


def half_gradient(xc_ref, grown, out_ref, half, scale):
    def put(g):
        g = g * scale
        out_ref[:1152, :] = g[:, :128].astype(BF)
        out_ref[1152:, :] = g[:, 128:].astype(BF)

    @pl.when(half == 0)
    def _():
        put(dot(xc_ref[:, :256], grown[:, 640:896], 1, 1))

    @pl.when(half == 1)
    def _():
        put(dot(xc_ref[:, :256], grown[:, 128:384], 1, 1) + dot(xc_ref[:, 256:], grown[:, 640:896], 1, 1))


def kept_kernel(xc_ref, grown, keep_ref, *, scale):
    half_gradient(xc_ref, grown, keep_ref, lax.axis_index("band") % 2, scale)


def backward_kernel(grown, pre_ref, win_ref, w2_ref, sel_ref, g1_ref, back_s, *, scale):
    z0 = z1 = 0.0
    for b in range(3):
        lo = (2 - b) * 128
        c0, c1 = grown[:, lo : lo + 256], grown[:, 512 + lo : 768 + lo]
        wa = w2_ref[1152 + b * 384 : 1536 + b * 384, :]
        wb = w2_ref[2304 + b * 384 : 2688 + b * 384, :]
        z0 = z0 + dot(wb, c0) + dot(wa, c1)
        z1 = z1 + dot(wb, c1)
    for f, z in enumerate((z0, z1)):
        z = z[128:256] + shifted(z[:128], 1) + shifted(z[256:], -1)
        back_s[0], back_s[1] = z[:, :128], z[:, 128:]
        a0, a1, a2, a3 = (
            jnp.concatenate([back_s[r, pl.ds(k, 32, stride=4), :] for r in range(2)], 1)
            for k in range(4)
        )
        s01, d01, s23, d23 = a0 + a1, a0 - a1, a2 + a3, a2 - a3
        act = jnp.concatenate([s01 + s23, d01 + d23, s01 - s23, d01 - d23], 0) * 0.5
        pre = pre_ref[:, f * 256 : f * 256 + 256]
        gate = jax.nn.sigmoid(pre)
        back = (act * gate * (1.0 + pre * (1.0 - gate))).astype(BF)
        if f == 0:
            late = dot(back, win_ref[:, :256], 1, 1)
        else:
            early = dot(back, win_ref[:, :256], 1, 1)
            late = late + dot(back, win_ref[:, 256:], 1, 1)
    for a, g in enumerate((early, late)):
        g = g * scale
        hi = g.astype(BF)
        lo = (g - hi.astype(F32)).astype(BF)
        total = 0.0
        for p in range(4):
            rows = slice(32 * p, 32 * p + 32)
            total = total + dot(hi[rows], sel_ref[p], 1, 1)
            total = total + dot(lo[rows], sel_ref[p], 1, 1)
        g1_ref[32 * a : 32 * a + 32, :] = total.astype(BF)


def join_kernel(keep_ref, got_ref, g1_ref, sum_ref):
    sum_ref[:2304, :] = (keep_ref[...].astype(F32) + got_ref[...].astype(F32)).astype(BF)
    sum_ref[2304:, :] = g1_ref[...]


def share_kernel(got_ref, lown_ref, lgot_ref, out_ref, lat_ref, rows, wide, *, count):
    lat = lown_ref[...] + lgot_ref[...].astype(F32)
    for i in range(4):
        rows[pl.ds(i, 64, stride=4), :] = lat[:, i * 128 : i * 128 + 128]
    lat_ref[...] = rows[...].astype(BF)
    size = got_ref.shape[0] // count
    bunch = 8 if count % 8 == 0 else count
    block = bunch * size
    total = got_ref[:block, :].astype(F32)
    for i in range(block, count * size, block):
        total = total + got_ref[i : i + block, :].astype(F32)
    wide[:block, :] = total
    total = wide[:size, :]
    for i in range(1, bunch):
        total = total + wide[i * size : i * size + size, :]
    for i in range(bunch):
        wide[i * size : i * size + size, :] = total
    total = wide[:block, :].astype(BF)
    for i in range(0, count * size, block):
        out_ref[i : i + block, :] = total


def widen(from_ref, wide, to_ref, sems, first):
    copies = []
    for i in range(3):
        at = i * 384
        wide[at : at + 384, :128] = from_ref[at : at + 384, :].astype(F32)
        wide[at : at + 384, 128:] = from_ref[1152 + at : 1536 + at, :].astype(F32)
        rows = pl.ds(at, 384)
        copies.append(pltpu.make_async_copy(wide.at[rows], to_ref.at[rows], sems.at[first + i]))
        copies[-1].start()
    return copies


def first_half_kernel(mine_ref, g2_ref, g1_ref, zero, own, sems):
    core = lax.axis_index("band") % 2
    zero[...] = jnp.zeros((1152, 256), F32)
    clear = pltpu.make_async_copy(zero, g2_ref.at[0], sems.at[0])
    clear.start()
    copies = [clear] + widen(mine_ref, own, g2_ref.at[1 + core], sems, 1)
    g1_ref[...] = mine_ref[2304:, :]
    for copy in copies:
        copy.wait()


def other_half_kernel(_, mine_ref, other_ref, g2_ref, g1_ref, half, taps_s, stage, sems):
    core = lax.axis_index("band") % 2
    both = mine_ref[...].astype(F32) + other_ref[2304:2368, :].astype(F32)
    taps = [jnp.transpose(both[32 * a : 32 * a + 32, :]) for a in range(2)]
    stage[...] = jnp.zeros((12, 48, 32), F32)
    for c in range(12):
        for a in range(2):
            stage[c, 9 * a + 9 : 9 * a + 18, :] = taps[a][9 * c : 9 * c + 9, :]
    for c in range(12):
        taps_s[c] = stage[c, :27, :]
    first = pltpu.make_async_copy(taps_s, g1_ref, sems.at[3])
    first.start()
    for copy in [first] + widen(other_ref, half, g2_ref.at[2 - core], sems, 0):
        copy.wait()


VMEM, HBM = pltpu.VMEM, pltpu.HBM


def call(kernel, outs, scratch, flops, *args, far=(), far_out=(), aliases=None):
    return pl.pallas_call(
        kernel,
        out_shape=[jax.ShapeDtypeStruct(*o) for o in outs],
        in_specs=[pl.BlockSpec(memory_space=HBM if i in far else VMEM) for i in range(len(args))],
        out_specs=[pl.BlockSpec(memory_space=HBM if i in far_out else VMEM) for i in range(len(outs))],
        scratch_shapes=[s if not isinstance(s, tuple) else pltpu.VMEM(*s) for s in scratch],
        input_output_aliases=aliases or {},
        compiler_params=pltpu.CompilerParams(vmem_limit_bytes=20 * 1024 * 1024),
        cost_estimate=pl.CostEstimate(flops=flops, bytes_accessed=1 << 20, transcendentals=0),
    )(*args)


def on_device(video, weight_one, weight_two, cotangent):
    n = lax.axis_size("band")
    flip = [(i, i ^ 1) for i in range(n)]
    frames, half_rows, half_cols = video.shape[1], n * 4, video.shape[3] // 2
    scale_one = 1.0 / math.sqrt(frames * half_rows * half_cols)
    scale_two = 1.0 / math.sqrt(frames * (half_rows // 2) * (half_cols // 2))

    flat, own = video.reshape(48, 512), cotangent.reshape(256, 128)

    def swap(x, k):
        return lax.ppermute(x, "chan", [(i, i ^ k) for i in range(4)])

    outer, inner, flat, own = call(
        edges_kernel,
        [((272, 128), BF), ((272, 128), BF), ((48, 512), BF), ((256, 128), BF)],
        [((256, 128), F32), ((64, 512), F32), ((160, 128), F32)],
        1 << 20,
        jnp.concatenate([own, jnp.pad(flat, ((0, 208), (0, 0)))], 1),
    )
    outer = lax.ppermute(outer, "band", [(i, i + 1 - 2 * (i % 2 == 0)) for i in range(1, n - 1)])
    inner = lax.ppermute(inner, "band", flip)
    cols, rows, sel = call(
        matrix_kernel,
        [((512, 512), BF), ((3, 256, 128), BF), ((4, 128, 256), BF)],
        [],
        1 << 20,
    )
    w1 = weight_one[9:].reshape(2, 9, 12, 32).transpose(0, 2, 1, 3).reshape(2, 108, 32)
    w1 = jnp.pad(w1, ((0, 0), (0, 20), (0, 0)))
    (own,) = call(
        grown_kernel, [((512, 128), BF)], [], 1 << 20, own, outer, inner, sel, w1,
        far=(3, 4),
    )
    near = swap(own, 1)
    w2 = weight_two.reshape(3456, 256)
    xc, pre, win, own = call(
        forward_kernel,
        [((1152, 512), BF), ((128, 512), F32), ((256, 512), BF), ((512, 128), BF)],
        [((2, 256, 512), BF), ((4, 128, 128), F32), ((160, 128), F32)],
        1 << 30,
        outer, flat, inner, cols, rows, sel, w1, own,
    )
    far = swap(own, 3)
    (near_part,) = call(first_rows_kernel, [((256, 128), BF)], [], 1 << 10, near, xc, far=(1,))
    (far_part,) = call(last_rows_kernel, [((256, 128), BF)], [], 1 << 10, far)
    others = [near, far, swap(near_part, 3), swap(far_part, 1)]
    lat_keep, lat_send = call(
        latent_kernel, [((2, 64, 512), BF)] * 2, [((256, 512), BF)], 1 << 30, xc, w2
    )
    (lat_send,) = call(
        hold_kernel, [((2, 64, 512), BF)], [], 1 << 10, lat_send, near_part,
        far=(0, 1), far_out=(0,), aliases={0: 0},
    )
    lat_got = swap(lat_send, 1)

    def second_grad(*refs):
        second_grad_kernel(*refs, scale=scale_two)

    cot, send, lat_own, lat_send = call(
        second_grad,
        [
            ((256, 1024), BF), ((2304, 128), BF),
            ((64, 512), F32), ((64, 512), BF),
        ],
        [((512, 128), F32)],
        1 << 30,
        xc, own, *others, lat_keep, lat_got,
    )
    lat_got = swap(lat_send, 3)
    got = lax.ppermute(send, "band", flip)

    def kept(*refs):
        kept_kernel(*refs, scale=scale_two)

    (keep,) = call(kept, [((2304, 128), BF)], [], 1 << 30, xc, cot)

    def backward(*refs):
        backward_kernel(*refs, scale=scale_one)

    (g1,) = call(
        backward, [((64, 128), BF)], [((2, 128, 128), F32)], 1 << 30, cot, pre, win, w2, sel
    )
    (part,) = call(join_kernel, [((2368, 128), BF)], [], 1 << 20, keep, got, g1)
    half = n // 2
    groups = [[2 * i + c for i in range(half)] for c in range(2)]

    def exchange(x):
        x = x.reshape(half, 1184 // half, 2, 128)
        x = lax.all_to_all(x, "band", 0, 0, tiled=True, axis_index_groups=groups)
        return x.reshape(2368, 128)

    def share(*refs):
        share_kernel(*refs, count=half)

    part = exchange(part)
    mine, latent = call(
        share,
        [((2368, 128), BF), ((256, 128), BF)],
        [((256, 128), F32), ((2368 // half * min(half, 8) + 16, 128), F32)],
        1 << 20,
        part, lat_own, lat_got,
    )
    mine = exchange(mine)
    other = lax.ppermute(mine, "band", flip)
    g2, g1 = call(
        first_half_kernel,
        [((3, 1152, 256), F32), ((64, 128), BF)],
        [((1152, 256), F32), ((1152, 256), F32), pltpu.SemaphoreType.DMA((4,))],
        1 << 20,
        mine,
        far_out=(0,),
    )
    g2, g1 = call(
        other_half_kernel,
        [((3, 1152, 256), F32), ((12, 27, 32), F32)],
        [((1152, 256), F32), ((12, 27, 32), F32), ((12, 48, 32), F32), pltpu.SemaphoreType.DMA((4,))],
        1 << 20,
        g2, g1, other,
        far=(0,), far_out=(0, 1), aliases={0: 0},
    )
    return latent.reshape(64, 2, 2, 128), jnp.transpose(g1, (1, 0, 2)), g2.reshape(27, 128, 256)


def solution(mesh):
    return jax.shard_map(
        on_device,
        mesh=mesh,
        in_specs=(
            P(None, None, "band", None),
            P(None, None, "chan"),
            P(None, "chan", None),
            P("chan", None, "band", None),
        ),
        out_specs=(P("chan", None, "band", None), P(None, None, "chan"), P(None, "chan", None)),
        check_vma=False,
    )
```
